32 devices in a mesh: dp: 16 (over z, y, x), seq: 2 (over core).
Axes of the slice: x: 2, y: 2, z: 4, core: 2. Of those that a mesh axis runs over, the one named last changes fastest.
Arguments:
- tokens: bfloat16 [16384, 768], P(('dp', 'seq')), may hold values from -6 to 6
- skip_values: bfloat16 [16384, 384], P(('dp', 'seq')), may hold values from -6 to 6
- doc_lengths: int32 [16, 6], P('dp'), may hold values from 1 to 682, as said below
- gain_first: bfloat16 [768], replicated, may hold values from 0.099609375 to 1.8984375
- shift_first: bfloat16 [768], replicated, may hold values from -3 to 3
- query_weight: bfloat16 [768, 768], replicated, may hold values from -0.21875 to 0.21875
- query_bias: bfloat16 [768], replicated, may hold values from -3 to 3
- key_weight: bfloat16 [768, 768], replicated, may hold values from -0.21875 to 0.21875
- value_weight: bfloat16 [768, 384], replicated, may hold values from -0.21875 to 0.21875
- value_bias: bfloat16 [384], replicated, may hold values from -3 to 3
- out_weight: bfloat16 [768, 768], replicated, may hold values from -0.875 to 0.875
- out_bias: bfloat16 [768], replicated, may hold values from -3 to 3
- gain_second: bfloat16 [768], replicated, may hold values from 0.099609375 to 1.8984375
- shift_second: bfloat16 [768], replicated, may hold values from -3 to 3
- up_weight: bfloat16 [768, 3072], replicated, may hold values from -0.21875 to 0.21875
- up_bias: bfloat16 [3072], replicated, may hold values from -3 to 3
- down_weight: bfloat16 [3072, 768], replicated, may hold values from -0.109375 to 0.109375
- down_bias: bfloat16 [768], replicated, may hold values from -3 to 3
- cotangent: bfloat16 [16384, 768], P(('dp', 'seq')), may hold values from -6 to 6
Outputs:
- output: bfloat16 [16384, 768], P(('dp', 'seq'))
- grad_tokens: bfloat16 [16384, 768], P(('dp', 'seq'))
- grad_skip_values: bfloat16 [16384, 384], P(('dp', 'seq'))
- grad_gain_first: float32 [768], replicated
- grad_shift_first: float32 [768], replicated
- grad_query_weight: float32 [768, 768], P('dp')
- grad_query_bias: float32 [768], replicated
- grad_key_weight: float32 [768, 768], P('dp')
- grad_value_weight: float32 [768, 384], P('dp')
- grad_value_bias: float32 [384], replicated
- grad_out_weight: float32 [768, 768], P('dp')
- grad_out_bias: float32 [768], replicated
- grad_gain_second: float32 [768], replicated
- grad_shift_second: float32 [768], replicated
- grad_up_weight: float32 [768, 3072], P('dp')
- grad_up_bias: float32 [3072], replicated
- grad_down_weight: float32 [3072, 768], P('dp')
- grad_down_bias: float32 [768], replicated
The draws below stay inside these ranges and needn't reach their ends.
Inputs may be any that keep to these rules, and one draw needn't show every extreme that they name: `doc_lengths`: each row lists 6 - 1 document lengths in order, then the number of padding positions at the row's end (1 or more); a row's entries sum to 1024, and exactly one document of each row has 682 positions.
All inputs are finite; a program needn't handle non-finite values.
Results may differ from the reference program's by a relative error of at most 0.014.
Values may be sent and summed in bfloat16 or wider, within the bound.
No kernel may reach another device: no remote copies, remote signals or barrier semaphores. Data moves between devices by JAX's collectives and lax.ppermute only.
A program may use at most 192 MiB of HBM per device.

```python
import jax
import jax.numpy as jnp
from jax import lax

D = 768
HEADS = 12
HEAD = 64
FF = 3072
FRESH = 6
LEN = 1024
DOCS = 6
DOC_MOST = 682
ROWS = 16
TOKENS = 16384


def draw_doc_lengths(key, part):
    key = jax.random.fold_in(key, 7)
    row_keys = jax.random.split(key, ROWS)

    def one_row(row_key):
        pad_key, cut_key, place_key = jax.random.split(row_key, 3)
        padding = jax.random.randint(pad_key, (), 1, LEN // 8).astype(jnp.int32)
        remain = (LEN - DOC_MOST - padding).astype(jnp.int32)
        others = DOCS - 2
        cut_points = jnp.sort(jax.random.randint(cut_key, (others - 1,), 1, remain - others + 2)).astype(jnp.int32)
        cut_points = cut_points + jnp.arange(others - 1, dtype=jnp.int32)
        bounds = jnp.concatenate([jnp.zeros((1,), jnp.int32), cut_points, remain[None]])
        pieces = bounds[1:] - bounds[:-1]
        long_slot = jax.random.randint(place_key, (), 0, DOCS - 1).astype(jnp.int32)
        places = jnp.arange(DOCS - 1, dtype=jnp.int32)
        before = pieces[jnp.clip(places, 0, others - 1)]
        behind = pieces[jnp.clip(places - 1, 0, others - 1)]
        docs_row = jnp.where(places < long_slot, before, jnp.where(places == long_slot, jnp.int32(DOC_MOST), behind))
        return jnp.concatenate([docs_row, padding[None]]).astype(jnp.int32)
    return jax.vmap(one_row)(row_keys)


def spiked(array, key, source, target, blocks, factor):
    def block_of(axis_at):
        return (jnp.arange(array.shape[axis_at]) // (array.shape[axis_at] // blocks)).reshape((-1,) + (1,) * (array.ndim - 1 - axis_at))

    one_side = jax.random.permutation(key, blocks)[block_of(target)]
    second = (block_of(target) + blocks // 2) % blocks
    return jnp.where((block_of(source) == one_side) | (block_of(source) == second), factor * array, array)


def block_scale(stream_key, extent, shards, smallest, top_value):
    factor_of, own = 1.0, jax.random.fold_in(stream_key, 6)
    for axis_at, shards_of in shards:
        draws = jnp.exp(jax.random.uniform(jax.random.fold_in(own, axis_at), (shards_of,), jnp.float32, smallest / len(shards), top_value / len(shards)))
        factor_of = factor_of * jnp.repeat(draws, extent[axis_at] // shards_of).reshape([-1 if axis == axis_at else 1 for axis in range(len(extent))])
    return factor_of


def bell_draw(rng, extent, scale, most, cuts=(), held_as=jnp.bfloat16):
    drawn = scale * jax.random.normal(rng, extent, jnp.float32)
    if cuts:
        drawn = drawn * block_scale(rng, extent, cuts, -0.22, 0.18)
    return jnp.clip(drawn, -most, most).astype(held_as)


def bell_draw_with(own_key, shape, scale, most, cuts, heavy, kind=jnp.bfloat16):
    values = scale * jax.random.normal(own_key, shape, jnp.float32)
    if cuts:
        values = values * block_scale(own_key, shape, cuts, -0.22, 0.18)
    return jnp.clip(spiked(values, jax.random.fold_in(own_key, 3), *heavy), -most, most).astype(kind)


def setup_inputs(seed: int = 0) -> dict:
    splits = jax.random.split(jax.random.key(seed), 20)
    tokens = bell_draw(splits[0], (TOKENS, D), 1.0, 6.0, ((0, 32),))
    skip_values = bell_draw(splits[1], (TOKENS, (HEADS - FRESH) * HEAD), 1.0, 6.0, ((0, 32),))
    doc_lengths = draw_doc_lengths(jax.random.fold_in(splits[19], 71), 0)
    gain_first = jnp.clip(1.0 + 0.18 * jax.random.normal(splits[3], (D,), jnp.float32), 0.099609375, 1.8984375).astype(jnp.bfloat16)
    shift_first = bell_draw(splits[4], (D,), 0.5, 3.0)
    query_weight = bell_draw(splits[5], (D, D), D ** -0.5, 0.21875)
    query_bias = bell_draw(splits[6], (D,), 0.5, 3.0)
    key_weight = bell_draw(splits[7], (D, D), D ** -0.5, 0.21875)
    value_weight = bell_draw(splits[8], (D, FRESH * HEAD), D ** -0.5, 0.21875)
    value_bias = bell_draw(splits[9], (FRESH * HEAD,), 0.5, 3.0)
    out_weight = bell_draw(splits[10], (D, D), (D // 16) ** -0.5, 0.875)
    out_bias = bell_draw(splits[11], (D,), 0.5, 3.0)
    gain_second = jnp.clip(1.0 + 0.18 * jax.random.normal(splits[12], (D,), jnp.float32), 0.099609375, 1.8984375).astype(jnp.bfloat16)
    shift_second = bell_draw(splits[13], (D,), 0.5, 3.0)
    up_weight = bell_draw(splits[14], (D, FF), D ** -0.5, 0.21875)
    up_bias = bell_draw(splits[15], (FF,), 0.5, 3.0)
    down_weight = bell_draw(splits[16], (FF, D), FF ** -0.5, 0.109375)
    down_bias = bell_draw(splits[17], (D,), 0.5, 3.0)
    cotangent = bell_draw_with(splits[18], (TOKENS, D), 1.0, 6.0, ((0, 32),), (0, 1, 32, 2.75))
    return {"tokens": tokens, "skip_values": skip_values, "doc_lengths": doc_lengths, "gain_first": gain_first, "shift_first": shift_first, "query_weight": query_weight, "query_bias": query_bias, "key_weight": key_weight, "value_weight": value_weight, "value_bias": value_bias, "out_weight": out_weight, "out_bias": out_bias, "gain_second": gain_second, "shift_second": shift_second, "up_weight": up_weight, "up_bias": up_bias, "down_weight": down_weight, "down_bias": down_bias, "cotangent": cotangent}


HIGHEST = lax.Precision.HIGHEST

@jax.custom_vjp
def low(v):
    return lax.optimization_barrier(v.astype(jnp.bfloat16)).astype(jnp.float32)

@jax.custom_vjp
def low_back(v):
    return v

def low_keep(v):
    return (low(v), None)

def low_pass(kept, grad):
    return (grad,)

def back_keep(v):
    return (v, None)

def back_low(kept, grad):
    return (low(grad),)
low.defvjp(low_keep, low_pass)
low_back.defvjp(back_keep, back_low)

def layer_norm(values, gain, shift):
    centre = values - lax.optimization_barrier(jnp.mean(values, axis=-1, keepdims=True))
    spread = lax.optimization_barrier(jnp.mean(centre * centre, axis=-1, keepdims=True))
    return centre * lax.rsqrt(spread + 1e-05) * gain + shift

def gelu_tanh(values):
    return jax.nn.gelu(values, approximate=True)

def allowed_pairs(length_row, total):
    count = length_row.shape[0]
    bounds = jnp.cumsum(length_row.astype(jnp.int32))
    places = jnp.arange(total, dtype=jnp.int32)
    segment = lax.optimization_barrier(jnp.sum((places[:, None] >= bounds[None, :count - 1]).astype(jnp.int32), axis=1))
    matching = segment[:, None] == segment[None, :]
    causal = places[None, :] <= places[:, None]
    usable = (segment[None, :] != count - 1) | (places[None, :] == places[:, None])
    return matching & causal & usable

def matmul(left, right):
    return jnp.dot(left, right, precision=HIGHEST, preferred_element_type=jnp.float32)

def block_row(weights, inputs, skips, length_row):
    gain_first, shift_first, query_weight, query_bias, key_weight, value_weight, value_bias, out_weight, out_bias, gain_second, shift_second, up_weight, up_bias, down_weight, down_bias = weights
    length = inputs.shape[0]
    normed = low(layer_norm(inputs, gain_first, shift_first))
    queries = low(low_back(matmul(normed, query_weight) + query_bias))
    keys_all = low(low_back(matmul(normed, key_weight)))
    fresh = low(low_back(matmul(normed, value_weight) + value_bias))
    skipped = low(low_back(skips))
    values = jnp.concatenate([fresh, skipped], axis=1)
    query_heads = queries.reshape(length, HEADS, HEAD)
    key_heads = keys_all.reshape(length, HEADS, HEAD)
    value_heads = values.reshape(length, HEADS, HEAD)
    score_scale = HEAD ** (-0.5)
    scores = low_back(jnp.einsum('qhd,khd->hqk', query_heads, key_heads, precision=HIGHEST) * score_scale)
    allowed = allowed_pairs(length_row, length)
    masked = jnp.where(allowed[None], scores, -1e+30)
    row_peak = lax.optimization_barrier(jnp.max(masked, axis=2, keepdims=True))
    log_total = row_peak + jnp.log(lax.optimization_barrier(jnp.sum(jnp.exp(masked - row_peak), axis=2, keepdims=True)))
    attention = low(jnp.exp(masked - log_total))
    attended = jnp.einsum('hqk,khd->qhd', attention, value_heads, precision=HIGHEST).reshape(length, HEADS * HEAD)
    attended = low(low_back(attended))
    branch = low_back(matmul(attended, out_weight) + out_bias)
    middle = inputs + branch
    normed_two = low(layer_norm(middle, gain_second, shift_second))
    hidden = low_back(matmul(normed_two, up_weight) + up_bias)
    activated = low(gelu_tanh(hidden))
    return middle + matmul(activated, down_weight) + down_bias

def reference(tokens, skip_values, doc_lengths, gain_first, shift_first, query_weight, query_bias, key_weight, value_weight, value_bias, out_weight, out_bias, gain_second, shift_second, up_weight, up_bias, down_weight, down_bias, cotangent):
    weights = tuple((item.astype(jnp.float32) for item in (gain_first, shift_first, query_weight, query_bias, key_weight, value_weight, value_bias, out_weight, out_bias, gain_second, shift_second, up_weight, up_bias, down_weight, down_bias)))
    skip_width = skip_values.shape[1]
    row_function = jax.checkpoint(block_row)

    def forward(inputs, skips, params):

        def advance(carry, slices):
            return (carry, row_function(params, slices[0], slices[1], slices[2]))
        ignored, rows_out = lax.scan(advance, None, (inputs.reshape(ROWS, LEN, D), skips.reshape(ROWS, LEN, skip_width), doc_lengths))
        return rows_out.reshape(ROWS * LEN, D)
    result, pull_back = jax.vjp(forward, tokens.astype(jnp.float32), skip_values.astype(jnp.float32), weights)
    grad_inputs, grad_skips, grads = pull_back(cotangent.astype(jnp.float32))
    return (result.astype(jnp.bfloat16), grad_inputs.astype(jnp.bfloat16), grad_skips.astype(jnp.bfloat16), grads[0], grads[1], grads[2], grads[3], grads[4], grads[5], grads[6], grads[7], grads[8], grads[9], grads[10], grads[11], grads[12], grads[13], grads[14])
```

```python
import functools

import jax
import jax.numpy as jnp
from jax import lax
from jax.experimental import pallas as pl
from jax.experimental.pallas import tpu as pltpu
from jax.sharding import PartitionSpec as P

HEAD = 64
FRESH = 6
PAIR = 2 * HEAD
QB = 256
LOG2E = 1.4426950408889634
GELU_C = 0.7978845608028654
GELU_A = 0.044715
f32 = jnp.float32
bf16 = jnp.bfloat16
NT = (((1,), (1,)), ((), ()))
TN = (((0,), (0,)), ((), ()))
CORE, PLACE, BOUND, PLACE_OTH = 0, 1, 17, 22
V_UP, V_DOWN, V_OUT, V_GAIN2, V_SHIFT2, V_GAIN1, V_SHIFT1, V_QUERY, V_VALUE = 0, 8, 10, 12, 14, 16, 18, 20, 22
V_ROWS = 24


def dot(left, right):
    return jnp.dot(left, right, preferred_element_type=f32)


def dot_nt(left, right):
    return lax.dot_general(left, right, NT, preferred_element_type=f32)


def dot_tn(left, right):
    return lax.dot_general(left, right, TN, preferred_element_type=f32)


def row_of(ref):
    return ref[...].astype(f32).reshape(1, -1)


def normalise(values):
    centre = values - jnp.mean(values, axis=-1, keepdims=True)
    spread = jnp.mean(centre * centre, axis=-1, keepdims=True)
    scale = lax.rsqrt(spread + 1e-05)
    return centre * scale, scale


def params(limit_mb, axes):
    return pltpu.CompilerParams(vmem_limit_bytes=limit_mb << 20, dimension_semantics=("arbitrary",) * axes)


def whole(shape):
    return pl.BlockSpec(shape, lambda *_: (0,) * len(shape))


def sds(shape, dtype):
    return jax.ShapeDtypeStruct(shape, dtype)


def project_kernel(scal, own, oth, skip_own, skip_oth, gain, shift, wq, bq, wk, wv, bv, q_ref, k_ref, v_ref, n_ref):
    step = pl.program_id(0)
    core = scal[CORE]
    mine = step < 2
    tokens = jnp.where(mine, own[...], oth[...]).astype(f32)
    xhat, _ = normalise(tokens)
    normed = (xhat * row_of(gain) + row_of(shift)).astype(bf16)
    n_ref[0] = normed
    q_ref[0] = (dot(normed, wq[...]) + row_of(bq)).astype(bf16) * jnp.asarray(HEAD**-0.5, bf16)
    k_ref[0] = dot(normed, wk[...]).astype(bf16)

    @pl.when(core == 0)
    def _():
        v_ref[0] = (dot(normed, wv[...]) + row_of(bv)).astype(bf16)

    @pl.when(core != 0)
    def _():
        v_ref[0] = jnp.where(mine, skip_own[...], skip_oth[...])


def project(scal, own, oth, skip_own, skip_oth, gain, shift, wq, bq, wk, wv, bv):
    rows, width = own.shape
    half = width // 2
    tile = rows // 2
    first = lambda s, sc: (jnp.minimum(s, 1), 0)
    second = lambda s, sc: (jnp.maximum(s - 2, 0), 0)
    col = lambda s, sc: (0, sc[CORE])
    out = lambda s, sc: (s // 2, s % 2, 0)
    return pl.pallas_call(
        project_kernel,
        grid_spec=pltpu.PrefetchScalarGridSpec(
            num_scalar_prefetch=1,
            grid=(4,),
            in_specs=[
                pl.BlockSpec((tile, width), first),
                pl.BlockSpec((tile, width), second),
                pl.BlockSpec((tile, half), first),
                pl.BlockSpec((tile, half), second),
                whole((width,)),
                whole((width,)),
                pl.BlockSpec((width, half), col),
                pl.BlockSpec((1, half), col),
                pl.BlockSpec((width, half), col),
                whole((width, half)),
                whole((half,)),
            ],
            out_specs=[pl.BlockSpec((1, tile, half), out)] * 3 + [pl.BlockSpec((1, tile, width), out)],
        ),
        out_shape=[sds((2, rows, half), bf16)] * 3 + [sds((2, rows, width), bf16)],
        compiler_params=params(40, 1),
    )(scal, own, oth, skip_own, skip_oth, gain, shift, wq, bq.reshape(1, -1), wk, wv, bv)


def first_allowed(scal, total):
    place = lax.broadcasted_iota(jnp.int32, (1, total), 1)
    start = jnp.zeros((1, total), jnp.int32)
    for k in range(4):
        start = jnp.where(place >= scal[BOUND + k], scal[BOUND + k], start)
    return jnp.where(place >= scal[BOUND + 4], place, start)


def allowed_block(start, low, high, first_query):
    key = lax.broadcasted_iota(jnp.int32, (high - low, QB), 0) + low
    ok = key >= start
    if high > first_query:
        ok = ok & (key <= lax.broadcasted_iota(jnp.int32, (high - low, QB), 1) + first_query)
    return ok


def head_part(values, h):
    lane = lax.broadcasted_iota(jnp.int32, values.shape, 1)
    return jnp.where((lane < HEAD) if h == 0 else (lane >= HEAD), values, jnp.zeros_like(values))


def attend_kernel(scal, q_ref, k_ref, v_ref, o_ref, lse_ref, kb, vt):
    core = scal[CORE]
    rows = q_ref.shape[1]
    total = 2 * rows
    for half in range(2):
        rel = core ^ half
        kb[half * rows : (half + 1) * rows, :] = k_ref[rel]
        vt[:, half * rows : (half + 1) * rows] = v_ref[rel].T
    start = first_allowed(scal, total)
    for qb in range(total // QB):
        low = qb * QB
        rel = core ^ (low // rows)
        off = low % rows
        query = q_ref[rel, pl.ds(off, QB), :]
        begin = start[:, low : low + QB]
        parts = []
        for h in range(2):
            qh = head_part(query, h)
            cuts = [(0, low), (low, low + QB)] if low else [(0, QB)]
            scores = []
            peak = None
            for a, b in cuts:
                s = dot_nt(kb[a:b, :], qh)
                s = jnp.where(allowed_block(begin, a, b, low), s, -1e30)
                top = jnp.max(s, axis=0, keepdims=True)
                peak = top if peak is None else jnp.maximum(peak, top)
                scores.append(s)
            peak2 = peak * LOG2E
            summed, acc = None, None
            for (a, b), s in zip(cuts, scores):
                e = jnp.exp2(s * LOG2E - peak2)
                part = jnp.sum(e, axis=0, keepdims=True)
                prod = dot(vt[h * HEAD : (h + 1) * HEAD, a:b], e.astype(bf16))
                summed = part if summed is None else summed + part
                acc = prod if acc is None else acc + prod
            lse_ref[0, h : h + 1, low : low + QB] = peak2 + jnp.log2(summed)
            parts.append(acc / summed)
        o_ref[rel, pl.ds(off, QB), :] = jnp.concatenate(parts, axis=0).T.astype(bf16)


def attend(scal, q, k, v):
    _, rows, half = q.shape
    pairs = half // PAIR
    block = pl.BlockSpec((2, rows, PAIR), lambda p, sc: (0, 0, p))
    return pl.pallas_call(
        attend_kernel,
        grid_spec=pltpu.PrefetchScalarGridSpec(
            num_scalar_prefetch=1,
            grid=(pairs,),
            in_specs=[block] * 3,
            out_specs=[block, pl.BlockSpec((1, 8, 2 * rows), lambda p, sc: (p, 0, 0))],
            scratch_shapes=[pltpu.VMEM((2 * rows, PAIR), bf16), pltpu.VMEM((PAIR, 2 * rows), bf16)],
        ),
        out_shape=[sds((2, rows, half), bf16), sds((pairs, 8, 2 * rows), f32)],
        compiler_params=params(40, 1),
    )(scal, q, k, v)


def mlp_kernel(
    scal, att_own, att_oth, tok, cot, wo, bo, gain, shift, up, ub, down, db,
    out_ref, gm_ref, ga_keep, ga_send, dn_keep, dn_send, up_keep, up_send, ow_keep, ow_send, vec_ref,
    mid, xhat_ref, scale_ref, normed, acc, back, dtile,
):
    step, sub = pl.program_id(0), pl.program_id(1)
    steps = pl.num_programs(0)
    core = scal[CORE]
    width = tok.shape[1]
    half = width // 2
    chunk = width // 16
    fchunk = half // 2

    def att_weight(which):
        return wo[pl.ds(pl.multiple_of(which * half, half), half), :]

    @pl.when((step == 0) & (sub == 0))
    def _():
        branch = dot(att_own[...], att_weight(core)) + dot(att_oth[...], att_weight(1 - core)) + row_of(bo)
        middle = tok[...].astype(f32) + branch
        xhat, scale = normalise(middle)
        mid[...] = middle
        xhat_ref[...] = xhat
        scale_ref[...] = scale
        normed[...] = (xhat * row_of(gain) + row_of(shift)).astype(bf16)
        acc[...] = jnp.zeros_like(acc)
        back[...] = jnp.zeros_like(back)
        vec_ref[...] = jnp.zeros_like(vec_ref)

    @pl.when(sub == 0)
    def _():
        tile = (step + (steps // 2) * (1 - core)) & (steps - 1)
        v = dot(normed[...], up[...]) + ub[...].astype(f32)
        sq = v * v
        t = jnp.tanh(v * (GELU_C + (GELU_C * GELU_A) * sq))
        half_t = 0.5 * (1.0 + t)
        act = (v * half_t).astype(bf16)
        slope = half_t + (0.5 * v) * (1.0 - t * t) * (GELU_C + (3.0 * GELU_C * GELU_A) * sq)
        acc[...] += dot(act, down[...])
        dtile[...] = dot_tn(act, cot[...]).astype(bf16).reshape(2, fchunk, width)
        grad = (dot_nt(cot[...], down[...]) * slope).astype(bf16)
        back[...] += dot_nt(grad, up[...])
        vec_ref[pl.ds(V_UP + tile, 1), :] = jnp.sum(grad.astype(f32), axis=0, keepdims=True)
        dup = dot_tn(normed[...], grad).astype(bf16).reshape(16, chunk, half)

        @pl.when(step < steps // 2)
        def _():
            for d in range(16):
                up_send[scal[PLACE_OTH + d], 0] = dup[d]

        @pl.when(step >= steps // 2)
        def _():
            for d in range(16):
                up_keep[scal[PLACE + d], 0] = dup[d]

    for which in range(2):

        @pl.when((sub == which) & (core == 0))
        def _():
            dn_keep[0] = dtile[which, :, :half]
            dn_send[0] = dtile[which, :, half:]

        @pl.when((sub == which) & (core != 0))
        def _():
            dn_keep[0] = dtile[which, :, half:]
            dn_send[0] = dtile[which, :, :half]

    @pl.when((step == steps - 1) & (sub == 1))
    def _():
        out_ref[...] = (mid[...] + acc[...] + row_of(db)).astype(bf16)
        g = back[...]
        xhat = xhat_ref[...]
        grad_out = cot[...].astype(f32)
        weighted = g * row_of(gain)
        dv = scale_ref[...] * (
            weighted
            - jnp.mean(weighted, axis=-1, keepdims=True)
            - xhat * jnp.mean(weighted * xhat, axis=-1, keepdims=True)
        )
        grad_middle = grad_out + dv
        gm_ref[...] = grad_middle
        branch = grad_middle.astype(bf16)

        def put(row, vector):
            vec_ref[row : row + 1, :] = vector[:, :half]
            vec_ref[row + 1 : row + 2, :] = vector[:, half:]

        put(V_DOWN, jnp.sum(grad_out, axis=0, keepdims=True))
        put(V_OUT, jnp.sum(branch.astype(f32), axis=0, keepdims=True))
        put(V_GAIN2, jnp.sum(g * xhat, axis=0, keepdims=True))
        put(V_SHIFT2, jnp.sum(g, axis=0, keepdims=True))
        ga_keep[...] = dot_nt(branch, att_weight(core)).astype(bf16)
        ga_send[...] = dot_nt(branch, att_weight(1 - core)).astype(bf16)
        wide_own = dot_tn(att_own[...], branch).astype(bf16).reshape(8, chunk, width)
        wide_oth = dot_tn(att_oth[...], branch).astype(bf16).reshape(8, chunk, width)

        def spread(keep, send):
            for d in range(8):
                own_place = scal[PLACE + core * 8 + d]
                oth_place = scal[PLACE + (1 - core) * 8 + d]
                ow_keep[own_place] = wide_own[d, :, keep]
                ow_keep[oth_place] = wide_oth[d, :, keep]
                ow_send[scal[PLACE_OTH + core * 8 + d]] = wide_own[d, :, send]
                ow_send[scal[PLACE_OTH + (1 - core) * 8 + d]] = wide_oth[d, :, send]

        left, right = slice(0, half), slice(half, width)
        pl.when(core == 0)(lambda: spread(left, right))
        pl.when(core != 0)(lambda: spread(right, left))


def mlp(scal, att_own, att_oth, tok, cot, wo, bo, gain, shift, up, ub, down, db):
    rows, width = tok.shape
    half = width // 2
    hidden = up.shape[1]
    steps = hidden // half
    tile = lambda s, sc: (s + (steps // 2) * (1 - sc[CORE])) & (steps - 1)
    place = lambda s, j, sc: (sc[PLACE + 2 * tile(s, sc) + j], 0, 0)
    place_oth = lambda s, j, sc: (sc[PLACE_OTH + 2 * tile(s, sc) + j], 0, 0)
    return pl.pallas_call(
        mlp_kernel,
        grid_spec=pltpu.PrefetchScalarGridSpec(
            num_scalar_prefetch=1,
            grid=(steps, 2),
            in_specs=[
                whole((rows, half)),
                whole((rows, half)),
                whole((rows, width)),
                whole((rows, width)),
                whole((width, width)),
                whole((width,)),
                whole((width,)),
                whole((width,)),
                pl.BlockSpec((width, half), lambda s, j, sc: (0, tile(s, sc))),
                pl.BlockSpec((1, half), lambda s, j, sc: (0, tile(s, sc))),
                pl.BlockSpec((half, width), lambda s, j, sc: (tile(s, sc), 0)),
                whole((width,)),
            ],
            out_specs=[
                whole((rows, width)),
                whole((rows, width)),
                whole((rows, half)),
                whole((rows, half)),
                pl.BlockSpec((1, half // 2, half), place),
                pl.BlockSpec((1, half // 2, half), place_oth),
                pl.BlockSpec((16, 1, width // 16, half), lambda s, j, sc: (0, jnp.maximum(s - steps // 2, 0), 0, 0)),
                pl.BlockSpec((16, 1, width // 16, half), lambda s, j, sc: (0, jnp.minimum(s, steps // 2 - 1), 0, 0)),
                whole((16, width // 16, half)),
                whole((16, width // 16, half)),
                whole((16, half)),
            ],
            scratch_shapes=[
                pltpu.VMEM((rows, width), f32),
                pltpu.VMEM((rows, width), f32),
                pltpu.VMEM((rows, 1), f32),
                pltpu.VMEM((rows, width), bf16),
                pltpu.VMEM((rows, width), f32),
                pltpu.VMEM((rows, width), f32),
                pltpu.VMEM((2, half // 2, width), bf16),
            ],
        ),
        out_shape=[
            sds((rows, width), bf16),
            sds((rows, width), f32),
            sds((rows, half), bf16),
            sds((rows, half), bf16),
            sds((16, half // 2, half), bf16),
            sds((16, half // 2, half), bf16),
            sds((16, steps // 2, width // 16, half), bf16),
            sds((16, steps // 2, width // 16, half), bf16),
            sds((16, width // 16, half), bf16),
            sds((16, width // 16, half), bf16),
            sds((16, half), f32),
        ],
        compiler_params=params(52, 2),
    )(scal, att_own, att_oth, tok, cot, wo, bo, gain, shift, up, ub.reshape(1, -1), down, db)


def pair_back(scal, q_ref, k_ref, v_ref, o_ref, lse_ref, do1, do2, n_ref, wq_ref, wk_ref, wv_ref, dv_ref, scratch):
    kb, vb, kt, db, dk_acc, dv_acc, x = scratch
    core = scal[CORE]
    rows = q_ref.shape[1]
    total = 2 * rows
    width = n_ref.shape[2]
    for hf in range(2):
        rel = core ^ hf
        cut = slice(hf * rows, (hf + 1) * rows)
        kb[cut, :] = k_ref[rel]
        vb[cut, :] = v_ref[rel]
        kt[:, cut] = k_ref[rel].T
    db[0] = do1[...]
    db[1] = do2[...]
    dk_acc[...] = jnp.zeros_like(dk_acc)
    dv_acc[...] = jnp.zeros_like(dv_acc)
    start = first_allowed(scal, total)
    for qb in range(total // QB):
        low = qb * QB
        rel = core ^ (low // rows)
        off = low % rows
        query = q_ref[rel, pl.ds(off, QB), :]
        grad = db[rel, pl.ds(off, QB), :]
        prod = (grad.astype(f32) * o_ref[rel, pl.ds(off, QB), :].astype(f32)).T
        begin = start[:, low : low + QB]
        parts = []
        for h in range(2):
            qh = head_part(query, h)
            gh = head_part(grad, h)
            delta = jnp.sum(prod[h * HEAD : (h + 1) * HEAD], axis=0, keepdims=True)
            total_log = lse_ref[0, h : h + 1, low : low + QB]
            acc = None
            for a, b in [(0, low), (low, low + QB)] if low else [(0, QB)]:
                s = dot_nt(kb[a:b, :], qh)
                p = jnp.where(allowed_block(begin, a, b, low), jnp.exp2(s * LOG2E - total_log), 0.0)
                dp = dot_nt(vb[a:b, :], gh)
                ds = (p * (dp - delta)).astype(bf16)
                dv_acc[a:b, :] += dot(p.astype(bf16), gh)
                dk_acc[a:b, :] += dot(ds, qh)
                part = dot(kt[h * HEAD : (h + 1) * HEAD, a:b], ds)
                acc = part if acc is None else acc + part
            parts.append(acc)
        x[rel, pl.ds(off, QB), 0:PAIR] = (jnp.concatenate(parts, axis=0).T * (HEAD**-0.5)).astype(bf16)
    for hf in range(2):
        rel = core ^ hf
        cut = slice(hf * rows, (hf + 1) * rows)
        x[rel, :, PAIR : 2 * PAIR] = dk_acc[cut, :].astype(bf16)
        dv = dv_acc[cut, :].astype(bf16)
        dv_ref[rel] = dv
        x[rel, :, 2 * PAIR :] = jnp.where(core == 0, dv, jnp.zeros_like(dv))
    grads = x[...].reshape(total, 3 * PAIR)
    dw = dot_tn(n_ref[...].reshape(total, width), grads).astype(bf16).reshape(16, width // 16, 3 * PAIR)
    back = (
        dot_nt(grads[:, :PAIR], wq_ref[...])
        + dot_nt(grads[:, PAIR : 2 * PAIR], wk_ref[...])
        + dot_nt(grads[:, 2 * PAIR :], wv_ref[...])
    )
    return dw, back, jnp.sum(grads.astype(f32), axis=0, keepdims=True)


def early_pairs_kernel(scal, *refs):
    inputs, (ow_keep, ow_recv), (t_ref, gn_ref, dv_ref, sums_ref), scratch = refs[:11], refs[11:13], refs[13:17], refs[17:]
    step = pl.program_id(0)
    dw, back, sums = pair_back(scal, *inputs, dv_ref, scratch)
    for d in range(16):
        t_ref[scal[PLACE + d], step] = dw[d]

    @pl.when(step == 0)
    def _():
        gn_ref[...] = back
        sums_ref[0:1, :] = sums
        t_ref[:, 2] = (ow_keep[...].astype(f32) + ow_recv[...].astype(f32)).astype(bf16)

    @pl.when(step != 0)
    def _():
        gn_ref[...] += back
        sums_ref[1:2, :] = sums


def last_pair_kernel(scal, *refs):
    inputs, (gn_in, sums_in, vec_in, own, oth), (t_ref, gn_ref, gs_ref, dv_ref), scratch = refs[:11], refs[11:16], refs[16:20], refs[20:]
    core = scal[CORE]
    dw, back, sums = pair_back(scal, *inputs, dv_ref, scratch)
    for d in range(16):
        t_ref[scal[PLACE + d]] = dw[d]
    rows = own.shape[0]
    half = own.shape[1] // 2
    g = back + gn_in[...]
    gn_ref[...] = g[:rows]
    gs_ref[...] = g[rows:].astype(bf16)
    gains, shifts = 0.0, 0.0
    for rel, tok in ((0, own), (1, oth)):
        xhat, _ = normalise(tok[...].astype(f32))
        part = g[rel * rows : (rel + 1) * rows]
        gains += jnp.sum(part * xhat, axis=0, keepdims=True)
        shifts += jnp.sum(part, axis=0, keepdims=True)
    every = [sums_in[0:1, :], sums_in[1:2, :], sums]
    query_bias = jnp.concatenate([s[:, :PAIR] for s in every], axis=1)
    value_bias = jnp.concatenate([s[:, 2 * PAIR :] for s in every], axis=1)
    none = jnp.zeros_like(query_bias)
    vec = [vec_in[...], gains[:, :half], gains[:, half:], shifts[:, :half], shifts[:, half:]]
    vec += [jnp.where(core == 0, query_bias, none), jnp.where(core == 0, none, query_bias), value_bias, none]
    t_ref[16] = split_high_low(jnp.concatenate(vec, axis=0))


def split_high_low(vec):
    high = vec.astype(bf16)
    return jnp.concatenate([high, (vec - high.astype(f32)).astype(bf16)], axis=0)


def join_high_low(block):
    return block[:V_ROWS].astype(f32) + block[V_ROWS:].astype(f32)


def back_specs(pairs_before, rows, width):
    half = width // 2
    pairs = half // PAIR
    pair = lambda p: p + pairs_before
    head = pl.BlockSpec((2, rows, PAIR), lambda p, sc: (0, 0, pair(p)))
    rel = pl.BlockSpec((rows, PAIR), lambda p, sc: (0, pair(p)))
    weight = pl.BlockSpec((width, PAIR), lambda p, sc: (0, sc[CORE] * pairs + pair(p)))
    in_specs = [head] * 4 + [
        pl.BlockSpec((1, 8, 2 * rows), lambda p, sc: (pair(p), 0, 0)),
        rel,
        rel,
        whole((2, rows, width)),
        weight,
        weight,
        pl.BlockSpec((width, PAIR), lambda p, sc: (0, pair(p))),
    ]
    scratch = [
        pltpu.VMEM((2 * rows, PAIR), bf16),
        pltpu.VMEM((2 * rows, PAIR), bf16),
        pltpu.VMEM((PAIR, 2 * rows), bf16),
        pltpu.VMEM((2, rows, PAIR), bf16),
        pltpu.VMEM((2 * rows, PAIR), f32),
        pltpu.VMEM((2 * rows, PAIR), f32),
        pltpu.VMEM((2, rows, 3 * PAIR), bf16),
    ]
    return in_specs, scratch


def early_pairs(scal, head_args, ow_keep, ow_recv):
    rows, width = head_args[7].shape[1:]
    half = width // 2
    in_specs, scratch = back_specs(0, rows, width)
    share = (16, width // 16, half)
    return pl.pallas_call(
        early_pairs_kernel,
        grid_spec=pltpu.PrefetchScalarGridSpec(
            num_scalar_prefetch=1,
            grid=(2,),
            in_specs=in_specs + [whole(share)] * 2,
            out_specs=[
                whole((16, 3, width // 16, half)),
                whole((2 * rows, width)),
                pl.BlockSpec((2, rows, PAIR), lambda p, sc: (0, 0, p)),
                whole((8, half)),
            ],
            scratch_shapes=scratch,
        ),
        out_shape=[
            sds((16, 3, width // 16, half), bf16),
            sds((2 * rows, width), f32),
            sds((2, rows, 2 * PAIR), bf16),
            sds((8, half), f32),
        ],
        compiler_params=params(48, 1),
    )(scal, *head_args, ow_keep, ow_recv)


def last_pair(scal, head_args, gn, sums, vec, own, oth):
    rows, width = own.shape
    half = width // 2
    in_specs, scratch = back_specs(2, rows, width)
    return pl.pallas_call(
        last_pair_kernel,
        grid_spec=pltpu.PrefetchScalarGridSpec(
            num_scalar_prefetch=1,
            grid=(1,),
            in_specs=in_specs
            + [whole((2 * rows, width)), whole((8, half)), whole((16, half)), whole((rows, width)), whole((rows, width))],
            out_specs=[
                whole((17, width // 16, half)),
                whole((rows, width)),
                whole((rows, width)),
                whole((2, rows, PAIR)),
            ],
            scratch_shapes=scratch,
        ),
        out_shape=[
            sds((17, width // 16, half), bf16),
            sds((rows, width), f32),
            sds((rows, width), bf16),
            sds((2, rows, PAIR), bf16),
        ],
        compiler_params=params(48, 1),
    )(scal, *head_args, gn, sums, vec, own, oth)


def first_norm_back_kernel(tok, gain, gn_own, gn_oth, grad_middle, out_ref):
    xhat, scale = normalise(tok[...].astype(f32))
    weighted = (gn_own[...] + gn_oth[...].astype(f32)) * row_of(gain)
    dv = scale * (
        weighted
        - jnp.mean(weighted, axis=-1, keepdims=True)
        - xhat * jnp.mean(weighted * xhat, axis=-1, keepdims=True)
    )
    out_ref[...] = (grad_middle[...] + dv).astype(bf16)


def first_norm_back(tok, gain, gn_own, gn_oth, grad_middle):
    rows, width = tok.shape
    tile = rows // 2
    block = pl.BlockSpec((tile, width), lambda s: (s, 0))
    return pl.pallas_call(
        first_norm_back_kernel,
        grid=(2,),
        in_specs=[block, whole((width,)), block, block, block],
        out_specs=block,
        out_shape=sds((rows, width), bf16),
        compiler_params=params(40, 1),
    )(tok, gain, gn_own, gn_oth, grad_middle)


def flip(values, bits, dp_count):
    pairs = [((d * 2 + c), ((d ^ bits[c]) * 2 + c)) for d in range(dp_count) for c in range(2)]
    return lax.ppermute(values, ("dp", "seq"), pairs)


def swap(values):
    return lax.ppermute(values, "seq", [(0, 1), (1, 0)])


STAGES = ((1, 2), (2, 1), (4, 4), (8, 8))


def halve(buffer):
    for bits in STAGES:
        half = buffer.shape[0] // 2
        buffer = buffer[:half] + flip(buffer[half:], bits, 16)
    return buffer


def add_with_vec_kernel(mine, theirs, out):
    count = out.shape[0] - 1
    out[:count] = mine[:count] + theirs[:count]
    out[count] = split_high_low(join_high_low(mine[2 * count]) + join_high_low(theirs[count]))


def halve_with_vec(buffer):
    for bits in STAGES:
        half = (buffer.shape[0] - 1) // 2
        theirs = flip(buffer[half:], bits, 16)
        buffer = pl.pallas_call(
            add_with_vec_kernel,
            out_shape=sds((half + 1,) + buffer.shape[1:], bf16),
            compiler_params=pltpu.CompilerParams(vmem_limit_bytes=32 << 20),
        )(buffer, theirs)
    return buffer


def finish_kernel(scal, *refs):
    (down, up, early, late, down2, up2, early2, late2), outs = refs[:8], refs[8:]
    gq, gk, gv, go, gu, gd = outs[:6]
    vec_out = outs[6:]
    half = down.shape[1]
    core = scal[CORE]

    def place(side, down, up, early, late):
        at = side * half
        gd[:, at : at + half] = down[...].astype(f32)
        for g in range(up.shape[0]):
            gu[:, (side * up.shape[0] + g) * half : (side * up.shape[0] + g + 1) * half] = up[g].astype(f32)
        go[:, at : at + half] = early[2].astype(f32)
        for p, piece in enumerate((early[0], early[1], late[0])):
            cols = slice(at + p * PAIR, at + (p + 1) * PAIR)
            gq[:, cols] = piece[:, :PAIR].astype(f32)
            gk[:, cols] = piece[:, PAIR : 2 * PAIR].astype(f32)
            if side == 0:
                gv[:, p * PAIR : (p + 1) * PAIR] = piece[:, 2 * PAIR :].astype(f32)

    @pl.when(core == 0)
    def _():
        place(0, down, up, early, late)
        place(1, down2, up2, early2, late2)

    @pl.when(core != 0)
    def _():
        place(1, down, up, early, late)
        place(0, down2, up2, early2, late2)

    put_vectors(join_high_low(late[1]) + join_high_low(late2[1]), vec_out)


def put_vectors(vec, refs):
    for ref, row in zip(refs, (V_GAIN1, V_SHIFT1, V_QUERY, V_VALUE, V_OUT, V_GAIN2, V_SHIFT2, V_UP, V_DOWN)):
        for k in range(ref.shape[0] // vec.shape[1]):
            ref[k * vec.shape[1] : (k + 1) * vec.shape[1]] = vec[row + k]


def finish(scal, own, oth, width, hidden, dp_count):
    half = width // 2
    rows = width // dp_count
    out_shape = [
        sds((rows, width), f32),
        sds((rows, width), f32),
        sds((rows, half), f32),
        sds((rows, width), f32),
        sds((rows, hidden), f32),
        sds((hidden // dp_count, width), f32),
    ] + [sds((n,), f32) for n in (width, width, width, half, width, width, width, hidden, width)]
    return pl.pallas_call(
        finish_kernel,
        grid_spec=pltpu.PrefetchScalarGridSpec(
            num_scalar_prefetch=1,
            grid=(1,),
            in_specs=[whole(x.shape) for x in own + oth],
            out_specs=[whole(s.shape) for s in out_shape],
        ),
        out_shape=out_shape,
        compiler_params=params(40, 1),
    )(scal, *own, *oth)


def finish_any(core, down, up, early, late):
    half = down.shape[2]
    vec = lax.psum(join_high_low(late[16]), ("dp", "seq"))

    def columns(pieces):
        mine = jnp.concatenate([x.reshape(-1, x.shape[-1]).astype(f32) for x in pieces], axis=1)
        share = lax.psum_scatter(mine, "dp", scatter_dimension=0, tiled=True)
        other = swap(share)
        return jnp.where(core == 0, jnp.concatenate([share, other], 1), jnp.concatenate([other, share], 1))

    thirds = [early[:, 0], early[:, 1], late[:16]]
    gq, gk, gv = (columns([x[..., i * PAIR : (i + 1) * PAIR] for x in thirds]) for i in range(3))
    go = columns([early[:, 2]])
    gu = columns([up[:, g] for g in range(up.shape[1])])
    gd = columns([down])
    flat = lambda row, n: vec[row : row + n].reshape(-1)
    vectors = [flat(V_GAIN1, 2), flat(V_SHIFT1, 2), flat(V_QUERY, 2), flat(V_VALUE, 1), flat(V_OUT, 2)]
    vectors += [flat(V_GAIN2, 2), flat(V_SHIFT2, 2), flat(V_UP, 8), flat(V_DOWN, 2)]
    return [gq, gk, gv[:, :half], go, gu, gd] + vectors


def per_device(
    dp_count,
    tokens,
    skip_values,
    doc_lengths,
    gain_first,
    shift_first,
    query_weight,
    query_bias,
    key_weight,
    value_weight,
    value_bias,
    out_weight,
    out_bias,
    gain_second,
    shift_second,
    up_weight,
    up_bias,
    down_weight,
    down_bias,
    cotangent,
):
    rows, width = tokens.shape
    hidden = up_weight.shape[1]
    core = lax.axis_index("seq")
    chunks = jnp.arange(16, dtype=jnp.int32)
    if dp_count == 16:
        off = chunks ^ lax.axis_index("dp")
        x_bit, y_bit, z_bits = off & 1, (off >> 1) & 1, ((off >> 2) & 1) * 2 + ((off >> 3) & 1)
        x_first, y_first = x_bit * 8 + y_bit * 4 + z_bits, y_bit * 8 + x_bit * 4 + z_bits
        place, place_oth = jnp.where(core == 0, x_first, y_first), jnp.where(core == 0, y_first, x_first)
    else:
        place = place_oth = chunks
    bounds = jnp.cumsum(doc_lengths[0])[:5]
    scal = jnp.concatenate([core[None], place, bounds, place_oth]).astype(jnp.int32)

    tokens_oth = swap(tokens)
    skip_oth = swap(skip_values)
    q, k, v, normed = project(
        scal, tokens, tokens_oth, skip_values, skip_oth, gain_first, shift_first,
        query_weight, query_bias, key_weight, value_weight, value_bias,
    )
    attended, log_total = attend(scal, q, k, v)
    att_oth = swap(attended[1])
    (output, grad_middle, ga_keep, ga_send, dn_keep, dn_send, up_keep, up_send, ow_keep, ow_send, vec) = mlp(
        scal, attended[0], att_oth, tokens, cotangent, out_weight, out_bias, gain_second, shift_second,
        up_weight, up_bias, down_weight, down_bias,
    )
    ga_oth = swap(ga_send)
    ow_recv = swap(ow_send)
    down_sum = dn_keep + swap(dn_send)
    up_sum = up_keep + swap(up_send)
    head_args = (q, k, v, attended, log_total, ga_keep, ga_oth, normed, query_weight, key_weight, value_weight)
    early, gn, dv_early, sums = early_pairs(scal, head_args, ow_keep, ow_recv)
    late, gn_own, gn_send, dv_late = last_pair(scal, head_args, gn, sums, vec, tokens, tokens_oth)
    grad_tokens = first_norm_back(tokens, gain_first, gn_own, swap(gn_send), grad_middle)
    dv = jnp.concatenate([dv_early, dv_late], axis=2)
    dv_oth = lax.ppermute(dv[1], "seq", [(1, 0)])
    grad_skip = jnp.where(core == 0, dv_oth, dv[0])
    if dp_count == 16:
        own = [halve(down_sum)[0], halve(up_sum)[0], halve(early)[0], halve_with_vec(late)]
        oth = [swap(x) for x in own]
        rest = finish(scal, own, oth, width, hidden, dp_count)
    else:
        rest = finish_any(core, down_sum, up_sum, early, late)
    gq, gk, gv, go, gu, gd, gain1, shift1, gqb, gvb, gob, gain2, shift2, gub, gdb = rest
    return (
        output, grad_tokens, grad_skip, gain1, shift1, gq, gqb, gk, gv, gvb, go, gob, gain2, shift2, gu, gub, gd, gdb,
    )


def solution(mesh):
    rows, full, shares = P(("dp", "seq"), None), P(), P("dp", None)
    return jax.shard_map(
        functools.partial(per_device, mesh.shape["dp"]),
        mesh=mesh,
        in_specs=(rows, rows, shares) + (full,) * 15 + (rows,),
        out_specs=(
            rows, rows, rows, full, full, shares, full, shares, shares, full, shares, full, full, full, shares, full,
            shares, full,
        ),
        check_vma=False,
    )
```

```python
import functools

import jax
import jax.numpy as jnp
from jax import lax
from jax.experimental import pallas as pl
from jax.experimental.pallas import tpu as pltpu
from jax.sharding import PartitionSpec as P

HEAD = 64
FRESH = 6
PAIR = 2 * HEAD
QB = 256
LOG2E = 1.4426950408889634
GELU_C = 0.7978845608028654
GELU_A = 0.044715
f32 = jnp.float32
bf16 = jnp.bfloat16
NT = (((1,), (1,)), ((), ()))
TN = (((0,), (0,)), ((), ()))
CORE, LENGTH, PLACE, PLACE_OTH, PLACE_Z, PLACE_Z_OTH = 0, 1, 6, 22, 38, 54
V_UP, V_DOWN, V_OUT, V_GAIN2, V_SHIFT2, V_GAIN1, V_SHIFT1, V_QUERY, V_VALUE = 0, 8, 10, 12, 14, 16, 18, 20, 22
V_ROWS = 24


def dot(left, right):
    return jnp.dot(left, right, preferred_element_type=f32)


def dot_nt(left, right):
    return lax.dot_general(left, right, NT, preferred_element_type=f32)


def dot_tn(left, right):
    return lax.dot_general(left, right, TN, preferred_element_type=f32)


def row_of(ref):
    return ref[...].astype(f32).reshape(1, -1)


def normalise(values):
    centre = values - jnp.mean(values, axis=-1, keepdims=True)
    spread = jnp.mean(centre * centre, axis=-1, keepdims=True)
    scale = lax.rsqrt(spread + 1e-05)
    return centre * scale, scale


def params(limit_mb, axes):
    return pltpu.CompilerParams(vmem_limit_bytes=limit_mb << 20, dimension_semantics=("arbitrary",) * axes)


def whole(shape):
    return pl.BlockSpec(shape, lambda *_: (0,) * len(shape))


def cost(micros):
    return pl.CostEstimate(flops=int(micros * 1e8), bytes_accessed=1 << 20, transcendentals=0)


def sds(shape, dtype):
    return jax.ShapeDtypeStruct(shape, dtype)


def project_kernel(scal, own, oth, skip_own, skip_oth, gain, shift, wq, bq, wk, wv, bv, q_ref, k_ref, v_ref, n_ref):
    step = pl.program_id(0)
    core = scal[CORE]
    mine = step < 2
    tokens = jnp.where(mine, own[...], oth[...]).astype(f32)
    xhat, _ = normalise(tokens)
    normed = (xhat * row_of(gain) + row_of(shift)).astype(bf16)
    n_ref[0] = normed
    half = q_ref.shape[2]
    bias = jnp.where(core == 0, row_of(bq)[:, :half], row_of(bq)[:, half:])
    q_ref[0] = (dot(normed, wq[...]) + bias).astype(bf16) * jnp.asarray(HEAD**-0.5, bf16)
    k_ref[0] = dot(normed, wk[...]).astype(bf16)

    @pl.when(core == 0)
    def _():
        v_ref[0] = (dot(normed, wv[...]) + row_of(bv)).astype(bf16)

    @pl.when(core != 0)
    def _():
        v_ref[0] = jnp.where(mine, skip_own[...], skip_oth[...])


def project(scal, own, oth, skip_own, skip_oth, gain, shift, wq, bq, wk, wv, bv):
    rows, width = own.shape
    half = width // 2
    tile = rows // 2
    first = lambda s, sc: (jnp.minimum(s, 1), 0)
    second = lambda s, sc: (jnp.maximum(s - 2, 0), 0)
    col = lambda s, sc: (0, sc[CORE])
    out = lambda s, sc: (s // 2, s % 2, 0)
    return pl.pallas_call(
        project_kernel,
        grid_spec=pltpu.PrefetchScalarGridSpec(
            num_scalar_prefetch=1,
            grid=(4,),
            in_specs=[
                pl.BlockSpec((tile, width), first),
                pl.BlockSpec((tile, width), second),
                pl.BlockSpec((tile, half), first),
                pl.BlockSpec((tile, half), second),
                whole((width,)),
                whole((width,)),
                pl.BlockSpec((width, half), col),
                whole((width,)),
                pl.BlockSpec((width, half), col),
                whole((width, half)),
                whole((half,)),
            ],
            out_specs=[pl.BlockSpec((1, tile, half), out)] * 3 + [pl.BlockSpec((1, tile, width), out)],
        ),
        out_shape=[sds((2, rows, half), bf16)] * 3 + [sds((2, rows, width), bf16)],
        compiler_params=params(56, 1),
    )(scal, own, oth, skip_own, skip_oth, gain, shift, wq, bq, wk, wv, bv)


def first_allowed(scal, total):
    place = lax.broadcasted_iota(jnp.int32, (1, total), 1)
    start = jnp.zeros((1, total), jnp.int32)
    bound = jnp.int32(0)
    for k in range(4):
        bound = bound + scal[LENGTH + k]
        start = jnp.where(place >= bound, bound, start)
    return jnp.where(place >= bound + scal[LENGTH + 4], place, start)


def allowed_block(start, low, high, first_query):
    key = lax.broadcasted_iota(jnp.int32, (high - low, QB), 0) + low
    ok = key >= start
    if high > first_query:
        ok = ok & (key <= lax.broadcasted_iota(jnp.int32, (high - low, QB), 1) + first_query)
    return ok


def head_part(values, h):
    lane = lax.broadcasted_iota(jnp.int32, values.shape, 1)
    return jnp.where((lane < HEAD) if h == 0 else (lane >= HEAD), values, jnp.zeros_like(values))


def key_rows(qb):
    return QB * (qb * (qb + 1) // 2), QB * (qb + 1)


def attend_kernel(scal, q_ref, k_ref, v_ref, o_own, o_oth, p_ref, kb, vt, o_ref):
    core = scal[CORE]
    rows = q_ref.shape[1]
    total = 2 * rows
    for half in range(2):
        rel = core ^ half
        kb[half * rows : (half + 1) * rows, :] = k_ref[rel]
        vt[:, half * rows : (half + 1) * rows] = v_ref[rel].T
    start = first_allowed(scal, total)
    items = [(qb, h) for qb in range(total // QB) for h in range(2)]

    def place(qb):
        return core ^ (qb * QB // rows), pl.ds(qb * QB % rows, QB)

    def scores(qb, h):
        low = qb * QB
        rel, at = place(qb)
        qh = head_part(q_ref[rel, at, :], h)
        return [(a, b, dot_nt(kb[a:b, :], qh)) for a, b in ([(0, low)] if low else []) + [(low, low + QB)]]

    done = {}
    ahead = scores(*items[0])
    for n, (qb, h) in enumerate(items):
        current = ahead
        if n + 1 < len(items):
            ahead = scores(*items[n + 1])
        low = qb * QB
        base, _ = key_rows(qb)
        begin = start[:, low : low + QB]
        peak = None
        masked = []
        for a, b, s in current:
            s = jnp.where(allowed_block(begin, a, b, low), s, -1e30)
            top = jnp.max(s, axis=0, keepdims=True)
            peak = top if peak is None else jnp.maximum(peak, top)
            masked.append((a, b, s))
        peak2 = peak * LOG2E
        raised = [(a, b, jnp.exp2(s * LOG2E - peak2)) for a, b, s in masked]
        summed = None
        for a, b, e in raised:
            part = jnp.sum(e, axis=0, keepdims=True)
            summed = part if summed is None else summed + part
        inverse = 1.0 / summed
        acc = None
        for a, b, e in raised:
            p = (e * inverse).astype(bf16)
            p_ref[0, h, base + a : base + b, :] = p
            part = dot(vt[h * HEAD : (h + 1) * HEAD, a:b], p)
            acc = part if acc is None else acc + part
        done[h] = acc
        if h == 1:
            rel, at = place(qb)
            o_ref[rel, at, :] = jnp.concatenate([done[0], done[1]], axis=0).T.astype(bf16)
    o_own[...] = o_ref[0]
    o_oth[...] = o_ref[1]


def attend(scal, q, k, v):
    _, rows, half = q.shape
    pairs = half // PAIR
    block = pl.BlockSpec((2, rows, PAIR), lambda p, sc: (0, 0, p))
    side = pl.BlockSpec((rows, PAIR), lambda p, sc: (0, p))
    packed = key_rows(2 * rows // QB)[0]
    return pl.pallas_call(
        attend_kernel,
        grid_spec=pltpu.PrefetchScalarGridSpec(
            num_scalar_prefetch=1,
            grid=(pairs,),
            in_specs=[block] * 3,
            out_specs=[side, side, pl.BlockSpec((1, 2, packed, QB), lambda p, sc: (p, 0, 0, 0))],
            scratch_shapes=[
                pltpu.VMEM((2 * rows, PAIR), bf16),
                pltpu.VMEM((PAIR, 2 * rows), bf16),
                pltpu.VMEM((2, rows, PAIR), bf16),
            ],
        ),
        out_shape=[sds((rows, half), bf16)] * 2 + [sds((pairs, 2, packed, QB), bf16)],
        cost_estimate=cost(10),
        compiler_params=params(56, 1),
    )(scal, q, k, v)


def mlp_kernel(
    scal, att_own, att_oth, tok, cot, wo, bo, gain, shift, up, ub, down, db,
    out_ref, gm_ref, ga_keep, ga_send, dn_keep, dn_send, up_keep, up_send, ow_keep, ow_send, vec_ref,
    mid, xhat_ref, scale_ref, normed, normed_t, acc, back, ubias, dtile, sems,
):
    step = pl.program_id(0)
    steps = pl.num_programs(0)
    core = scal[CORE]
    width = tok.shape[1]
    half = width // 2
    chunk = width // 16
    fchunk = half // 2
    parts = width // fchunk
    slot = step & 1

    def att_weight(which):
        return wo[pl.ds(pl.multiple_of(which * half, half), half), :]

    def copies(at, tile):
        found = []
        for n in range(parts):
            for k, (out, side, table) in enumerate(((dn_keep, core, PLACE), (dn_send, 1 - core, PLACE_OTH))):
                cols = pl.ds(pl.multiple_of(side * half, half), half)
                found.append(
                    pltpu.make_async_copy(
                        dtile.at[at, n, :, cols], out.at[scal[table + tile * parts + n]], sems.at[at, n, k]
                    )
                )
        return found

    @pl.when(step == 0)
    def _():
        branch = dot(att_own[...], att_weight(core)) + dot(att_oth[...], att_weight(1 - core)) + row_of(bo)
        middle = tok[...].astype(f32) + branch
        xhat, scale = normalise(middle)
        mid[...] = middle
        xhat_ref[...] = xhat
        scale_ref[...] = scale
        value = (xhat * row_of(gain) + row_of(shift)).astype(bf16)
        normed[...] = value
        normed_t[...] = value.T
        acc[...] = jnp.zeros_like(acc)
        back[...] = jnp.zeros_like(back)
        ubias[...] = row_of(ub)

    tile = (step + (steps // 2) * (1 - core)) & (steps - 1)

    @pl.when(step >= 2)
    def _():
        for copy in copies(slot, tile):
            copy.wait()

    v = dot(normed[...], up[...]) + ubias[:, pl.ds(pl.multiple_of(tile * width, width), width)]
    sq = v * v
    t = jnp.tanh(v * (GELU_C + (GELU_C * GELU_A) * sq))
    half_t = 0.5 * (1.0 + t)
    act = (v * half_t).astype(bf16)
    slope = half_t + (0.5 * v) * (1.0 - t * t) * (GELU_C + (3.0 * GELU_C * GELU_A) * sq)
    acc[...] += dot(act, down[...])
    dtile[slot] = dot_tn(act, cot[...]).astype(bf16).reshape(parts, fchunk, width)
    for copy in copies(slot, tile):
        copy.start()
    grad = (dot_nt(cot[...], down[...]) * slope).astype(bf16)
    back[...] += dot_nt(grad, up[...])
    sums = jnp.sum(grad.astype(f32), axis=0, keepdims=True)
    for g in range(2):
        vec_ref[pl.ds(V_UP + 2 * tile + g, 1), :] = sums[:, g * half : (g + 1) * half]
    dup = dot(normed_t[...], grad).astype(bf16).reshape(16, chunk, width)

    def place_up(ref, table):
        for d in range(16):
            for g in range(2):
                ref[scal[table + d], g] = dup[d, :, g * half : (g + 1) * half]

    pl.when(step < steps // 2)(lambda: place_up(up_send, PLACE_Z_OTH))
    pl.when(step >= steps // 2)(lambda: place_up(up_keep, PLACE_Z))

    @pl.when(step == steps - 1)
    def _():
        out_ref[...] = (mid[...] + acc[...] + row_of(db)).astype(bf16)
        g = back[...]
        xhat = xhat_ref[...]
        grad_out = cot[...].astype(f32)
        weighted = g * row_of(gain)
        dv = scale_ref[...] * (
            weighted
            - jnp.mean(weighted, axis=-1, keepdims=True)
            - xhat * jnp.mean(weighted * xhat, axis=-1, keepdims=True)
        )
        grad_middle = grad_out + dv
        gm_ref[...] = grad_middle
        branch = grad_middle.astype(bf16)

        def put(row, vector):
            vec_ref[row : row + 1, :] = vector[:, :half]
            vec_ref[row + 1 : row + 2, :] = vector[:, half:]

        put(V_DOWN, jnp.sum(grad_out, axis=0, keepdims=True))
        put(V_OUT, jnp.sum(branch.astype(f32), axis=0, keepdims=True))
        put(V_GAIN2, jnp.sum(g * xhat, axis=0, keepdims=True))
        put(V_SHIFT2, jnp.sum(g, axis=0, keepdims=True))
        ga_keep[...] = dot_nt(branch, att_weight(core)).astype(bf16)
        ga_send[...] = dot_nt(branch, att_weight(1 - core)).astype(bf16)
        wide_own = dot_tn(att_own[...], branch).astype(bf16).reshape(8, chunk, width)
        wide_oth = dot_tn(att_oth[...], branch).astype(bf16).reshape(8, chunk, width)

        def spread(keep, send):
            for d in range(8):
                own_place = scal[PLACE + core * 8 + d]
                oth_place = scal[PLACE + (1 - core) * 8 + d]
                ow_keep[own_place] = wide_own[d, :, keep]
                ow_keep[oth_place] = wide_oth[d, :, keep]
                ow_send[scal[PLACE_OTH + core * 8 + d]] = wide_own[d, :, send]
                ow_send[scal[PLACE_OTH + (1 - core) * 8 + d]] = wide_oth[d, :, send]

        left, right = slice(0, half), slice(half, width)
        pl.when(core == 0)(lambda: spread(left, right))
        pl.when(core != 0)(lambda: spread(right, left))
        for at in range(2):
            for copy in copies(at, tile):
                copy.wait()


def mlp(scal, att_own, att_oth, tok, cot, wo, bo, gain, shift, up, ub, down, db):
    rows, width = tok.shape
    half = width // 2
    hidden = up.shape[1]
    steps = hidden // width
    tile = lambda s, sc: (s + (steps // 2) * (1 - sc[CORE])) & (steps - 1)
    share = (16, 2, width // 16, half)
    return pl.pallas_call(
        mlp_kernel,
        grid_spec=pltpu.PrefetchScalarGridSpec(
            num_scalar_prefetch=1,
            grid=(steps,),
            in_specs=[
                whole((rows, half)),
                whole((rows, half)),
                whole((rows, width)),
                whole((rows, width)),
                whole((width, width)),
                whole((width,)),
                whole((width,)),
                whole((width,)),
                pl.BlockSpec((width, width), lambda s, sc: (0, tile(s, sc))),
                whole((hidden,)),
                pl.BlockSpec((width, width), lambda s, sc: (tile(s, sc), 0)),
                whole((width,)),
            ],
            out_specs=[
                whole((rows, width)),
                whole((rows, width)),
                whole((rows, half)),
                whole((rows, half)),
                pl.BlockSpec(memory_space=pl.ANY),
                pl.BlockSpec(memory_space=pl.ANY),
                pl.BlockSpec(share, lambda s, sc: (0, jnp.maximum(s - steps // 2, 0), 0, 0)),
                pl.BlockSpec(share, lambda s, sc: (0, jnp.minimum(s, steps // 2 - 1), 0, 0)),
                whole((16, width // 16, half)),
                whole((16, width // 16, half)),
                whole((16, half)),
            ],
            scratch_shapes=[
                pltpu.VMEM((rows, width), f32),
                pltpu.VMEM((rows, width), f32),
                pltpu.VMEM((rows, 1), f32),
                pltpu.VMEM((rows, width), bf16),
                pltpu.VMEM((width, rows), bf16),
                pltpu.VMEM((rows, width), f32),
                pltpu.VMEM((rows, width), f32),
                pltpu.VMEM((1, hidden), f32),
                pltpu.VMEM((2, 4, half // 2, width), bf16),
                pltpu.SemaphoreType.DMA((2, 4, 2)),
            ],
        ),
        out_shape=[
            sds((rows, width), bf16),
            sds((rows, width), f32),
            sds((rows, half), bf16),
            sds((rows, half), bf16),
            sds((16, half // 2, half), bf16),
            sds((16, half // 2, half), bf16),
            sds((16, steps, width // 16, half), bf16),
            sds((16, steps, width // 16, half), bf16),
            sds((16, width // 16, half), bf16),
            sds((16, width // 16, half), bf16),
            sds((16, half), f32),
        ],
        cost_estimate=cost(28),
        compiler_params=params(44, 1),
    )(scal, att_own, att_oth, tok, cot, wo, bo, gain, shift, up, ub, down, db)


def pair_back(scal, q_ref, k_ref, v_ref, o1, o2, p_ref, do1, do2, n_ref, x, scratch):
    vb, kt, db, ob, dk_acc, dv_acc = scratch
    core = scal[CORE]
    rows = q_ref.shape[1]
    total = 2 * rows
    width = n_ref.shape[2]
    for hf in range(2):
        rel = core ^ hf
        cut = slice(hf * rows, (hf + 1) * rows)
        vb[cut, :] = v_ref[rel]
        kt[:, cut] = k_ref[rel].T
    db[0] = do1[...]
    db[1] = do2[...]
    ob[0] = o1[...]
    ob[1] = o2[...]
    dk_acc[...] = jnp.zeros_like(dk_acc)
    dv_acc[...] = jnp.zeros_like(dv_acc)
    items = [(qb, h) for qb in reversed(range(total // QB)) for h in range(2)]

    def place(qb):
        return core ^ (qb * QB // rows), pl.ds(qb * QB % rows, QB)

    def grad_probs(qb, h):
        rel, at = place(qb)
        return dot_nt(vb[0 : (qb + 1) * QB, :], head_part(db[rel, at, :], h))

    ahead = grad_probs(*items[0])
    parts = []
    for n, (qb, h) in enumerate(items):
        dp = ahead
        if n + 1 < len(items):
            ahead = grad_probs(*items[n + 1])
        rel, at = place(qb)
        base, keys = key_rows(qb)
        cut = slice(h * HEAD, (h + 1) * HEAD)
        if h == 0:
            query_t = q_ref[rel, at, :].T
            grad_t = db[rel, at, :].T
            both = grad_t.astype(f32) * ob[rel, at, :].T.astype(f32)
        delta = jnp.sum(both[cut], axis=0, keepdims=True)
        p = p_ref[0, h, base : base + keys, :]
        ds = (p.astype(f32) * (dp - delta)).astype(bf16)
        dv_acc[cut, 0:keys] += dot_nt(grad_t[cut], p)
        dk_acc[cut, 0:keys] += dot_nt(query_t[cut], ds)
        parts.append(dot(kt[cut, 0:keys], ds))
        if h == 1:
            x[rel, at, 0:PAIR] = (jnp.concatenate(parts, axis=0).T * (HEAD**-0.5)).astype(bf16)
            parts = []
    for hf in range(2):
        rel = core ^ hf
        cut = slice(hf * rows, (hf + 1) * rows)
        x[rel, :, PAIR : 2 * PAIR] = dk_acc[:, cut].T.astype(bf16)
        x[rel, :, 2 * PAIR :] = dv_acc[:, cut].T.astype(bf16)
    grads = x[...].reshape(total, 3 * PAIR)
    dw = dot_tn(n_ref[...].reshape(total, width), grads).astype(bf16).reshape(16, width // 16, 3 * PAIR)
    return dw, jnp.sum(grads.astype(f32), axis=0, keepdims=True)


def first_pair_kernel(scal, *refs):
    inputs, (t_ref, x, sums_ref), scratch = refs[:9], refs[9:12], refs[12:]
    dw, sums = pair_back(scal, *inputs, x, scratch)
    sums_ref[0:1, :] = sums
    for d in range(16):
        t_ref[scal[PLACE + d]] = dw[d]


def second_pair_kernel(scal, *refs):
    inputs, (t_in, ow_keep, ow_recv), (t_ref, x, sums_ref), scratch = refs[:9], refs[9:12], refs[12:15], refs[15:]
    t_ref[:, 0] = t_in[...]
    t_ref[:, 2] = (ow_keep[...].astype(f32) + ow_recv[...].astype(f32)).astype(bf16)
    dw, sums = pair_back(scal, *inputs, x, scratch)
    sums_ref[0:1, :] = sums
    for d in range(16):
        t_ref[scal[PLACE + d], 1] = dw[d]


def last_pair_kernel(scal, *refs):
    inputs, (x0, x1, sums0, sums1, vec_in, own, oth, wq, wk, wv) = refs[:9], refs[9:19]
    (t_ref, gn_ref, gs_ref, dv_own, dv_send), (x, xs, ws, *scratch) = refs[19:24], refs[24:]
    core = scal[CORE]
    dw, sums = pair_back(scal, *inputs, x, scratch)
    for d in range(16):
        t_ref[scal[PLACE + d]] = dw[d]
    rows = own.shape[0]
    half = own.shape[1] // 2
    for p, piece in enumerate((x0, x1, x)):
        left = p * 3 * PAIR
        xs[:, left : left + 3 * PAIR] = piece[...].reshape(2 * rows, 3 * PAIR)
        dv_own[:, p * PAIR : (p + 1) * PAIR] = piece[0, :, 2 * PAIR :]
        dv_send[:, p * PAIR : (p + 1) * PAIR] = piece[1, :, 2 * PAIR :]
        for k, weight in enumerate((wq, wk, wv)):
            ws[:, left + k * PAIR : left + (k + 1) * PAIR] = weight[:, p * PAIR : (p + 1) * PAIR]

    @pl.when(core != 0)
    def _():
        for p in range(3):
            ws[:, p * 3 * PAIR + 2 * PAIR : (p + 1) * 3 * PAIR] = jnp.zeros((ws.shape[0], PAIR), bf16)

    g = dot_nt(xs[...], ws[...])
    gn_ref[...] = g[:rows]
    gs_ref[...] = g[rows:].astype(bf16)
    gains, shifts = 0.0, 0.0
    for rel, tok in ((0, own), (1, oth)):
        xhat, _ = normalise(tok[...].astype(f32))
        part = g[rel * rows : (rel + 1) * rows]
        gains += jnp.sum(part * xhat, axis=0, keepdims=True)
        shifts += jnp.sum(part, axis=0, keepdims=True)
    every = [sums0[0:1, :], sums1[0:1, :], sums]
    query_bias = jnp.concatenate([s[:, :PAIR] for s in every], axis=1)
    value_bias = jnp.concatenate([s[:, 2 * PAIR :] for s in every], axis=1)
    none = jnp.zeros_like(query_bias)
    vec = [vec_in[...], gains[:, :half], gains[:, half:], shifts[:, :half], shifts[:, half:]]
    vec += [jnp.where(core == 0, query_bias, none), jnp.where(core == 0, none, query_bias)]
    vec += [jnp.where(core == 0, value_bias, none), none]
    t_ref[16] = split_high_low(jnp.concatenate(vec, axis=0))


def pair_call(scal, pair, head_args, more):
    rows, width = head_args[8].shape[1:]
    half = width // 2
    chunk = width // 16
    head = pl.BlockSpec((2, rows, PAIR), lambda p, sc: (0, 0, pair))
    rel = pl.BlockSpec((rows, PAIR), lambda p, sc: (0, pair))
    in_specs = [head] * 3 + [
        rel,
        rel,
        pl.BlockSpec((1, 2, key_rows(2 * rows // QB)[0], QB), lambda p, sc: (pair, 0, 0, 0)),
        rel,
        rel,
        whole((2, rows, width)),
    ]
    scratch = [
        pltpu.VMEM((2 * rows, PAIR), bf16),
        pltpu.VMEM((PAIR, 2 * rows), bf16),
        pltpu.VMEM((2, rows, PAIR), bf16),
        pltpu.VMEM((2, rows, PAIR), bf16),
        pltpu.VMEM((PAIR, 2 * rows), f32),
        pltpu.VMEM((PAIR, 2 * rows), f32),
    ]
    grads = sds((2, rows, 3 * PAIR), bf16)
    more_specs = [whole(x.shape) for x in more]
    if pair == 2:
        column = pl.BlockSpec((width, half), lambda p, sc: (0, sc[CORE]))
        more_specs[-3:] = [column, column, whole((width, half))]
        scratch = [
            pltpu.VMEM(grads.shape, bf16),
            pltpu.VMEM((2 * rows, 9 * PAIR), bf16),
            pltpu.VMEM((width, 9 * PAIR), bf16),
        ] + scratch
        out_shape = [
            sds((17, chunk, half), bf16), sds((rows, width), f32), sds((rows, width), bf16), sds((rows, half), bf16),
            sds((rows, half), bf16),
        ]
    else:
        out_shape = [sds((16, 3, chunk, half) if pair else (16, chunk, half), bf16), grads, sds((8, half), f32)]
    return pl.pallas_call(
        (first_pair_kernel, second_pair_kernel, last_pair_kernel)[pair],
        grid_spec=pltpu.PrefetchScalarGridSpec(
            num_scalar_prefetch=1,
            grid=(1,),
            in_specs=in_specs + more_specs,
            out_specs=[whole(x.shape) for x in out_shape],
            scratch_shapes=scratch,
        ),
        out_shape=out_shape,
        cost_estimate=cost(12 if pair == 2 else 8),
        compiler_params=params(44, 1),
    )(scal, *head_args, *more)


def split_high_low(vec):
    high = vec.astype(bf16)
    return jnp.concatenate([high, (vec - high.astype(f32)).astype(bf16)], axis=0)


def join_high_low(block):
    return block[:V_ROWS].astype(f32) + block[V_ROWS:].astype(f32)


def first_norm_back_kernel(scal, tok, gain, gn_own, gn_oth, grad_middle, dv_own, dv_oth, out_ref, skip_ref):
    skip_ref[...] = jnp.where(scal[CORE] == 0, dv_oth[...], dv_own[...])
    xhat, scale = normalise(tok[...].astype(f32))
    weighted = (gn_own[...] + gn_oth[...].astype(f32)) * row_of(gain)
    dv = scale * (
        weighted
        - jnp.mean(weighted, axis=-1, keepdims=True)
        - xhat * jnp.mean(weighted * xhat, axis=-1, keepdims=True)
    )
    out_ref[...] = (grad_middle[...] + dv).astype(bf16)


def first_norm_back(scal, tok, gain, gn_own, gn_oth, grad_middle, dv_own, dv_oth):
    rows, width = tok.shape
    tile = rows // 2
    block = pl.BlockSpec((tile, width), lambda s, sc: (s, 0))
    narrow = pl.BlockSpec((tile, width // 2), lambda s, sc: (s, 0))
    return pl.pallas_call(
        first_norm_back_kernel,
        grid_spec=pltpu.PrefetchScalarGridSpec(
            num_scalar_prefetch=1,
            grid=(2,),
            in_specs=[block, whole((width,)), block, block, block, narrow, narrow],
            out_specs=[block, narrow],
        ),
        out_shape=[sds((rows, width), bf16), sds((rows, width // 2), bf16)],
        cost_estimate=cost(4),
        compiler_params=params(32, 1),
    )(scal, tok, gain, gn_own, gn_oth, grad_middle, dv_own, dv_oth)


def flip(values, bits, dp_count):
    pairs = [((d * 2 + c), ((d ^ bits[c]) * 2 + c)) for d in range(dp_count) for c in range(2)]
    return lax.ppermute(values, ("dp", "seq"), pairs)


def swap(values):
    return lax.ppermute(values, "seq", [(0, 1), (1, 0)])


STAGES = ((1, 2), (2, 1), (4, 4), (8, 8))
STAGES_Z = ((4, 4), (1, 2), (2, 1), (8, 8))


def after(value, *others):
    return lax.optimization_barrier((value,) + others)[0]


class Halving:
    def __init__(self, parts, stages=STAGES):
        self.parts = list(parts)
        self.size = parts[0].shape[0]
        self.stages = stages
        self.stage = 0

    def total(self, low, high):
        out = self.parts[0][low:high]
        for part in self.parts[1:]:
            out = out + part[low:high]
        return out

    def send(self, token):
        *self.parts, token = lax.optimization_barrier((*self.parts, token))
        if self.stage:
            self.parts = [lax.optimization_barrier(self.total(0, self.size))]
        self.size //= 2
        upper = self.total(self.size, 2 * self.size)
        self.parts = self.parts + [flip(upper, self.stages[self.stage], 16)]
        self.stage += 1
        return upper

    def result(self, token=None):
        if token is not None:
            *self.parts, _ = lax.optimization_barrier((*self.parts, token))
        return self.total(0, self.size)


def add_with_vec_kernel(mine, theirs, out):
    count = out.shape[0] - 1
    out[:count] = mine[:count] + theirs[:count]
    out[count] = split_high_low(join_high_low(mine[2 * count]) + join_high_low(theirs[count]))


class HalvingWithVec(Halving):
    def add(self):
        if len(self.parts) > 1:
            mine, theirs = self.parts
            half = theirs.shape[0] - 1
            summed = pl.pallas_call(
                add_with_vec_kernel,
                out_shape=sds(theirs.shape, bf16),
                compiler_params=pltpu.CompilerParams(vmem_limit_bytes=16 << 20),
            )(mine, theirs)
            self.parts = [summed]

    def send(self, token):
        *self.parts, token = lax.optimization_barrier((*self.parts, token))
        self.add()
        buffer = self.parts[0]
        upper = buffer[(buffer.shape[0] - 1) // 2 :]
        self.parts = [buffer, flip(upper, self.stages[self.stage], 16)]
        self.stage += 1
        return upper

    def result(self, token=None):
        self.add()
        return self.parts[0]


def both_sides(core, own, oth, put):
    @pl.when(core == 0)
    def _():
        put(0, own)
        put(1, oth)

    @pl.when(core != 0)
    def _():
        put(1, own)
        put(0, oth)


def finish_feed_kernel(scal, down, up, down2, up2, gu, gd):
    half = down.shape[1]

    def put(side, shares):
        down, up = shares
        gd[:, side * half : (side + 1) * half] = down[...].astype(f32)
        for g in range(up.shape[0]):
            at = (side * up.shape[0] + g) * half
            gu[:, at : at + half] = up[g].astype(f32)

    both_sides(scal[CORE], (down, up), (down2, up2), put)


def finish_heads_kernel(scal, early, late, early2, late2, gq, gk, gv, go, *vectors):
    half = early.shape[2]

    def put(side, shares):
        early, late = shares
        at = side * half
        go[:, at : at + half] = early[2].astype(f32)
        for p, piece in enumerate((early[0], early[1], late[0])):
            cols = slice(at + p * PAIR, at + (p + 1) * PAIR)
            gq[:, cols] = piece[:, :PAIR].astype(f32)
            gk[:, cols] = piece[:, PAIR : 2 * PAIR].astype(f32)
            if side == 0:
                gv[:, p * PAIR : (p + 1) * PAIR] = piece[:, 2 * PAIR :].astype(f32)

    both_sides(scal[CORE], (early, late), (early2, late2), put)
    vec = join_high_low(late[1]) + join_high_low(late2[1])
    for ref, row in zip(vectors, (V_GAIN1, V_SHIFT1, V_QUERY, V_VALUE, V_OUT, V_GAIN2, V_SHIFT2, V_UP, V_DOWN)):
        for k in range(ref.shape[0] // half):
            ref[k * half : (k + 1) * half] = vec[row + k]


def finish(kernel, scal, shares, out_shape):
    out_shape = [sds(shape, f32) for shape in out_shape]
    return pl.pallas_call(
        kernel,
        grid_spec=pltpu.PrefetchScalarGridSpec(
            num_scalar_prefetch=1,
            grid=(1,),
            in_specs=[whole(x.shape) for x in shares],
            out_specs=[whole(s.shape) for s in out_shape],
        ),
        out_shape=out_shape,
        cost_estimate=cost(3),
        compiler_params=params(24, 1),
    )(scal, *shares)


def finish_any(core, down, up, early, late):
    half = down.shape[2]
    vec = lax.psum(join_high_low(late[16]), ("dp", "seq"))

    def columns(pieces):
        mine = jnp.concatenate([x.reshape(-1, x.shape[-1]).astype(f32) for x in pieces], axis=1)
        share = lax.psum_scatter(mine, "dp", scatter_dimension=0, tiled=True)
        other = swap(share)
        return jnp.where(core == 0, jnp.concatenate([share, other], 1), jnp.concatenate([other, share], 1))

    thirds = [early[:, 0], early[:, 1], late[:16]]
    gq, gk, gv = (columns([x[..., i * PAIR : (i + 1) * PAIR] for x in thirds]) for i in range(3))
    go = columns([early[:, 2]])
    gu = columns([up[:, g] for g in range(up.shape[1])])
    gd = columns([down])
    flat = lambda row, n: vec[row : row + n].reshape(-1)
    vectors = [flat(V_GAIN1, 2), flat(V_SHIFT1, 2), flat(V_QUERY, 2), flat(V_VALUE, 1), flat(V_OUT, 2)]
    vectors += [flat(V_GAIN2, 2), flat(V_SHIFT2, 2), flat(V_UP, 8), flat(V_DOWN, 2)]
    return [gq, gk, gv[:, :half], go, gu, gd] + vectors


def per_device(
    dp_count,
    tokens,
    skip_values,
    doc_lengths,
    gain_first,
    shift_first,
    query_weight,
    query_bias,
    key_weight,
    value_weight,
    value_bias,
    out_weight,
    out_bias,
    gain_second,
    shift_second,
    up_weight,
    up_bias,
    down_weight,
    down_bias,
    cotangent,
):
    rows, width = tokens.shape
    hidden = up_weight.shape[1]
    core = lax.axis_index("seq")
    chunks = jnp.arange(16, dtype=jnp.int32)
    if dp_count == 16:
        off = chunks ^ lax.axis_index("dp")
        x_bit, y_bit, z_bits = off & 1, (off >> 1) & 1, ((off >> 2) & 1) * 2 + ((off >> 3) & 1)
        x_first, y_first = x_bit * 8 + y_bit * 4 + z_bits, y_bit * 8 + x_bit * 4 + z_bits
        place, place_oth = jnp.where(core == 0, x_first, y_first), jnp.where(core == 0, y_first, x_first)
        z_first = lambda xy: (xy & 12) // 2 + (xy & 2) * 4 + (xy & 1)
        places = [place, place_oth, z_first(place), z_first(place_oth)]
    else:
        places = [chunks] * 4
    scal = jnp.concatenate([core[None], doc_lengths[0, :5]] + places).astype(jnp.int32)

    tokens_oth = swap(tokens)
    skip_oth = swap(skip_values)
    q, k, v, normed = project(
        scal, tokens, tokens_oth, skip_values, skip_oth, gain_first, shift_first,
        query_weight, query_bias, key_weight, value_weight, value_bias,
    )
    att_own, att_send, probs = attend(scal, q, k, v)
    att_oth = swap(att_send)
    (output, grad_middle, ga_keep, ga_send, dn_keep, dn_send, up_keep, up_send, ow_keep, ow_send, vec) = mlp(
        scal, att_own, att_oth, tokens, cotangent, out_weight, out_bias, gain_second, shift_second,
        up_weight, up_bias, down_weight, down_bias,
    )
    whole_tiles = dp_count == 16
    ga_oth = swap(ga_send)
    dn_send, up_send, ow_send, _ = lax.optimization_barrier((dn_send, up_send, ow_send, ga_oth))
    dn_recv, up_recv, ow_recv = swap(dn_send), swap(up_send), swap(ow_send)
    down = Halving((dn_keep, dn_recv))
    up = Halving((up_keep, up_recv), STAGES_Z)
    head_args = [q, k, v, att_own, att_send, probs, ga_keep, ga_oth, normed]
    t0, x0, sums0 = pair_call(scal, 0, head_args, ())
    token = sums0
    if whole_tiles:
        token = down.send(token)
        token = up.send(token)
    t01, x1, sums1 = pair_call(scal, 1, head_args, (after(t0, token), ow_keep, ow_recv))
    token = sums1
    early = Halving((t01,))
    if whole_tiles:
        token = early.send(token)
        token = down.send(token)
    late, gn_own, gn_send, dv_own, dv_send = pair_call(
        scal, 2, head_args,
        (after(x0, token), x1, sums0, sums1, vec, tokens, tokens_oth, query_weight, key_weight, value_weight),
    )
    gn_oth = swap(gn_send)
    dv_oth = lax.ppermute(dv_send, "seq", [(1, 0)])
    if whole_tiles:
        last = HalvingWithVec((late,))
        token = gn_send
        for chain in (last, down, up, early, last, down):
            token = chain.send(token)
        gn_own, gn_oth, dv_own, dv_oth, token = lax.optimization_barrier((gn_own, gn_oth, dv_own, dv_oth, token))
    grad_tokens, grad_skip = first_norm_back(scal, tokens, gain_first, gn_own, gn_oth, grad_middle, dv_own, dv_oth)
    if whole_tiles:
        token = grad_tokens
        for chain in (up, early, last, up, early, last):
            token = chain.send(token)
        shares = [down.result(token)[0], up.result(token)[0]]
        shares += [swap(x) for x in shares]
        rows_in, wide = width // dp_count, (width // dp_count, width)
        gu, gd = finish(finish_feed_kernel, scal, shares, [(rows_in, hidden), (hidden // dp_count, width)])
        shares = [early.result(token)[0], last.result()]
        shares += [swap(x) for x in shares]
        vectors = [(n,) for n in (width, width, width, width // 2, width, width, width, hidden, width)]
        rest = finish(
            finish_heads_kernel, scal, shares, [wide, wide, (rows_in, width // 2), wide] + vectors
        )
        gq, gk, gv, go, gain1, shift1, gqb, gvb, gob, gain2, shift2, gub, gdb = rest
    else:
        rest = finish_any(core, down.result(), up.result(), early.result(), late)
        gq, gk, gv, go, gu, gd, gain1, shift1, gqb, gvb, gob, gain2, shift2, gub, gdb = rest
    return (
        output, grad_tokens, grad_skip, gain1, shift1, gq, gqb, gk, gv, gvb, go, gob, gain2, shift2, gu, gub, gd, gdb,
    )


def solution(mesh):
    rows, full, shares = P(("dp", "seq"), None), P(), P("dp", None)
    return jax.shard_map(
        functools.partial(per_device, mesh.shape["dp"]),
        mesh=mesh,
        in_specs=(rows, rows, shares) + (full,) * 15 + (rows,),
        out_specs=(
            rows, rows, rows, full, full, shares, full, shares, shares, full, shares, full, full, full, shares, full,
            shares, full,
        ),
        check_vma=False,
    )
```

```python
import functools

import jax
import jax.numpy as jnp
from jax import lax
from jax.experimental import pallas as pl
from jax.experimental.pallas import tpu as pltpu
from jax.sharding import PartitionSpec as P

HEAD = 64
FRESH = 6
PAIR = 2 * HEAD
QB = 256
FRONT_MB = 46
MLP_MB = 52
LOG2E = 1.4426950408889634
GELU_C = 0.7978845608028654
GELU_A = 0.044715
f32 = jnp.float32
bf16 = jnp.bfloat16
NT = (((1,), (1,)), ((), ()))
TN = (((0,), (0,)), ((), ()))
CORE, LENGTH, PLACE, PLACE_OTH, PLACE_Z, PLACE_Z_OTH = 0, 1, 6, 22, 38, 54
V_UP, V_DOWN, V_OUT, V_GAIN2, V_SHIFT2, V_GAIN1, V_SHIFT1, V_QUERY, V_VALUE = 0, 8, 10, 12, 14, 16, 18, 20, 22
V_ROWS = 24


def dot(left, right):
    return jnp.dot(left, right, preferred_element_type=f32)


def dot_nt(left, right):
    return lax.dot_general(left, right, NT, preferred_element_type=f32)


def dot_tn(left, right):
    return lax.dot_general(left, right, TN, preferred_element_type=f32)


def row_of(ref):
    return ref[...].astype(f32).reshape(1, -1)


def normalise(values):
    centre = values - jnp.mean(values, axis=-1, keepdims=True)
    spread = jnp.mean(centre * centre, axis=-1, keepdims=True)
    scale = lax.rsqrt(spread + 1e-05)
    return centre * scale, scale


def params(limit_mb, axes):
    return pltpu.CompilerParams(vmem_limit_bytes=limit_mb << 20, dimension_semantics=("arbitrary",) * axes)


def whole(shape):
    return pl.BlockSpec(shape, lambda *_: (0,) * len(shape))


def cost(micros):
    return pl.CostEstimate(flops=int(micros), bytes_accessed=0, transcendentals=0)


def sds(shape, dtype):
    return jax.ShapeDtypeStruct(shape, dtype)


def first_allowed(scal, total):
    place = lax.broadcasted_iota(jnp.int32, (1, total), 1)
    start = jnp.zeros((1, total), jnp.int32)
    bound = jnp.int32(0)
    for k in range(4):
        bound = bound + scal[LENGTH + k]
        start = jnp.where(place >= bound, bound, start)
    return jnp.where(place >= bound + scal[LENGTH + 4], place, start)


def allowed_block(start, low, high, first_query):
    key = lax.broadcasted_iota(jnp.int32, (high - low, QB), 0) + low
    ok = key >= start
    if high > first_query:
        ok = ok & (key <= lax.broadcasted_iota(jnp.int32, (high - low, QB), 1) + first_query)
    return ok


def head_part(values, h):
    lane = lax.broadcasted_iota(jnp.int32, values.shape, 1)
    return jnp.where((lane < HEAD) if h == 0 else (lane >= HEAD), values, jnp.zeros_like(values))


def key_rows(qb):
    return QB * (qb * (qb + 1) // 2), QB * (qb + 1)


def attend_pair(scal, pair, q_ref, k_ref, v_ref, o_own, o_oth, probs, kb, vt, ob):
    core = scal[CORE]
    rows = q_ref.shape[1]
    total = 2 * rows
    lanes = slice(pair * PAIR, (pair + 1) * PAIR)
    for half in range(2):
        rel = core ^ half
        kb[half * rows : (half + 1) * rows, :] = k_ref[rel, :, lanes]
        vt[:, half * rows : (half + 1) * rows] = v_ref[rel, :, lanes].T
    start = first_allowed(scal, total)
    items = [(qb, h) for qb in range(total // QB) for h in range(2)]

    def place(qb):
        return core ^ (qb * QB // rows), pl.ds(qb * QB % rows, QB)

    def scores(qb, h):
        low = qb * QB
        rel, at = place(qb)
        qh = head_part(q_ref[rel, at, lanes], h)
        return [(a, b, dot_nt(kb[a:b, :], qh)) for a, b in ([(0, low)] if low else []) + [(low, low + QB)]]

    done = {}
    ahead = scores(*items[0])
    for n, (qb, h) in enumerate(items):
        current = ahead
        if n + 1 < len(items):
            ahead = scores(*items[n + 1])
        low = qb * QB
        base, _ = key_rows(qb)
        begin = start[:, low : low + QB]
        peak = None
        masked = []
        for a, b, s in current:
            s = jnp.where(allowed_block(begin, a, b, low), s, -1e30)
            top = jnp.max(s, axis=0, keepdims=True)
            peak = top if peak is None else jnp.maximum(peak, top)
            masked.append((a, b, s))
        peak2 = peak * LOG2E
        raised = [(a, b, jnp.exp2(s * LOG2E - peak2)) for a, b, s in masked]
        summed = None
        for a, b, e in raised:
            part = jnp.sum(e, axis=0, keepdims=True)
            summed = part if summed is None else summed + part
        inverse = 1.0 / summed
        acc = None
        for a, b, e in raised:
            p = (e * inverse).astype(bf16)
            probs[h, base + a : base + b, :] = p
            part = dot(vt[h * HEAD : (h + 1) * HEAD, a:b], p)
            acc = part if acc is None else acc + part
        done[h] = acc
        if h == 1:
            rel, at = place(qb)
            ob[rel, at, :] = jnp.concatenate([done[0], done[1]], axis=0).T.astype(bf16)
    o_own[:, lanes] = ob[0]
    o_oth[:, lanes] = ob[1]


def front_kernel(
    scal, tok, oth, skip, skip_oth, vectors, wq, wk, wv,
    q_ref, k_ref, v_ref, n_ref, o_own, o_oth, p_ref,
    tok_s, skip_s, wq_s, wk_s, wv_s, probs, kb, vt, ob, sems, psems,
):
    core = scal[CORE]
    half = q_ref.shape[2]
    cols = pl.ds(pl.multiple_of(core * half, half), half)
    pieces = (
        (wq.at[:, cols], wq_s), (wk.at[:, cols], wk_s), (tok, tok_s), (wv, wv_s), (skip, skip_s),
    )
    fetch = [pltpu.make_async_copy(src, dst, sems.at[n]) for n, (src, dst) in enumerate(pieces)]
    for copy in fetch:
        copy.start()
    joined = row_of(vectors)
    width = 2 * half
    gain, shift, bq, bv = (joined[:, at : at + n] for at, n in ((0, width), (width, width), (2 * width, width), (3 * width, half)))
    bias = jnp.where(core == 0, bq[:, :half], bq[:, half:])
    for rel in (1, 0):
        if rel == 0:
            fetch[2].wait()
        xhat, _ = normalise((oth if rel else tok_s)[...].astype(f32))
        normed = (xhat * gain + shift).astype(bf16)
        n_ref[rel] = normed
        if rel:
            fetch[0].wait()
        q_ref[rel] = (dot(normed, wq_s[...]) + bias).astype(bf16) * jnp.asarray(HEAD**-0.5, bf16)
        if rel:
            fetch[1].wait()
        k_ref[rel] = dot(normed, wk_s[...]).astype(bf16)
    fetch[3].wait()
    fetch[4].wait()

    @pl.when(core == 0)
    def _():
        for rel in range(2):
            v_ref[rel] = (dot(n_ref[rel], wv_s[...]) + bv).astype(bf16)

    @pl.when(core != 0)
    def _():
        v_ref[0] = skip_s[...]
        v_ref[1] = skip_oth[...]

    out = []
    for pair in range(half // PAIR):
        slot = pair % 2
        if pair >= 2:
            out[pair - 2].wait()
        attend_pair(scal, pair, q_ref, k_ref, v_ref, o_own, o_oth, probs.at[slot], kb, vt, ob)
        out.append(pltpu.make_async_copy(probs.at[slot], p_ref.at[pair], psems.at[pair]))
        out[pair].start()
    for copy in out[-2:]:
        copy.wait()


def front(scal, tok, oth, skip, skip_oth, vectors, wq, wk, wv):
    rows, width = tok.shape
    half = width // 2
    pairs = half // PAIR
    packed = key_rows(2 * rows // QB)[0]
    here = pl.BlockSpec(memory_space=pltpu.VMEM)
    far = pl.BlockSpec(memory_space=pltpu.HBM)
    return pl.pallas_call(
        front_kernel,
        in_specs=[pl.BlockSpec(memory_space=pltpu.SMEM), far, here, far, here, here, far, far, far],
        out_specs=[here] * 6 + [far],
        scratch_shapes=[
            pltpu.VMEM((rows, width), f32),
            pltpu.VMEM((rows, half), bf16),
            pltpu.VMEM((width, half), bf16),
            pltpu.VMEM((width, half), bf16),
            pltpu.VMEM((width, half), bf16),
            pltpu.VMEM((2, 2, packed, QB), bf16),
            pltpu.VMEM((2 * rows, PAIR), bf16),
            pltpu.VMEM((PAIR, 2 * rows), bf16),
            pltpu.VMEM((2, rows, PAIR), bf16),
            pltpu.SemaphoreType.DMA((5,)),
            pltpu.SemaphoreType.DMA((pairs,)),
        ],
        out_shape=[sds((2, rows, half), bf16)] * 3
        + [sds((2, rows, width), bf16)]
        + [sds((rows, half), bf16)] * 2
        + [sds((pairs, 2, packed, QB), bf16)],
        cost_estimate=cost(14),
        compiler_params=pltpu.CompilerParams(vmem_limit_bytes=FRONT_MB << 20),
    )(scal, tok, oth, skip, skip_oth, vectors, wq, wk, wv)


TILES = 4


def mlp_kernel(
    scal, att_own, att_oth, tok_far, cot_far, wo_far, bo, gain, shift, up_far, ub, down_far, db,
    out_far, gm_far, ga_keep, ga_send, dn_keep, dn_send, up_keep, up_send, ow_keep, ow_send, vec_ref,
    tok, cot, wo, up, down, ubias, normed, normed_t, xhat_ref, out_s, gm_s, dn_s, up_s, sems, out_sems, dn_sems, up_sems,
):
    core = scal[CORE]
    width = tok.shape[1]
    half = width // 2
    chunk = width // 16
    fchunk = half // 2
    parts = width // fchunk
    tiles = [(s + (TILES // 2) * (1 - core)) & (TILES - 1) for s in range(TILES)]
    span = [pl.ds(pl.multiple_of(t * width, width), width) for t in tiles]

    def fetch(src, dst, n):
        copy = pltpu.make_async_copy(src, dst, sems.at[n])
        copy.start()
        return copy

    wo_in, tok_in = fetch(wo_far, wo, 0), fetch(tok_far, tok, 1)
    up_in, down_in = [fetch(up_far.at[:, span[0]], up.at[0], 3)], []
    cot_in = fetch(cot_far, cot, 2)
    for s in range(TILES):
        if s:
            up_in.append(fetch(up_far.at[:, span[s]], up.at[s], 3 + 2 * s))
        down_in.append(fetch(down_far.at[span[s], :], down.at[s], 4 + 2 * s))

    def att_weight(which):
        return wo[pl.ds(pl.multiple_of(which * half, half), half), :]

    ubias[...] = row_of(ub)
    wo_in.wait()
    tok_in.wait()
    branch = dot(att_own[...], att_weight(core)) + dot(att_oth[...], att_weight(1 - core)) + row_of(bo)
    middle = tok[...].astype(f32) + branch
    xhat, scale = normalise(middle)
    xhat_ref[...] = xhat
    value = (xhat * row_of(gain) + row_of(shift)).astype(bf16)
    normed[...] = value
    normed_t[...] = value.T
    acc = middle + row_of(db)
    back = None
    sent = []
    up_in[0].wait()
    cot_in.wait()
    down_in[0].wait()
    ahead = dot(normed[...], up[0])
    for s in range(TILES):
        wide = dot_nt(cot[...], down[s])
        v = ahead + ubias[:, span[s]]
        if s + 1 < TILES:
            up_in[s + 1].wait()
            down_in[s + 1].wait()
            ahead = dot(normed[...], up[s + 1])
        sq = v * v
        t = jnp.tanh(v * (GELU_C + (GELU_C * GELU_A) * sq))
        half_t = 0.5 * (1.0 + t)
        act = (v * half_t).astype(bf16)
        slope = half_t + (0.5 * v) * (1.0 - t * t) * (GELU_C + (3.0 * GELU_C * GELU_A) * sq)
        grad = (wide * slope).astype(bf16)
        dn_s[s] = dot_tn(act, cot[...]).astype(bf16).reshape(parts, fchunk, width)
        for n in range(parts):
            for k, (out, side, table) in enumerate(((dn_keep, core, PLACE), (dn_send, 1 - core, PLACE_OTH))):
                cols = pl.ds(pl.multiple_of(side * half, half), half)
                place = scal[table + tiles[s] * parts + n]
                sent.append(pltpu.make_async_copy(dn_s.at[s, n, :, cols], out.at[place], dn_sems.at[s, n, k]))
                sent[-1].start()
        dup = dot(normed_t[...], grad).astype(bf16).reshape(16, chunk, width)
        keep = s >= TILES // 2
        for d in range(16):
            place = scal[(PLACE_Z if keep else PLACE_Z_OTH) + d]
            for g in range(2):
                up_s[s, place, g] = dup[d, :, g * half : (g + 1) * half]
        at = pl.ds(2 * (s % (TILES // 2)), 2)
        sent.append(pltpu.make_async_copy(up_s.at[s], (up_keep if keep else up_send).at[:, at], up_sems.at[s]))
        sent[-1].start()
        acc = acc + dot(act, down[s])
        part = dot_nt(grad, up[s])
        back = part if back is None else back + part
        sums = jnp.sum(grad.astype(f32), axis=0, keepdims=True)
        for g in range(2):
            vec_ref[pl.ds(V_UP + 2 * tiles[s] + g, 1), :] = sums[:, g * half : (g + 1) * half]
    out_s[...] = acc.astype(bf16)
    sent.append(pltpu.make_async_copy(out_s, out_far, out_sems.at[0]))
    sent[-1].start()
    xhat = xhat_ref[...]
    grad_out = cot[...].astype(f32)
    weighted = back * row_of(gain)
    dv = scale * (
        weighted
        - jnp.mean(weighted, axis=-1, keepdims=True)
        - xhat * jnp.mean(weighted * xhat, axis=-1, keepdims=True)
    )
    grad_middle = grad_out + dv
    gm_s[...] = grad_middle
    sent.append(pltpu.make_async_copy(gm_s, gm_far, out_sems.at[1]))
    sent[-1].start()
    branch = grad_middle.astype(bf16)

    def put(row, vector):
        vec_ref[row : row + 1, :] = vector[:, :half]
        vec_ref[row + 1 : row + 2, :] = vector[:, half:]

    put(V_DOWN, jnp.sum(grad_out, axis=0, keepdims=True))
    put(V_OUT, jnp.sum(branch.astype(f32), axis=0, keepdims=True))
    put(V_GAIN2, jnp.sum(back * xhat, axis=0, keepdims=True))
    put(V_SHIFT2, jnp.sum(back, axis=0, keepdims=True))
    ga_keep[...] = dot_nt(branch, att_weight(core)).astype(bf16)
    ga_send[...] = dot_nt(branch, att_weight(1 - core)).astype(bf16)
    wide_own = dot_tn(att_own[...], branch).astype(bf16).reshape(8, chunk, width)
    wide_oth = dot_tn(att_oth[...], branch).astype(bf16).reshape(8, chunk, width)

    def spread(keep, send):
        for d in range(8):
            own_place = scal[PLACE + core * 8 + d]
            oth_place = scal[PLACE + (1 - core) * 8 + d]
            ow_keep[own_place] = wide_own[d, :, keep]
            ow_keep[oth_place] = wide_oth[d, :, keep]
            ow_send[scal[PLACE_OTH + core * 8 + d]] = wide_own[d, :, send]
            ow_send[scal[PLACE_OTH + (1 - core) * 8 + d]] = wide_oth[d, :, send]

    left, right = slice(0, half), slice(half, width)
    pl.when(core == 0)(lambda: spread(left, right))
    pl.when(core != 0)(lambda: spread(right, left))
    for copy in sent:
        copy.wait()


def mlp(scal, att_own, att_oth, tok, cot, wo, bo, gain, shift, up, ub, down, db):
    rows, width = tok.shape
    half = width // 2
    hidden = up.shape[1]
    assert hidden == TILES * width
    here = pl.BlockSpec(memory_space=pltpu.VMEM)
    far = pl.BlockSpec(memory_space=pltpu.HBM)
    return pl.pallas_call(
        mlp_kernel,
        in_specs=[pl.BlockSpec(memory_space=pltpu.SMEM)]
        + [here] * 2
        + [far] * 3
        + [here] * 3
        + [far, here, far, here],
        out_specs=[far, far, here, here, far, far, far, far, here, here, here],
        scratch_shapes=[
            pltpu.VMEM((rows, width), bf16),
            pltpu.VMEM((rows, width), bf16),
            pltpu.VMEM((width, width), bf16),
            pltpu.VMEM((TILES, width, width), bf16),
            pltpu.VMEM((TILES, width, width), bf16),
            pltpu.VMEM((1, hidden), f32),
            pltpu.VMEM((rows, width), bf16),
            pltpu.VMEM((width, rows), bf16),
            pltpu.VMEM((rows, width), f32),
            pltpu.VMEM((rows, width), bf16),
            pltpu.VMEM((rows, width), f32),
            pltpu.VMEM((TILES, 4, half // 2, width), bf16),
            pltpu.VMEM((TILES, 16, 2, width // 16, half), bf16),
            pltpu.SemaphoreType.DMA((3 + 2 * TILES,)),
            pltpu.SemaphoreType.DMA((2,)),
            pltpu.SemaphoreType.DMA((TILES, 4, 2)),
            pltpu.SemaphoreType.DMA((TILES,)),
        ],
        out_shape=[
            sds((rows, width), bf16),
            sds((rows, width), f32),
            sds((rows, half), bf16),
            sds((rows, half), bf16),
            sds((16, half // 2, half), bf16),
            sds((16, half // 2, half), bf16),
            sds((16, TILES, width // 16, half), bf16),
            sds((16, TILES, width // 16, half), bf16),
            sds((16, width // 16, half), bf16),
            sds((16, width // 16, half), bf16),
            sds((16, half), f32),
        ],
        cost_estimate=cost(28),
        compiler_params=pltpu.CompilerParams(vmem_limit_bytes=MLP_MB << 20),
    )(scal, att_own, att_oth, tok, cot, wo, bo, gain, shift, up, ub, down, db)


def pair_back(scal, q_ref, k_ref, v_ref, o1, o2, p_ref, do1, do2, n_ref, x, scratch):
    vb, kt, db, ob, dk_acc, dv_acc = scratch
    core = scal[CORE]
    rows = q_ref.shape[1]
    total = 2 * rows
    width = n_ref.shape[2]
    for hf in range(2):
        rel = core ^ hf
        cut = slice(hf * rows, (hf + 1) * rows)
        vb[cut, :] = v_ref[rel]
        kt[:, cut] = k_ref[rel].T
    db[0] = do1[...]
    db[1] = do2[...]
    ob[0] = o1[...]
    ob[1] = o2[...]
    dk_acc[...] = jnp.zeros_like(dk_acc)
    dv_acc[...] = jnp.zeros_like(dv_acc)
    items = [(qb, h) for qb in reversed(range(total // QB)) for h in range(2)]

    def place(qb):
        return core ^ (qb * QB // rows), pl.ds(qb * QB % rows, QB)

    def grad_probs(qb, h):
        rel, at = place(qb)
        return dot_nt(vb[0 : (qb + 1) * QB, :], head_part(db[rel, at, :], h))

    ahead = grad_probs(*items[0])
    parts = []
    for n, (qb, h) in enumerate(items):
        dp = ahead
        if n + 1 < len(items):
            ahead = grad_probs(*items[n + 1])
        rel, at = place(qb)
        base, keys = key_rows(qb)
        cut = slice(h * HEAD, (h + 1) * HEAD)
        if h == 0:
            query_t = q_ref[rel, at, :].T
            grad_t = db[rel, at, :].T
            both = grad_t.astype(f32) * ob[rel, at, :].T.astype(f32)
        delta = jnp.sum(both[cut], axis=0, keepdims=True)
        p = p_ref[0, h, base : base + keys, :]
        ds = (p.astype(f32) * (dp - delta)).astype(bf16)
        dv_acc[cut, 0:keys] += dot_nt(grad_t[cut], p)
        dk_acc[cut, 0:keys] += dot_nt(query_t[cut], ds)
        parts.append(dot(kt[cut, 0:keys], ds))
        if h == 1:
            x[rel, at, 0:PAIR] = (jnp.concatenate(parts, axis=0).T * (HEAD**-0.5)).astype(bf16)
            parts = []
    for hf in range(2):
        rel = core ^ hf
        cut = slice(hf * rows, (hf + 1) * rows)
        x[rel, :, PAIR : 2 * PAIR] = dk_acc[:, cut].T.astype(bf16)
        x[rel, :, 2 * PAIR :] = dv_acc[:, cut].T.astype(bf16)
    grads = x[...].reshape(total, 3 * PAIR)
    dw = dot_tn(n_ref[...].reshape(total, width), grads).astype(bf16).reshape(16, width // 16, 3 * PAIR)
    return dw, jnp.sum(grads.astype(f32), axis=0, keepdims=True)


def first_pair_kernel(scal, *refs):
    inputs, (t_ref, x, sums_ref), scratch = refs[:9], refs[9:12], refs[12:]
    dw, sums = pair_back(scal, *inputs, x, scratch)
    sums_ref[0:1, :] = sums
    for d in range(16):
        t_ref[scal[PLACE + d]] = dw[d]


def second_pair_kernel(scal, *refs):
    inputs, (t_in, ow_keep, ow_recv), (t_ref, x, sums_ref), scratch = refs[:9], refs[9:12], refs[12:15], refs[15:]
    t_ref[:, 0] = t_in[...]
    t_ref[:, 2] = (ow_keep[...].astype(f32) + ow_recv[...].astype(f32)).astype(bf16)
    dw, sums = pair_back(scal, *inputs, x, scratch)
    sums_ref[0:1, :] = sums
    for d in range(16):
        t_ref[scal[PLACE + d], 1] = dw[d]


def last_pair_kernel(scal, *refs):
    inputs, (x0, x1, sums0, sums1, vec_in, own, oth, wq, wk, wv) = refs[:9], refs[9:19]
    (t_ref, gn_ref, gs_ref, dv_own), (x, xs, ws, *scratch) = refs[19:23], refs[23:]
    core = scal[CORE]
    dw, sums = pair_back(scal, *inputs, x, scratch)
    for d in range(16):
        t_ref[scal[PLACE + d]] = dw[d]
    rows = own.shape[0]
    half = own.shape[1] // 2
    for p, piece in enumerate((x0, x1, x)):
        left = p * 3 * PAIR
        xs[:, left : left + 3 * PAIR] = piece[...].reshape(2 * rows, 3 * PAIR)
        dv_own[:, p * PAIR : (p + 1) * PAIR] = piece[0, :, 2 * PAIR :]
        gs_ref[:, 2 * half + p * PAIR : 2 * half + (p + 1) * PAIR] = piece[1, :, 2 * PAIR :]
        for k, weight in enumerate((wq, wk, wv)):
            ws[:, left + k * PAIR : left + (k + 1) * PAIR] = weight[:, p * PAIR : (p + 1) * PAIR]

    g = dot_nt(xs[...], ws[...])
    gn_ref[...] = g[:rows]
    gs_ref[:, : 2 * half] = g[rows:].astype(bf16)
    gains, shifts = 0.0, 0.0
    for rel, tok in ((0, own), (1, oth)):
        xhat, _ = normalise(tok[...].astype(f32))
        part = g[rel * rows : (rel + 1) * rows]
        gains += jnp.sum(part * xhat, axis=0, keepdims=True)
        shifts += jnp.sum(part, axis=0, keepdims=True)
    every = [sums0[0:1, :], sums1[0:1, :], sums]
    query_bias = jnp.concatenate([s[:, :PAIR] for s in every], axis=1)
    value_bias = jnp.concatenate([s[:, 2 * PAIR :] for s in every], axis=1)
    none = jnp.zeros_like(query_bias)
    vec = [vec_in[...], gains[:, :half], gains[:, half:], shifts[:, :half], shifts[:, half:]]
    vec += [jnp.where(core == 0, query_bias, none), jnp.where(core == 0, none, query_bias)]
    vec += [jnp.where(core == 0, value_bias, none), none]
    t_ref[16] = split_high_low(jnp.concatenate(vec, axis=0))


def pair_call(scal, pair, head_args, more):
    rows, width = head_args[8].shape[1:]
    half = width // 2
    chunk = width // 16
    head = pl.BlockSpec((2, rows, PAIR), lambda p, sc: (0, 0, pair))
    rel = pl.BlockSpec((rows, PAIR), lambda p, sc: (0, pair))
    in_specs = [head] * 3 + [
        rel,
        rel,
        pl.BlockSpec((1, 2, key_rows(2 * rows // QB)[0], QB), lambda p, sc: (pair, 0, 0, 0)),
        rel,
        rel,
        whole((2, rows, width)),
    ]
    scratch = [
        pltpu.VMEM((2 * rows, PAIR), bf16),
        pltpu.VMEM((PAIR, 2 * rows), bf16),
        pltpu.VMEM((2, rows, PAIR), bf16),
        pltpu.VMEM((2, rows, PAIR), bf16),
        pltpu.VMEM((PAIR, 2 * rows), f32),
        pltpu.VMEM((PAIR, 2 * rows), f32),
    ]
    grads = sds((2, rows, 3 * PAIR), bf16)
    more_specs = [whole(x.shape) for x in more]
    if pair == 2:
        column = pl.BlockSpec((width, half), lambda p, sc: (0, sc[CORE]))
        more_specs[-3:] = [column, column, whole((width, half))]
        scratch = [
            pltpu.VMEM(grads.shape, bf16),
            pltpu.VMEM((2 * rows, 9 * PAIR), bf16),
            pltpu.VMEM((width, 9 * PAIR), bf16),
        ] + scratch
        out_shape = [
            sds((17, chunk, half), bf16), sds((rows, width), f32), sds((rows, width + half), bf16),
            sds((rows, half), bf16),
        ]
    else:
        out_shape = [sds((16, 3, chunk, half) if pair else (16, chunk, half), bf16), grads, sds((8, half), f32)]
    return pl.pallas_call(
        (first_pair_kernel, second_pair_kernel, last_pair_kernel)[pair],
        grid_spec=pltpu.PrefetchScalarGridSpec(
            num_scalar_prefetch=1,
            grid=(1,),
            in_specs=in_specs + more_specs,
            out_specs=[whole(x.shape) for x in out_shape],
            scratch_shapes=scratch,
        ),
        out_shape=out_shape,
        cost_estimate=cost(12 if pair == 2 else 8),
        compiler_params=params(44, 1),
    )(scal, *head_args, *more)


def split_high_low(vec):
    high = vec.astype(bf16)
    return jnp.concatenate([high, (vec - high.astype(f32)).astype(bf16)], axis=0)


def join_high_low(block):
    return block[:V_ROWS].astype(f32) + block[V_ROWS:].astype(f32)


def first_norm_back_kernel(scal, tok, gain, gn_own, arrived, grad_middle, dv_own, out_ref, skip_ref):
    width = tok.shape[1]
    gn_oth = arrived[:, :width]
    skip_ref[...] = jnp.where(scal[CORE] == 0, arrived[:, width:], dv_own[...])
    xhat, scale = normalise(tok[...].astype(f32))
    weighted = (gn_own[...] + gn_oth.astype(f32)) * row_of(gain)
    dv = scale * (
        weighted
        - jnp.mean(weighted, axis=-1, keepdims=True)
        - xhat * jnp.mean(weighted * xhat, axis=-1, keepdims=True)
    )
    out_ref[...] = (grad_middle[...] + dv).astype(bf16)


def first_norm_back(scal, tok, gain, gn_own, arrived, grad_middle, dv_own):
    rows, width = tok.shape
    tile = rows // 2
    block = pl.BlockSpec((tile, width), lambda s, sc: (s, 0))
    narrow = pl.BlockSpec((tile, width // 2), lambda s, sc: (s, 0))
    both = pl.BlockSpec((tile, width + width // 2), lambda s, sc: (s, 0))
    return pl.pallas_call(
        first_norm_back_kernel,
        grid_spec=pltpu.PrefetchScalarGridSpec(
            num_scalar_prefetch=1,
            grid=(2,),
            in_specs=[block, whole((width,)), block, both, block, narrow],
            out_specs=[block, narrow],
        ),
        out_shape=[sds((rows, width), bf16), sds((rows, width // 2), bf16)],
        cost_estimate=cost(4),
        compiler_params=params(32, 1),
    )(scal, tok, gain, gn_own, arrived, grad_middle, dv_own)


def flip(values, bits, dp_count):
    pairs = [((d * 2 + c), ((d ^ bits[c]) * 2 + c)) for d in range(dp_count) for c in range(2)]
    return lax.ppermute(values, ("dp", "seq"), pairs)


def swap(values):
    return lax.ppermute(values, "seq", [(0, 1), (1, 0)])


BEFORE_LAST = ('early', 'down')
AFTER_LAST = ('last', 'down', 'early', 'up', 'last', 'down', 'early', 'norm', 'last', 'up', 'early', 'last', 'up')
STAGES = ((1, 2), (2, 1), (4, 4), (8, 8))
STAGES_Z = ((4, 4), (1, 2), (2, 1), (8, 8))


def after(value, *others):
    return lax.optimization_barrier((value,) + others)[0]


class Halving:
    def __init__(self, parts, stages=STAGES):
        self.parts = list(parts)
        self.size = parts[0].shape[0]
        self.stages = list(stages)
        self.begun = False

    def total(self, low, high):
        out = self.parts[0][low:high]
        for part in self.parts[1:]:
            out = out + part[low:high]
        return out

    def upper(self):
        if self.begun:
            self.parts = [lax.optimization_barrier(self.total(0, self.size))]
        self.begun = True
        self.size //= 2
        return self.total(self.size, 2 * self.size)

    def result(self):
        return self.total(0, self.size)


def add_with_vec_kernel(mine, theirs, out):
    count = out.shape[0] - 1
    out[:count] = mine[:count] + theirs[:count]
    out[count] = split_high_low(join_high_low(mine[2 * count]) + join_high_low(theirs[count]))


class HalvingWithVec(Halving):
    def add(self):
        if len(self.parts) > 1:
            mine, theirs = self.parts
            self.parts = [
                pl.pallas_call(
                    add_with_vec_kernel,
                    out_shape=sds(theirs.shape, bf16),
                    compiler_params=pltpu.CompilerParams(vmem_limit_bytes=16 << 20),
                )(mine, theirs)
            ]

    def upper(self):
        self.add()
        return self.parts[0][(self.parts[0].shape[0] - 1) // 2 :]

    def result(self):
        self.add()
        return self.parts[0]


def arrived(chain, token):
    *chain.parts, token = lax.optimization_barrier((*chain.parts, token))
    return token


def send(token, *chains):
    for chain in chains:
        token = arrived(chain, token)
    bits = [chain.stages.pop(0) for chain in chains]
    assert all(b == bits[0] for b in bits)
    uppers = [chain.upper() for chain in chains]
    if len(chains) == 1:
        chains[0].parts.append(flip(uppers[0], bits[0], 16))
        return uppers[0]
    flat = [x.reshape(-1, x.shape[-1]) for x in uppers]
    token = jnp.concatenate(flat, axis=0)
    came = flip(token, bits[0], 16)
    at = 0
    for chain, x, rows in zip(chains, uppers, flat):
        chain.parts.append(came[at : at + rows.shape[0]].reshape(x.shape))
        at += rows.shape[0]
    return token


def both_sides(core, own, oth, put):
    @pl.when(core == 0)
    def _():
        put(0, own)
        put(1, oth)

    @pl.when(core != 0)
    def _():
        put(1, own)
        put(0, oth)


def finish_first_kernel(scal, down, early, down2, early2, gd, go):
    half = down.shape[1]

    def put(side, shares):
        down, early = shares
        gd[:, side * half : (side + 1) * half] = down[...].astype(f32)
        go[:, side * half : (side + 1) * half] = early[2].astype(f32)

    both_sides(scal[CORE], (down, early), (down2, early2), put)


def finish_last_kernel(scal, up, early, late, up2, early2, late2, gu, gq, gk, gv, *vectors):
    half = early.shape[2]

    def put(side, shares):
        up, early, late = shares
        for g in range(up.shape[0]):
            at = (side * up.shape[0] + g) * half
            gu[:, at : at + half] = up[g].astype(f32)
        at = side * half
        for p, piece in enumerate((early[0], early[1], late[0])):
            cols = slice(at + p * PAIR, at + (p + 1) * PAIR)
            gq[:, cols] = piece[:, :PAIR].astype(f32)
            gk[:, cols] = piece[:, PAIR : 2 * PAIR].astype(f32)
            if side == 0:
                gv[:, p * PAIR : (p + 1) * PAIR] = piece[:, 2 * PAIR :].astype(f32)

    both_sides(scal[CORE], (up, early, late), (up2, early2, late2), put)
    vec = join_high_low(late[1]) + join_high_low(late2[1])
    for ref, row in zip(vectors, (V_GAIN1, V_SHIFT1, V_QUERY, V_VALUE, V_OUT, V_GAIN2, V_SHIFT2, V_UP, V_DOWN)):
        for k in range(ref.shape[0] // half):
            ref[k * half : (k + 1) * half] = vec[row + k]


def finish(kernel, scal, shares, out_shape):
    out_shape = [sds(shape, f32) for shape in out_shape]
    return pl.pallas_call(
        kernel,
        grid_spec=pltpu.PrefetchScalarGridSpec(
            num_scalar_prefetch=1,
            grid=(1,),
            in_specs=[whole(x.shape) for x in shares],
            out_specs=[whole(s.shape) for s in out_shape],
        ),
        out_shape=out_shape,
        cost_estimate=cost(3),
        compiler_params=params(24, 1),
    )(scal, *shares)


def finish_any(core, down, up, early, late):
    half = down.shape[2]
    vec = lax.psum(join_high_low(late[16]), ("dp", "seq"))

    def columns(pieces):
        mine = jnp.concatenate([x.reshape(-1, x.shape[-1]).astype(f32) for x in pieces], axis=1)
        share = lax.psum_scatter(mine, "dp", scatter_dimension=0, tiled=True)
        other = swap(share)
        return jnp.where(core == 0, jnp.concatenate([share, other], 1), jnp.concatenate([other, share], 1))

    thirds = [early[:, 0], early[:, 1], late[:16]]
    gq, gk, gv = (columns([x[..., i * PAIR : (i + 1) * PAIR] for x in thirds]) for i in range(3))
    go = columns([early[:, 2]])
    gu = columns([up[:, g] for g in range(up.shape[1])])
    gd = columns([down])
    flat = lambda row, n: vec[row : row + n].reshape(-1)
    vectors = [flat(V_GAIN1, 2), flat(V_SHIFT1, 2), flat(V_QUERY, 2), flat(V_VALUE, 1), flat(V_OUT, 2)]
    vectors += [flat(V_GAIN2, 2), flat(V_SHIFT2, 2), flat(V_UP, 8), flat(V_DOWN, 2)]
    return [gq, gk, gv[:, :half], go, gu, gd] + vectors


def per_device(
    dp_count,
    tokens,
    skip_values,
    doc_lengths,
    gain_first,
    shift_first,
    query_weight,
    query_bias,
    key_weight,
    value_weight,
    value_bias,
    out_weight,
    out_bias,
    gain_second,
    shift_second,
    up_weight,
    up_bias,
    down_weight,
    down_bias,
    cotangent,
):
    rows, width = tokens.shape
    hidden = up_weight.shape[1]
    core = lax.axis_index("seq")
    chunks = jnp.arange(16, dtype=jnp.int32)
    if dp_count == 16:
        off = chunks ^ lax.axis_index("dp")
        x_bit, y_bit, z_bits = off & 1, (off >> 1) & 1, ((off >> 2) & 1) * 2 + ((off >> 3) & 1)
        x_first, y_first = x_bit * 8 + y_bit * 4 + z_bits, y_bit * 8 + x_bit * 4 + z_bits
        place, place_oth = jnp.where(core == 0, x_first, y_first), jnp.where(core == 0, y_first, x_first)
        z_first = lambda xy: (xy & 12) // 2 + (xy & 2) * 4 + (xy & 1)
        places = [place, place_oth, z_first(place), z_first(place_oth)]
    else:
        places = [chunks] * 4
    scal = jnp.concatenate([core[None], doc_lengths[0, :5]] + places).astype(jnp.int32)

    value_weight = jnp.where(core == 0, value_weight, jnp.zeros_like(value_weight))
    tokens_oth = swap(tokens)
    skip_oth = swap(skip_values)
    q, k, v, normed, att_own, att_send, probs = front(
        scal, tokens.astype(f32), tokens_oth, jnp.where(core == 0, jnp.zeros_like(skip_values), skip_values), skip_oth,
        jnp.concatenate([gain_first, shift_first, query_bias, value_bias]).astype(f32),
        query_weight, key_weight, value_weight,
    )
    att_oth = swap(att_send)
    (output, grad_middle, ga_keep, ga_send, dn_keep, dn_send, up_keep, up_send, ow_keep, ow_send, vec) = mlp(
        scal, att_own, att_oth, tokens, cotangent, out_weight, out_bias, gain_second, shift_second,
        up_weight, up_bias, down_weight, down_bias,
    )
    whole_tiles = dp_count == 16
    ga_oth = swap(ga_send)
    dn_send, up_send, ow_send, _ = lax.optimization_barrier((dn_send, up_send, ow_send, ga_oth))
    dn_recv, up_recv, ow_recv = swap(dn_send), swap(up_send), swap(ow_send)
    down = Halving((dn_keep, dn_recv))
    up = Halving((up_keep, up_recv), STAGES_Z)
    head_args = [q, k, v, att_own, att_send, probs, ga_keep, ga_oth, normed]
    t0, x0, sums0 = pair_call(scal, 0, head_args, ())
    token = sums0
    if whole_tiles:
        token = send(token, down)
        token = send(token, up)
    t01, x1, sums1 = pair_call(scal, 1, head_args, (after(t0, token), ow_keep, ow_recv))
    token = sums1
    early = Halving((t01,))
    if whole_tiles:
        for chains in BEFORE_LAST:
            token = send(token, *(dict(early=early, down=down, up=up)[c] for c in chains.split()))
    late, gn_own, gn_send, dv_own = pair_call(
        scal, 2, head_args,
        (after(x0, token), x1, sums0, sums1, vec, tokens, tokens_oth, query_weight, key_weight, value_weight),
    )
    gn_oth = swap(gn_send)
    if whole_tiles:
        last = HalvingWithVec((late,))
        token = gn_send
        every = dict(early=early, down=down, up=up, last=last)
        for chains in AFTER_LAST:
            if chains == "gn!":
                gn_oth, token = lax.optimization_barrier((gn_oth, token))
                continue
            if chains.endswith("!"):
                chain = every[chains[:-1]]
                arrived(chain, token)
                token = chain.result()
                chain.parts = [token]
                continue
            if chains != "norm":
                token = send(token, *(every[c] for c in chains.split()))
                continue
            gn_held, token = lax.optimization_barrier((gn_oth, token))
            grad_tokens, grad_skip = first_norm_back(scal, tokens, gain_first, gn_own, gn_held, grad_middle, dv_own)
            token = grad_tokens
        high, wide = width // dp_count, (width // dp_count, width)
        token = arrived(down, token)
        arrived(early, token)
        down, early = down.result()[0], early.result()[0]
        down2, early2 = swap(down), swap(early)
        gd, go = finish(finish_first_kernel, scal, (down, early, down2, early2), [(hidden // dp_count, width), wide])
        arrived(up, gd)
        arrived(last, gd)
        up, last = up.result()[0], last.result()
        shares = (up, early, last, swap(up), early2, swap(last))
        vectors = [(n,) for n in (width, width, width, width // 2, width, width, width, hidden, width)]
        rest = finish(finish_last_kernel, scal, shares, [(high, hidden), wide, wide, (high, width // 2)] + vectors)
        gu, gq, gk, gv, gain1, shift1, gqb, gvb, gob, gain2, shift2, gub, gdb = rest
    else:
        grad_tokens, grad_skip = first_norm_back(scal, tokens, gain_first, gn_own, gn_oth, grad_middle, dv_own)
        rest = finish_any(core, down.result(), up.result(), early.result(), late)
        gq, gk, gv, go, gu, gd, gain1, shift1, gqb, gvb, gob, gain2, shift2, gub, gdb = rest
    return (
        output, grad_tokens, grad_skip, gain1, shift1, gq, gqb, gk, gv, gvb, go, gob, gain2, shift2, gu, gub, gd, gdb,
    )


def solution(mesh):
    rows, full, shares = P(("dp", "seq"), None), P(), P("dp", None)
    return jax.shard_map(
        functools.partial(per_device, mesh.shape["dp"]),
        mesh=mesh,
        in_specs=(rows, rows, shares) + (full,) * 15 + (rows,),
        out_specs=(
            rows, rows, rows, full, full, shares, full, shares, shares, full, shares, full, full, full, shares, full,
            shares, full,
        ),
        check_vma=False,
    )
```

```python
import functools

import jax
import jax.numpy as jnp
from jax import lax
from jax.experimental import pallas as pl
from jax.experimental.pallas import tpu as pltpu
from jax.sharding import PartitionSpec as P

HEAD = 64
FRESH = 6
PAIR = 2 * HEAD
QB = 256
FRONT_MB = 46
MLP_MB = 52
LOG2E = 1.4426950408889634
GELU_C = 0.7978845608028654
GELU_A = 0.044715
f32 = jnp.float32
bf16 = jnp.bfloat16
NT = (((1,), (1,)), ((), ()))
TN = (((0,), (0,)), ((), ()))
CORE, PLACE_T = 0, 1
PLACE_D, PLACE_D_OTH, PLACE_U, PLACE_U_OTH, PLACE_E, PLACE_E_OTH = 17, 33, 49, 65, 81, 97
V_UP, V_DOWN, V_OUT, V_GAIN2, V_SHIFT2, V_GAIN1, V_SHIFT1, V_QUERY, V_VALUE = 0, 8, 10, 12, 14, 16, 18, 20, 22
V_ROWS = 24


def dot(left, right):
    return jnp.dot(left, right, preferred_element_type=f32)


def dot_nt(left, right):
    return lax.dot_general(left, right, NT, preferred_element_type=f32)


def dot_tn(left, right):
    return lax.dot_general(left, right, TN, preferred_element_type=f32)


def row_of(ref):
    return ref[...].astype(f32).reshape(1, -1)


def normalise(values):
    centre = values - jnp.mean(values, axis=-1, keepdims=True)
    spread = jnp.mean(centre * centre, axis=-1, keepdims=True)
    scale = lax.rsqrt(spread + 1e-05)
    return centre * scale, scale


def params(limit_mb, axes):
    return pltpu.CompilerParams(vmem_limit_bytes=limit_mb << 20, dimension_semantics=("arbitrary",) * axes)


def whole(shape):
    return pl.BlockSpec(shape, lambda *_: (0,) * len(shape))


def cost(micros):
    return pl.CostEstimate(flops=int(micros), bytes_accessed=0, transcendentals=0)


def sds(shape, dtype):
    return jax.ShapeDtypeStruct(shape, dtype)


def first_allowed(lengths, total):
    place = lax.broadcasted_iota(jnp.int32, (1, total), 1)
    start = jnp.zeros((1, total), jnp.int32)
    bound = jnp.int32(0)
    for k in range(4):
        bound = bound + lengths[0, k]
        start = jnp.where(place >= bound, bound, start)
    return jnp.where(place >= bound + lengths[0, 4], place, start)


def allowed_block(start, low, high, first_query):
    key = lax.broadcasted_iota(jnp.int32, (high - low, QB), 0) + low
    ok = key >= start
    if high > first_query:
        ok = ok & (key <= lax.broadcasted_iota(jnp.int32, (high - low, QB), 1) + first_query)
    return ok


def head_part(values, h):
    lane = lax.broadcasted_iota(jnp.int32, values.shape, 1)
    return jnp.where((lane < HEAD) if h == 0 else (lane >= HEAD), values, jnp.zeros_like(values))


def key_rows(qb):
    return QB * (qb * (qb + 1) // 2), QB * (qb + 1)


def attend_pair(scal, lengths, pair, q_ref, k_ref, v_ref, o_own, o_oth, probs, kb, vt, ob):
    core = scal[CORE]
    rows = q_ref.shape[1]
    total = 2 * rows
    lanes = slice(pair * PAIR, (pair + 1) * PAIR)
    for half in range(2):
        rel = core ^ half
        kb[half * rows : (half + 1) * rows, :] = k_ref[rel, :, lanes]
        vt[:, half * rows : (half + 1) * rows] = v_ref[rel, :, lanes].T
    start = first_allowed(lengths, total)
    items = [(qb, h) for qb in range(total // QB) for h in range(2)]

    def place(qb):
        return core ^ (qb * QB // rows), pl.ds(qb * QB % rows, QB)

    def scores(qb, h):
        low = qb * QB
        rel, at = place(qb)
        qh = head_part(q_ref[rel, at, lanes], h)
        return [(a, b, dot_nt(kb[a:b, :], qh)) for a, b in ([(0, low)] if low else []) + [(low, low + QB)]]

    done = {}
    ahead = scores(*items[0])
    for n, (qb, h) in enumerate(items):
        current = ahead
        if n + 1 < len(items):
            ahead = scores(*items[n + 1])
        low = qb * QB
        base, _ = key_rows(qb)
        begin = start[:, low : low + QB]
        peak = None
        masked = []
        for a, b, s in current:
            s = jnp.where(allowed_block(begin, a, b, low), s, -1e30)
            top = jnp.max(s, axis=0, keepdims=True)
            peak = top if peak is None else jnp.maximum(peak, top)
            masked.append((a, b, s))
        peak2 = peak * LOG2E
        raised = [(a, b, jnp.exp2(s * LOG2E - peak2)) for a, b, s in masked]
        summed = None
        for a, b, e in raised:
            part = jnp.sum(e, axis=0, keepdims=True)
            summed = part if summed is None else summed + part
        inverse = 1.0 / summed
        acc = None
        for a, b, e in raised:
            p = (e * inverse).astype(bf16)
            probs[h, base + a : base + b, :] = p
            part = dot(vt[h * HEAD : (h + 1) * HEAD, a:b], p)
            acc = part if acc is None else acc + part
        done[h] = acc
        if h == 1:
            rel, at = place(qb)
            ob[rel, at, :] = jnp.concatenate([done[0], done[1]], axis=0).T.astype(bf16)
    o_own[:, lanes] = ob[0]
    o_oth[:, lanes] = ob[1]


def front_kernel(
    scal, lengths, tok, oth, skip, skip_oth, vectors, wq, wk, wv,
    q_ref, k_ref, v_ref, n_ref, o_own, o_oth, p_ref,
    tok_s, skip_s, wq_s, wk_s, wv_s, probs, kb, vt, ob, sems, psems,
):
    core = scal[CORE]
    half = q_ref.shape[2]
    cols = pl.ds(pl.multiple_of(core * half, half), half)
    pieces = (
        (wq.at[:, cols], wq_s), (wk.at[:, cols], wk_s), (tok, tok_s), (wv, wv_s), (skip, skip_s),
    )
    fetch = [pltpu.make_async_copy(src, dst, sems.at[n]) for n, (src, dst) in enumerate(pieces)]
    for copy in fetch:
        copy.start()
    joined = row_of(vectors)
    width = 2 * half
    gain, shift, bq, bv = (joined[:, at : at + n] for at, n in ((0, width), (width, width), (2 * width, width), (3 * width, half)))
    bias = jnp.where(core == 0, bq[:, :half], bq[:, half:])
    for rel in (1, 0):
        if rel == 0:
            fetch[2].wait()
        xhat, _ = normalise((oth if rel else tok_s)[...].astype(f32))
        normed = (xhat * gain + shift).astype(bf16)
        n_ref[rel] = normed
        if rel:
            fetch[0].wait()
        q_ref[rel] = (dot(normed, wq_s[...]) + bias).astype(bf16) * jnp.asarray(HEAD**-0.5, bf16)
        if rel:
            fetch[1].wait()
        k_ref[rel] = dot(normed, wk_s[...]).astype(bf16)
    fetch[3].wait()
    fetch[4].wait()

    @pl.when(core == 0)
    def _():
        for rel in range(2):
            v_ref[rel] = (dot(n_ref[rel], wv_s[...]) + bv).astype(bf16)

    @pl.when(core != 0)
    def _():
        v_ref[0] = skip_s[...]
        v_ref[1] = skip_oth[...]

    out = []
    for pair in range(half // PAIR):
        slot = pair % 2
        if pair >= 2:
            out[pair - 2].wait()
        attend_pair(scal, lengths, pair, q_ref, k_ref, v_ref, o_own, o_oth, probs.at[slot], kb, vt, ob)
        out.append(pltpu.make_async_copy(probs.at[slot], p_ref.at[pair], psems.at[pair]))
        out[pair].start()
    for copy in out[-2:]:
        copy.wait()


def front(scal, lengths, tok, oth, skip, skip_oth, vectors, wq, wk, wv):
    rows, width = tok.shape
    half = width // 2
    pairs = half // PAIR
    packed = key_rows(2 * rows // QB)[0]
    here = pl.BlockSpec(memory_space=pltpu.VMEM)
    far = pl.BlockSpec(memory_space=pltpu.HBM)
    return pl.pallas_call(
        front_kernel,
        in_specs=[pl.BlockSpec(memory_space=pltpu.SMEM)] * 2 + [far, here, far, here, here, far, far, far],
        out_specs=[here] * 6 + [far],
        scratch_shapes=[
            pltpu.VMEM((rows, width), f32),
            pltpu.VMEM((rows, half), bf16),
            pltpu.VMEM((width, half), bf16),
            pltpu.VMEM((width, half), bf16),
            pltpu.VMEM((width, half), bf16),
            pltpu.VMEM((2, 2, packed, QB), bf16),
            pltpu.VMEM((2 * rows, PAIR), bf16),
            pltpu.VMEM((PAIR, 2 * rows), bf16),
            pltpu.VMEM((2, rows, PAIR), bf16),
            pltpu.SemaphoreType.DMA((5,)),
            pltpu.SemaphoreType.DMA((pairs,)),
        ],
        out_shape=[sds((2, rows, half), bf16)] * 3
        + [sds((2, rows, width), bf16)]
        + [sds((rows, half), bf16)] * 2
        + [sds((pairs, 2, packed, QB), bf16)],
        cost_estimate=cost(14),
        compiler_params=pltpu.CompilerParams(vmem_limit_bytes=FRONT_MB << 20),
    )(scal, lengths, tok, oth, skip, skip_oth, vectors, wq, wk, wv)


TILES = 4


def mlp_kernel(
    scal, att_own, att_oth, tok_far, cot_far, wo_far, bo, gain, shift, up_far, ub, down_far, db,
    out_far, gm_far, ga_keep, ga_send, dn_keep, dn_send, up_keep, up_send, ow_keep, ow_send, vec_ref,
    tok, cot, wo, up, down, ubias, normed, normed_t, xhat_ref, out_s, gm_s, dn_s, up_s, sems, out_sems, dn_sems, up_sems,
):
    core = scal[CORE]
    width = tok.shape[1]
    half = width // 2
    chunk = width // 16
    fchunk = half // 2
    parts = width // fchunk
    tiles = [(s + (TILES // 2) * (1 - core)) & (TILES - 1) for s in range(TILES)]
    span = [pl.ds(pl.multiple_of(t * width, width), width) for t in tiles]

    def fetch(src, dst, n):
        copy = pltpu.make_async_copy(src, dst, sems.at[n])
        copy.start()
        return copy

    wo_in, tok_in = fetch(wo_far, wo, 0), fetch(tok_far, tok, 1)
    up_in, down_in = [fetch(up_far.at[:, span[0]], up.at[0], 3)], []
    cot_in = fetch(cot_far, cot, 2)
    for s in range(TILES):
        if s:
            up_in.append(fetch(up_far.at[:, span[s]], up.at[s], 3 + 2 * s))
        down_in.append(fetch(down_far.at[span[s], :], down.at[s], 4 + 2 * s))

    def att_weight(which):
        return wo[pl.ds(pl.multiple_of(which * half, half), half), :]

    ubias[...] = row_of(ub)
    wo_in.wait()
    tok_in.wait()
    branch = dot(att_own[...], att_weight(core)) + dot(att_oth[...], att_weight(1 - core)) + row_of(bo)
    middle = tok[...].astype(f32) + branch
    xhat, scale = normalise(middle)
    xhat_ref[...] = xhat
    value = (xhat * row_of(gain) + row_of(shift)).astype(bf16)
    normed[...] = value
    normed_t[...] = value.T
    acc = middle + row_of(db)
    back = None
    sent = []
    up_in[0].wait()
    cot_in.wait()
    down_in[0].wait()
    ahead = dot(normed[...], up[0])
    for s in range(TILES):
        wide = dot_nt(cot[...], down[s])
        v = ahead + ubias[:, span[s]]
        if s + 1 < TILES:
            up_in[s + 1].wait()
            down_in[s + 1].wait()
            ahead = dot(normed[...], up[s + 1])
        sq = v * v
        t = jnp.tanh(v * (GELU_C + (GELU_C * GELU_A) * sq))
        half_t = 0.5 * (1.0 + t)
        act = (v * half_t).astype(bf16)
        slope = half_t + (0.5 * v) * (1.0 - t * t) * (GELU_C + (3.0 * GELU_C * GELU_A) * sq)
        grad = (wide * slope).astype(bf16)
        dn_s[s] = dot_tn(act, cot[...]).astype(bf16).reshape(parts, fchunk, width)
        for n in range(parts):
            for k, (out, side, table) in enumerate(((dn_keep, core, PLACE_D), (dn_send, 1 - core, PLACE_D_OTH))):
                cols = pl.ds(pl.multiple_of(side * half, half), half)
                place = scal[table + tiles[s] * parts + n]
                sent.append(pltpu.make_async_copy(dn_s.at[s, n, :, cols], out.at[place], dn_sems.at[s, n, k]))
                sent[-1].start()
        dup = dot(normed_t[...], grad).astype(bf16).reshape(16, chunk, width)
        keep = s >= TILES // 2
        for d in range(16):
            place = scal[(PLACE_U if keep else PLACE_U_OTH) + d]
            for g in range(2):
                up_s[s, place, g] = dup[d, :, g * half : (g + 1) * half]
        at = pl.ds(2 * (s % (TILES // 2)), 2)
        sent.append(pltpu.make_async_copy(up_s.at[s], (up_keep if keep else up_send).at[:, at], up_sems.at[s]))
        sent[-1].start()
        acc = acc + dot(act, down[s])
        part = dot_nt(grad, up[s])
        back = part if back is None else back + part
        sums = jnp.sum(grad.astype(f32), axis=0, keepdims=True)
        for g in range(2):
            vec_ref[pl.ds(V_UP + 2 * tiles[s] + g, 1), :] = sums[:, g * half : (g + 1) * half]
    out_s[...] = acc.astype(bf16)
    sent.append(pltpu.make_async_copy(out_s, out_far, out_sems.at[0]))
    sent[-1].start()
    xhat = xhat_ref[...]
    grad_out = cot[...].astype(f32)
    weighted = back * row_of(gain)
    dv = scale * (
        weighted
        - jnp.mean(weighted, axis=-1, keepdims=True)
        - xhat * jnp.mean(weighted * xhat, axis=-1, keepdims=True)
    )
    grad_middle = grad_out + dv
    gm_s[...] = grad_middle
    sent.append(pltpu.make_async_copy(gm_s, gm_far, out_sems.at[1]))
    sent[-1].start()
    branch = grad_middle.astype(bf16)

    def put(row, vector):
        vec_ref[row : row + 1, :] = vector[:, :half]
        vec_ref[row + 1 : row + 2, :] = vector[:, half:]

    put(V_DOWN, jnp.sum(grad_out, axis=0, keepdims=True))
    put(V_OUT, jnp.sum(branch.astype(f32), axis=0, keepdims=True))
    put(V_GAIN2, jnp.sum(back * xhat, axis=0, keepdims=True))
    put(V_SHIFT2, jnp.sum(back, axis=0, keepdims=True))
    ga_keep[...] = dot_nt(branch, att_weight(core)).astype(bf16)
    ga_send[...] = dot_nt(branch, att_weight(1 - core)).astype(bf16)
    wide_own = dot_tn(att_own[...], branch).astype(bf16).reshape(8, chunk, width)
    wide_oth = dot_tn(att_oth[...], branch).astype(bf16).reshape(8, chunk, width)

    def spread(keep, send):
        for d in range(8):
            own_place = scal[PLACE_E + core * 8 + d]
            oth_place = scal[PLACE_E + (1 - core) * 8 + d]
            ow_keep[own_place] = wide_own[d, :, keep]
            ow_keep[oth_place] = wide_oth[d, :, keep]
            ow_send[scal[PLACE_E_OTH + core * 8 + d]] = wide_own[d, :, send]
            ow_send[scal[PLACE_E_OTH + (1 - core) * 8 + d]] = wide_oth[d, :, send]

    left, right = slice(0, half), slice(half, width)
    pl.when(core == 0)(lambda: spread(left, right))
    pl.when(core != 0)(lambda: spread(right, left))
    for copy in sent:
        copy.wait()


def mlp(scal, att_own, att_oth, tok, cot, wo, bo, gain, shift, up, ub, down, db):
    rows, width = tok.shape
    half = width // 2
    hidden = up.shape[1]
    assert hidden == TILES * width
    here = pl.BlockSpec(memory_space=pltpu.VMEM)
    far = pl.BlockSpec(memory_space=pltpu.HBM)
    return pl.pallas_call(
        mlp_kernel,
        in_specs=[pl.BlockSpec(memory_space=pltpu.SMEM)]
        + [here] * 2
        + [far] * 3
        + [here] * 3
        + [far, here, far, here],
        out_specs=[far, far, here, here, far, far, far, far, here, here, here],
        scratch_shapes=[
            pltpu.VMEM((rows, width), bf16),
            pltpu.VMEM((rows, width), bf16),
            pltpu.VMEM((width, width), bf16),
            pltpu.VMEM((TILES, width, width), bf16),
            pltpu.VMEM((TILES, width, width), bf16),
            pltpu.VMEM((1, hidden), f32),
            pltpu.VMEM((rows, width), bf16),
            pltpu.VMEM((width, rows), bf16),
            pltpu.VMEM((rows, width), f32),
            pltpu.VMEM((rows, width), bf16),
            pltpu.VMEM((rows, width), f32),
            pltpu.VMEM((TILES, 4, half // 2, width), bf16),
            pltpu.VMEM((TILES, 16, 2, width // 16, half), bf16),
            pltpu.SemaphoreType.DMA((3 + 2 * TILES,)),
            pltpu.SemaphoreType.DMA((2,)),
            pltpu.SemaphoreType.DMA((TILES, 4, 2)),
            pltpu.SemaphoreType.DMA((TILES,)),
        ],
        out_shape=[
            sds((rows, width), bf16),
            sds((rows, width), f32),
            sds((rows, half), bf16),
            sds((rows, half), bf16),
            sds((16, half // 2, half), bf16),
            sds((16, half // 2, half), bf16),
            sds((16, TILES, width // 16, half), bf16),
            sds((16, TILES, width // 16, half), bf16),
            sds((16, width // 16, half), bf16),
            sds((16, width // 16, half), bf16),
            sds((16, half), f32),
        ],
        cost_estimate=cost(28),
        compiler_params=pltpu.CompilerParams(vmem_limit_bytes=MLP_MB << 20),
    )(scal, att_own, att_oth, tok, cot, wo, bo, gain, shift, up, ub, down, db)


def pair_back(scal, q_ref, k_ref, v_ref, o1, o2, p_ref, do1, do2, n_ref, x, scratch):
    vb, kt, db, ob, dk_acc, dv_acc = scratch
    core = scal[CORE]
    rows = q_ref.shape[1]
    total = 2 * rows
    width = n_ref.shape[2]
    for hf in range(2):
        rel = core ^ hf
        cut = slice(hf * rows, (hf + 1) * rows)
        vb[cut, :] = v_ref[rel]
        kt[:, cut] = k_ref[rel].T
    db[0] = do1[...]
    db[1] = do2[...]
    ob[0] = o1[...]
    ob[1] = o2[...]
    dk_acc[...] = jnp.zeros_like(dk_acc)
    dv_acc[...] = jnp.zeros_like(dv_acc)
    items = [(qb, h) for qb in reversed(range(total // QB)) for h in range(2)]

    def place(qb):
        return core ^ (qb * QB // rows), pl.ds(qb * QB % rows, QB)

    def grad_probs(qb, h):
        rel, at = place(qb)
        return dot_nt(vb[0 : (qb + 1) * QB, :], head_part(db[rel, at, :], h))

    ahead = grad_probs(*items[0])
    parts = []
    for n, (qb, h) in enumerate(items):
        dp = ahead
        if n + 1 < len(items):
            ahead = grad_probs(*items[n + 1])
        rel, at = place(qb)
        base, keys = key_rows(qb)
        cut = slice(h * HEAD, (h + 1) * HEAD)
        if h == 0:
            query_t = q_ref[rel, at, :].T
            grad_t = db[rel, at, :].T
            both = grad_t.astype(f32) * ob[rel, at, :].T.astype(f32)
        delta = jnp.sum(both[cut], axis=0, keepdims=True)
        p = p_ref[0, h, base : base + keys, :]
        ds = (p.astype(f32) * (dp - delta)).astype(bf16)
        dv_acc[cut, 0:keys] += dot_nt(grad_t[cut], p)
        dk_acc[cut, 0:keys] += dot_nt(query_t[cut], ds)
        parts.append(dot(kt[cut, 0:keys], ds))
        if h == 1:
            x[rel, at, 0:PAIR] = (jnp.concatenate(parts, axis=0).T * (HEAD**-0.5)).astype(bf16)
            parts = []
    for hf in range(2):
        rel = core ^ hf
        cut = slice(hf * rows, (hf + 1) * rows)
        x[rel, :, PAIR : 2 * PAIR] = dk_acc[:, cut].T.astype(bf16)
        x[rel, :, 2 * PAIR :] = dv_acc[:, cut].T.astype(bf16)
    grads = x[...].reshape(total, 3 * PAIR)
    dw = dot_tn(n_ref[...].reshape(total, width), grads).astype(bf16).reshape(16, width // 16, 3 * PAIR)
    return dw, jnp.sum(grads.astype(f32), axis=0, keepdims=True)


def first_pair_kernel(scal, *refs):
    inputs, (t_ref, x, sums_ref), scratch = refs[:9], refs[9:12], refs[12:]
    dw, sums = pair_back(scal, *inputs, x, scratch)
    sums_ref[0:1, :] = sums
    for d in range(16):
        t_ref[scal[PLACE_E + d]] = dw[d]


def second_pair_kernel(scal, *refs):
    inputs, (t_in, ow_keep, ow_recv), (t_low, t_high, x, sums_ref) = refs[:9], refs[9:12], refs[12:16]
    t_ref, *scratch = refs[16:]
    sides = ((t_low, slice(0, 8)), (t_high, slice(8, 16)))
    for out, at in sides:
        out[:, 0] = t_in[at]
        out[:, 2] = (ow_keep[at].astype(f32) + ow_recv[at].astype(f32)).astype(bf16)
    dw, sums = pair_back(scal, *inputs, x, scratch)
    sums_ref[0:1, :] = sums
    for d in range(16):
        t_ref[scal[PLACE_E + d]] = dw[d]
    for out, at in sides:
        out[:, 1] = t_ref[at]


def last_pair_kernel(scal, *refs):
    inputs, (x0, x1, sums0, sums1, vec_in, own, oth, wq, wk, wv) = refs[:9], refs[9:19]
    (t_ref, gn_ref, gs_ref, dv_own), (x, xs, ws, *scratch) = refs[19:23], refs[23:]
    core = scal[CORE]
    dw, sums = pair_back(scal, *inputs, x, scratch)
    for d in range(16):
        t_ref[scal[PLACE_T + d]] = dw[d]
    rows = own.shape[0]
    half = own.shape[1] // 2
    for p, piece in enumerate((x0, x1, x)):
        left = p * 3 * PAIR
        xs[:, left : left + 3 * PAIR] = piece[...].reshape(2 * rows, 3 * PAIR)
        dv_own[:, p * PAIR : (p + 1) * PAIR] = piece[0, :, 2 * PAIR :]
        gs_ref[:, 2 * half + p * PAIR : 2 * half + (p + 1) * PAIR] = piece[1, :, 2 * PAIR :]
        for k, weight in enumerate((wq, wk, wv)):
            ws[:, left + k * PAIR : left + (k + 1) * PAIR] = weight[:, p * PAIR : (p + 1) * PAIR]

    g = dot_nt(xs[...], ws[...])
    gn_ref[...] = g[:rows]
    gs_ref[:, : 2 * half] = g[rows:].astype(bf16)
    gains, shifts = 0.0, 0.0
    for rel, tok in ((0, own), (1, oth)):
        xhat, _ = normalise(tok[...].astype(f32))
        part = g[rel * rows : (rel + 1) * rows]
        gains += jnp.sum(part * xhat, axis=0, keepdims=True)
        shifts += jnp.sum(part, axis=0, keepdims=True)
    every = [sums0[0:1, :], sums1[0:1, :], sums]
    query_bias = jnp.concatenate([s[:, :PAIR] for s in every], axis=1)
    value_bias = jnp.concatenate([s[:, 2 * PAIR :] for s in every], axis=1)
    none = jnp.zeros_like(query_bias)
    vec = [vec_in[...], gains[:, :half], gains[:, half:], shifts[:, :half], shifts[:, half:]]
    vec += [jnp.where(core == 0, query_bias, none), jnp.where(core == 0, none, query_bias)]
    vec += [jnp.where(core == 0, value_bias, none), none]
    t_ref[16] = split_high_low(jnp.concatenate(vec, axis=0))


def pair_call(scal, pair, head_args, more):
    rows, width = head_args[8].shape[1:]
    half = width // 2
    chunk = width // 16
    head = pl.BlockSpec((2, rows, PAIR), lambda p, sc: (0, 0, pair))
    rel = pl.BlockSpec((rows, PAIR), lambda p, sc: (0, pair))
    in_specs = [head] * 3 + [
        rel,
        rel,
        pl.BlockSpec((1, 2, key_rows(2 * rows // QB)[0], QB), lambda p, sc: (pair, 0, 0, 0)),
        rel,
        rel,
        whole((2, rows, width)),
    ]
    scratch = [
        pltpu.VMEM((2 * rows, PAIR), bf16),
        pltpu.VMEM((PAIR, 2 * rows), bf16),
        pltpu.VMEM((2, rows, PAIR), bf16),
        pltpu.VMEM((2, rows, PAIR), bf16),
        pltpu.VMEM((PAIR, 2 * rows), f32),
        pltpu.VMEM((PAIR, 2 * rows), f32),
    ]
    grads = sds((2, rows, 3 * PAIR), bf16)
    more_specs = [whole(x.shape) for x in more]
    if pair == 2:
        column = pl.BlockSpec((width, half), lambda p, sc: (0, sc[CORE]))
        more_specs[-3:] = [column, column, whole((width, half))]
        scratch = [
            pltpu.VMEM(grads.shape, bf16),
            pltpu.VMEM((2 * rows, 9 * PAIR), bf16),
            pltpu.VMEM((width, 9 * PAIR), bf16),
        ] + scratch
        out_shape = [
            sds((17, chunk, half), bf16), sds((rows, width), f32), sds((rows, width + half), bf16),
            sds((rows, half), bf16),
        ]
    elif pair == 1:
        scratch = [pltpu.VMEM((16, chunk, half), bf16)] + scratch
        out_shape = [sds((8, 3, chunk, half), bf16)] * 2 + [grads, sds((8, half), f32)]
    else:
        out_shape = [sds((16, chunk, half), bf16), grads, sds((8, half), f32)]
    return pl.pallas_call(
        (first_pair_kernel, second_pair_kernel, last_pair_kernel)[pair],
        grid_spec=pltpu.PrefetchScalarGridSpec(
            num_scalar_prefetch=1,
            grid=(1,),
            in_specs=in_specs + more_specs,
            out_specs=[whole(x.shape) for x in out_shape],
            scratch_shapes=scratch,
        ),
        out_shape=out_shape,
        cost_estimate=cost(12 if pair == 2 else 8),
        compiler_params=params(44, 1),
    )(scal, *head_args, *more)


def split_high_low(vec):
    high = vec.astype(bf16)
    return jnp.concatenate([high, (vec - high.astype(f32)).astype(bf16)], axis=0)


def join_high_low(block):
    return block[:V_ROWS].astype(f32) + block[V_ROWS:].astype(f32)


def first_norm_back_kernel(scal, tok, gain, gn_own, arrived, grad_middle, dv_own, out_ref, skip_ref):
    width = tok.shape[1]
    gn_oth = arrived[:, :width]
    skip_ref[...] = jnp.where(scal[CORE] == 0, arrived[:, width:], dv_own[...])
    xhat, scale = normalise(tok[...].astype(f32))
    weighted = (gn_own[...] + gn_oth.astype(f32)) * row_of(gain)
    dv = scale * (
        weighted
        - jnp.mean(weighted, axis=-1, keepdims=True)
        - xhat * jnp.mean(weighted * xhat, axis=-1, keepdims=True)
    )
    out_ref[...] = (grad_middle[...] + dv).astype(bf16)


def first_norm_back(scal, tok, gain, gn_own, arrived, grad_middle, dv_own):
    rows, width = tok.shape
    tile = rows // 2
    block = pl.BlockSpec((tile, width), lambda s, sc: (s, 0))
    narrow = pl.BlockSpec((tile, width // 2), lambda s, sc: (s, 0))
    both = pl.BlockSpec((tile, width + width // 2), lambda s, sc: (s, 0))
    return pl.pallas_call(
        first_norm_back_kernel,
        grid_spec=pltpu.PrefetchScalarGridSpec(
            num_scalar_prefetch=1,
            grid=(2,),
            in_specs=[block, whole((width,)), block, both, block, narrow],
            out_specs=[block, narrow],
        ),
        out_shape=[sds((rows, width), bf16), sds((rows, width // 2), bf16)],
        cost_estimate=cost(4),
        compiler_params=params(32, 1),
    )(scal, tok, gain, gn_own, arrived, grad_middle, dv_own)


def flip(values, bits, dp_count):
    pairs = [((d * 2 + c), ((d ^ bits[c]) * 2 + c)) for d in range(dp_count) for c in range(2)]
    return lax.ppermute(values, ("dp", "seq"), pairs)


def swap(values):
    return lax.ppermute(values, "seq", [(0, 1), (1, 0)])


BEFORE_LAST = ('early', 'down')
AFTER_LAST = ('last', 'down', 'early', 'up', 'last', 'down', 'early', 'norm', 'down!', 'last', 'up', 'early', 'last', 'up')
STAGES = ((1, 2), (2, 1), (4, 4), (8, 8))
ORDER_D, ORDER_U, ORDER_E = (0, 1, 2, 3), (2, 0, 1, 3), (0, 1, 2, 3)


def stages(order):
    return [STAGES[n] for n in order]


def after(value, *others):
    return lax.optimization_barrier((value,) + others)[0]


class Halving:
    def __init__(self, parts, stages=STAGES, high=None):
        self.parts = list(parts)
        self.high = high
        self.size = parts[0].shape[0] * (1 if high is None else 2)
        self.stages = list(stages)
        self.begun = False

    def total(self, low, high):
        out = self.parts[0][low:high]
        for part in self.parts[1:]:
            out = out + part[low:high]
        return out

    def upper(self):
        if self.begun:
            self.parts = [lax.optimization_barrier(self.total(0, self.size))]
        self.begun = True
        self.size //= 2
        if self.high is not None:
            first, self.high = self.high, None
            return first
        return self.total(self.size, 2 * self.size)

    def result(self):
        return self.total(0, self.size)


def add_with_vec_kernel(mine, theirs, out):
    count = out.shape[0] - 1
    out[:count] = mine[:count] + theirs[:count]
    out[count] = split_high_low(join_high_low(mine[2 * count]) + join_high_low(theirs[count]))


class HalvingWithVec(Halving):
    def add(self):
        if len(self.parts) > 1:
            mine, theirs = self.parts
            self.parts = [
                pl.pallas_call(
                    add_with_vec_kernel,
                    out_shape=sds(theirs.shape, bf16),
                    compiler_params=pltpu.CompilerParams(vmem_limit_bytes=16 << 20),
                )(mine, theirs)
            ]

    def upper(self):
        self.add()
        return self.parts[0][(self.parts[0].shape[0] - 1) // 2 :]

    def result(self):
        self.add()
        return self.parts[0]


def arrived(chain, token):
    if chain.high is not None:
        chain.high, token = lax.optimization_barrier((chain.high, token))
    *chain.parts, token = lax.optimization_barrier((*chain.parts, token))
    return token


def send(token, *chains):
    for chain in chains:
        token = arrived(chain, token)
    bits = [chain.stages.pop(0) for chain in chains]
    assert all(b == bits[0] for b in bits)
    uppers = [chain.upper() for chain in chains]
    if len(chains) == 1:
        chains[0].parts.append(flip(uppers[0], bits[0], 16))
        return uppers[0]
    flat = [x.reshape(-1, x.shape[-1]) for x in uppers]
    token = jnp.concatenate(flat, axis=0)
    came = flip(token, bits[0], 16)
    at = 0
    for chain, x, rows in zip(chains, uppers, flat):
        chain.parts.append(came[at : at + rows.shape[0]].reshape(x.shape))
        at += rows.shape[0]
    return token


def both_sides(core, own, oth, put):
    @pl.when(core == 0)
    def _():
        put(0, own)
        put(1, oth)

    @pl.when(core != 0)
    def _():
        put(1, own)
        put(0, oth)


def finish_first_kernel(scal, down, early, down2, early2, gd, go):
    half = down.shape[1]

    def put(side, shares):
        down, early = shares
        gd[:, side * half : (side + 1) * half] = down[...].astype(f32)
        go[:, side * half : (side + 1) * half] = early[2].astype(f32)

    both_sides(scal[CORE], (down, early), (down2, early2), put)


def finish_last_kernel(scal, up, early, late, up2, early2, late2, gu, gq, gk, gv, *vectors):
    half = early.shape[2]

    def put(side, shares):
        up, early, late = shares
        for g in range(up.shape[0]):
            at = (side * up.shape[0] + g) * half
            gu[:, at : at + half] = up[g].astype(f32)
        at = side * half
        for p, piece in enumerate((early[0], early[1], late[0])):
            cols = slice(at + p * PAIR, at + (p + 1) * PAIR)
            gq[:, cols] = piece[:, :PAIR].astype(f32)
            gk[:, cols] = piece[:, PAIR : 2 * PAIR].astype(f32)
            if side == 0:
                gv[:, p * PAIR : (p + 1) * PAIR] = piece[:, 2 * PAIR :].astype(f32)

    both_sides(scal[CORE], (up, early, late), (up2, early2, late2), put)
    vec = join_high_low(late[1]) + join_high_low(late2[1])
    for ref, row in zip(vectors, (V_GAIN1, V_SHIFT1, V_QUERY, V_VALUE, V_OUT, V_GAIN2, V_SHIFT2, V_UP, V_DOWN)):
        for k in range(ref.shape[0] // half):
            ref[k * half : (k + 1) * half] = vec[row + k]


def finish(kernel, scal, shares, out_shape):
    out_shape = [sds(shape, f32) for shape in out_shape]
    return pl.pallas_call(
        kernel,
        grid_spec=pltpu.PrefetchScalarGridSpec(
            num_scalar_prefetch=1,
            grid=(1,),
            in_specs=[whole(x.shape) for x in shares],
            out_specs=[whole(s.shape) for s in out_shape],
        ),
        out_shape=out_shape,
        cost_estimate=cost(3),
        compiler_params=params(24, 1),
    )(scal, *shares)


def finish_any(core, down, up, early, late):
    half = down.shape[2]
    vec = lax.psum(join_high_low(late[16]), ("dp", "seq"))

    def columns(pieces):
        mine = jnp.concatenate([x.reshape(-1, x.shape[-1]).astype(f32) for x in pieces], axis=1)
        share = lax.psum_scatter(mine, "dp", scatter_dimension=0, tiled=True)
        other = swap(share)
        return jnp.where(core == 0, jnp.concatenate([share, other], 1), jnp.concatenate([other, share], 1))

    thirds = [early[:, 0], early[:, 1], late[:16]]
    gq, gk, gv = (columns([x[..., i * PAIR : (i + 1) * PAIR] for x in thirds]) for i in range(3))
    go = columns([early[:, 2]])
    gu = columns([up[:, g] for g in range(up.shape[1])])
    gd = columns([down])
    flat = lambda row, n: vec[row : row + n].reshape(-1)
    vectors = [flat(V_GAIN1, 2), flat(V_SHIFT1, 2), flat(V_QUERY, 2), flat(V_VALUE, 1), flat(V_OUT, 2)]
    vectors += [flat(V_GAIN2, 2), flat(V_SHIFT2, 2), flat(V_UP, 8), flat(V_DOWN, 2)]
    return [gq, gk, gv[:, :half], go, gu, gd] + vectors


def scalars(core, me, whole_tiles):
    at = jnp.arange(1 + 16 * 7, dtype=jnp.int32)
    table, chunk = (at - 1) >> 4, (at - 1) & 15
    if whole_tiles:
        off = chunk ^ me
        other = (table > 0) & ((table & 1) == 0)
        x_first = jnp.where(other, 1 - core, core) == 0
        x_bit, y_bit = off & 1, (off >> 1) & 1
        bits = (jnp.where(x_first, x_bit, y_bit), jnp.where(x_first, y_bit, x_bit), (off >> 2) & 1, (off >> 3) & 1)
        group = (table + 1) >> 1
        chunk = jnp.zeros_like(off)
        for b, bit in enumerate(bits):
            weight = jnp.int32(8 >> b)
            for g, order in enumerate((ORDER_D, ORDER_U, ORDER_E)):
                weight = jnp.where(group == g + 1, jnp.int32(8 >> order.index(b)), weight)
            chunk = chunk + bit * weight
    return jnp.where(at == 0, core, chunk).astype(jnp.int32)


def per_device(
    dp_count,
    tokens,
    skip_values,
    doc_lengths,
    gain_first,
    shift_first,
    query_weight,
    query_bias,
    key_weight,
    value_weight,
    value_bias,
    out_weight,
    out_bias,
    gain_second,
    shift_second,
    up_weight,
    up_bias,
    down_weight,
    down_bias,
    cotangent,
):
    rows, width = tokens.shape
    hidden = up_weight.shape[1]
    core = lax.axis_index("seq")
    scal = scalars(core, lax.axis_index("dp"), dp_count == 16)
    value_weight = jnp.where(core == 0, value_weight, jnp.zeros_like(value_weight))
    tokens_oth = swap(tokens)
    skip_oth = swap(skip_values)
    q, k, v, normed, att_own, att_send, probs = front(
        scal, doc_lengths, tokens.astype(f32), tokens_oth, jnp.where(core == 0, jnp.zeros_like(skip_values), skip_values), skip_oth,
        jnp.concatenate([gain_first, shift_first, query_bias, value_bias]).astype(f32),
        query_weight, key_weight, value_weight,
    )
    att_oth = swap(att_send)
    (output, grad_middle, ga_keep, ga_send, dn_keep, dn_send, up_keep, up_send, ow_keep, ow_send, vec) = mlp(
        scal, att_own, att_oth, tokens, cotangent, out_weight, out_bias, gain_second, shift_second,
        up_weight, up_bias, down_weight, down_bias,
    )
    whole_tiles = dp_count == 16
    ga_oth = swap(ga_send)
    dn_send, up_send, ow_send, _ = lax.optimization_barrier((dn_send, up_send, ow_send, ga_oth))
    dn_recv, up_recv, ow_recv = swap(dn_send), swap(up_send), swap(ow_send)
    down = Halving((dn_keep, dn_recv), stages(ORDER_D))
    up = Halving((up_keep, up_recv), stages(ORDER_U))
    head_args = [q, k, v, att_own, att_send, probs, ga_keep, ga_oth, normed]
    t0, x0, sums0 = pair_call(scal, 0, head_args, ())
    token = sums0
    if whole_tiles:
        token = send(token, down)
        token = send(token, up)
    early_low, early_high, x1, sums1 = pair_call(scal, 1, head_args, (after(t0, token), ow_keep, ow_recv))
    token = sums1
    early = Halving((early_low,), stages(ORDER_E), early_high)
    if whole_tiles:
        for chains in BEFORE_LAST:
            token = send(token, *(dict(early=early, down=down, up=up)[c] for c in chains.split()))
    late, gn_own, gn_send, dv_own = pair_call(
        scal, 2, head_args,
        (after(x0, token), x1, sums0, sums1, vec, tokens, tokens_oth, query_weight, key_weight, value_weight),
    )
    gn_oth = swap(gn_send)
    if whole_tiles:
        last = HalvingWithVec((late,))
        token = gn_send
        every = dict(early=early, down=down, up=up, last=last)
        for chains in AFTER_LAST:
            if chains == "gn!":
                gn_oth, token = lax.optimization_barrier((gn_oth, token))
                continue
            if chains.endswith("!"):
                chain = every[chains[:-1]]
                arrived(chain, token)
                token = chain.result()
                chain.parts = [token]
                continue
            if chains != "norm":
                token = send(token, *(every[c] for c in chains.split()))
                continue
            gn_held, token = lax.optimization_barrier((gn_oth, token))
            grad_tokens, grad_skip = first_norm_back(scal, tokens, gain_first, gn_own, gn_held, grad_middle, dv_own)
            token = grad_tokens
        high, wide = width // dp_count, (width // dp_count, width)
        token = arrived(down, token)
        arrived(early, token)
        down, early = down.result()[0], early.result()[0]
        down2, early2 = swap(down), swap(early)
        gd, go = finish(finish_first_kernel, scal, (down, early, down2, early2), [(hidden // dp_count, width), wide])
        arrived(up, gd)
        arrived(last, gd)
        up, last = up.result()[0], last.result()
        shares = (up, early, last, swap(up), early2, swap(last))
        vectors = [(n,) for n in (width, width, width, width // 2, width, width, width, hidden, width)]
        rest = finish(finish_last_kernel, scal, shares, [(high, hidden), wide, wide, (high, width // 2)] + vectors)
        gu, gq, gk, gv, gain1, shift1, gqb, gvb, gob, gain2, shift2, gub, gdb = rest
    else:
        grad_tokens, grad_skip = first_norm_back(scal, tokens, gain_first, gn_own, gn_oth, grad_middle, dv_own)
        rest = finish_any(core, down.result(), up.result(), jnp.concatenate([early_low, early_high]), late)
        gq, gk, gv, go, gu, gd, gain1, shift1, gqb, gvb, gob, gain2, shift2, gub, gdb = rest
    return (
        output, grad_tokens, grad_skip, gain1, shift1, gq, gqb, gk, gv, gvb, go, gob, gain2, shift2, gu, gub, gd, gdb,
    )


def solution(mesh):
    rows, full, shares = P(("dp", "seq"), None), P(), P("dp", None)
    return jax.shard_map(
        functools.partial(per_device, mesh.shape["dp"]),
        mesh=mesh,
        in_specs=(rows, rows, shares) + (full,) * 15 + (rows,),
        out_specs=(
            rows, rows, rows, full, full, shares, full, shares, shares, full, shares, full, full, full, shares, full,
            shares, full,
        ),
        check_vma=False,
    )
```

```python
import functools

import jax
import jax.numpy as jnp
from jax import lax
from jax.experimental import pallas as pl
from jax.experimental.pallas import tpu as pltpu
from jax.sharding import PartitionSpec as P

HEAD = 64
FRESH = 6
PAIR = 2 * HEAD
QB = 256
FRONT_MB = 46
MLP_MB = 52
LOG2E = 1.4426950408889634
GELU_C = 0.7978845608028654
GELU_A = 0.044715
f32 = jnp.float32
bf16 = jnp.bfloat16
NT = (((1,), (1,)), ((), ()))
TN = (((0,), (0,)), ((), ()))
CORE, PLACE_T = 0, 1
PLACE_D, PLACE_D_OTH, PLACE_U, PLACE_U_OTH, PLACE_E, PLACE_E_OTH = 17, 33, 49, 65, 81, 97
V_UP, V_DOWN, V_OUT, V_GAIN2, V_SHIFT2, V_GAIN1, V_SHIFT1, V_QUERY, V_VALUE = 0, 8, 10, 12, 14, 16, 18, 20, 22
V_ROWS = 24


def dot(left, right):
    return jnp.dot(left, right, preferred_element_type=f32)


def dot_nt(left, right):
    return lax.dot_general(left, right, NT, preferred_element_type=f32)


def dot_tn(left, right):
    return lax.dot_general(left, right, TN, preferred_element_type=f32)


def row_of(ref):
    return ref[...].astype(f32).reshape(1, -1)


def normalise(values):
    centre = values - jnp.mean(values, axis=-1, keepdims=True)
    spread = jnp.mean(centre * centre, axis=-1, keepdims=True)
    scale = lax.rsqrt(spread + 1e-05)
    return centre * scale, scale


def params(limit_mb, axes):
    return pltpu.CompilerParams(vmem_limit_bytes=limit_mb << 20, dimension_semantics=("arbitrary",) * axes)


def whole(shape):
    return pl.BlockSpec(shape, lambda *_: (0,) * len(shape))


def cost(micros):
    return pl.CostEstimate(flops=int(micros), bytes_accessed=0, transcendentals=0)


def sds(shape, dtype):
    return jax.ShapeDtypeStruct(shape, dtype)


def first_allowed(lengths, total):
    place = lax.broadcasted_iota(jnp.int32, (1, total), 1)
    start = jnp.zeros((1, total), jnp.int32)
    bound = jnp.int32(0)
    for k in range(4):
        bound = bound + lengths[0, k]
        start = jnp.where(place >= bound, bound, start)
    return jnp.where(place >= bound + lengths[0, 4], place, start)


def allowed_block(start, low, high, first_query):
    key = lax.broadcasted_iota(jnp.int32, (high - low, QB), 0) + low
    ok = key >= start
    if high > first_query:
        ok = ok & (key <= lax.broadcasted_iota(jnp.int32, (high - low, QB), 1) + first_query)
    return ok


def head_part(values, h):
    lane = lax.broadcasted_iota(jnp.int32, values.shape, 1)
    return jnp.where((lane < HEAD) if h == 0 else (lane >= HEAD), values, jnp.zeros_like(values))


def key_rows(qb):
    return QB * (qb * (qb + 1) // 2), QB * (qb + 1)


def attend_pair(scal, lengths, pair, q_ref, k_ref, v_ref, o_own, o_oth, probs, kb, vt, ob):
    core = scal[CORE]
    rows = q_ref.shape[1]
    total = 2 * rows
    lanes = slice(pair * PAIR, (pair + 1) * PAIR)
    for half in range(2):
        rel = core ^ half
        kb[half * rows : (half + 1) * rows, :] = k_ref[rel, :, lanes]
        vt[:, half * rows : (half + 1) * rows] = v_ref[rel, :, lanes].T
    start = first_allowed(lengths, total)
    items = [(qb, h) for qb in range(total // QB) for h in range(2)]

    def place(qb):
        return core ^ (qb * QB // rows), pl.ds(qb * QB % rows, QB)

    def scores(qb, h):
        low = qb * QB
        rel, at = place(qb)
        qh = head_part(q_ref[rel, at, lanes], h)
        return [(a, b, dot_nt(kb[a:b, :], qh)) for a, b in ([(0, low)] if low else []) + [(low, low + QB)]]

    done = {}
    ahead = scores(*items[0])
    for n, (qb, h) in enumerate(items):
        current = ahead
        if n + 1 < len(items):
            ahead = scores(*items[n + 1])
        low = qb * QB
        base, _ = key_rows(qb)
        begin = start[:, low : low + QB]
        peak = None
        masked = []
        for a, b, s in current:
            s = jnp.where(allowed_block(begin, a, b, low), s, -1e30)
            top = jnp.max(s, axis=0, keepdims=True)
            peak = top if peak is None else jnp.maximum(peak, top)
            masked.append((a, b, s))
        peak2 = peak * LOG2E
        raised = [(a, b, jnp.exp2(s * LOG2E - peak2)) for a, b, s in masked]
        summed = None
        for a, b, e in raised:
            part = jnp.sum(e, axis=0, keepdims=True)
            summed = part if summed is None else summed + part
        inverse = 1.0 / summed
        acc = None
        for a, b, e in raised:
            p = (e * inverse).astype(bf16)
            probs[h, base + a : base + b, :] = p
            part = dot(vt[h * HEAD : (h + 1) * HEAD, a:b], p)
            acc = part if acc is None else acc + part
        done[h] = acc
        if h == 1:
            rel, at = place(qb)
            ob[rel, at, :] = jnp.concatenate([done[0], done[1]], axis=0).T.astype(bf16)
    o_own[:, lanes] = ob[0]
    o_oth[:, lanes] = ob[1]


def front_kernel(
    scal, lengths, tok, oth, skip, skip_oth, vectors, wq, wk, wv,
    q_ref, k_ref, v_ref, n_ref, o_own, o_oth, p_ref,
    tok_s, skip_s, wqk_s, wv_s, probs, kb, vt, ob, sems, psems,
):
    core = scal[CORE]
    half = q_ref.shape[2]
    cols = pl.ds(pl.multiple_of(core * half, half), half)
    pieces = (
        (wq.at[:, cols], wqk_s.at[:, :half]), (wk.at[:, cols], wqk_s.at[:, half:]), (tok, tok_s), (wv, wv_s), (skip, skip_s),
    )
    fetch = [pltpu.make_async_copy(src, dst, sems.at[n]) for n, (src, dst) in enumerate(pieces)]
    for copy in fetch:
        copy.start()
    joined = row_of(vectors)
    width = 2 * half
    gain, shift, bq, bv = (joined[:, at : at + n] for at, n in ((0, width), (width, width), (2 * width, width), (3 * width, half)))
    bias = jnp.where(core == 0, bq[:, :half], bq[:, half:])
    for rel in (1, 0):
        if rel == 0:
            fetch[2].wait()
        xhat, _ = normalise((oth if rel else tok_s)[...].astype(f32))
        normed = (xhat * gain + shift).astype(bf16)
        n_ref[rel] = normed
        if rel:
            fetch[0].wait()
            fetch[1].wait()
        both = dot(normed, wqk_s[...])
        q_ref[rel] = (both[:, :half] + bias).astype(bf16) * jnp.asarray(HEAD**-0.5, bf16)
        k_ref[rel] = both[:, half:].astype(bf16)
    fetch[3].wait()
    fetch[4].wait()

    @pl.when(core == 0)
    def _():
        for rel in range(2):
            v_ref[rel] = (dot(n_ref[rel], wv_s[...]) + bv).astype(bf16)

    @pl.when(core != 0)
    def _():
        v_ref[0] = skip_s[...]
        v_ref[1] = skip_oth[...]

    out = []
    for pair in range(half // PAIR):
        slot = pair % 2
        if pair >= 2:
            out[pair - 2].wait()
        attend_pair(scal, lengths, pair, q_ref, k_ref, v_ref, o_own, o_oth, probs.at[slot], kb, vt, ob)
        out.append(pltpu.make_async_copy(probs.at[slot], p_ref.at[pair], psems.at[pair]))
        out[pair].start()
    for copy in out[-2:]:
        copy.wait()


def front(scal, lengths, tok, oth, skip, skip_oth, vectors, wq, wk, wv):
    rows, width = tok.shape
    half = width // 2
    pairs = half // PAIR
    packed = key_rows(2 * rows // QB)[0]
    here = pl.BlockSpec(memory_space=pltpu.VMEM)
    far = pl.BlockSpec(memory_space=pltpu.HBM)
    return pl.pallas_call(
        front_kernel,
        in_specs=[pl.BlockSpec(memory_space=pltpu.SMEM)] * 2 + [far, here, far, here, here, far, far, far],
        out_specs=[here] * 6 + [far],
        scratch_shapes=[
            pltpu.VMEM((rows, width), f32),
            pltpu.VMEM((rows, half), bf16),
            pltpu.VMEM((width, width), bf16),
            pltpu.VMEM((width, half), bf16),
            pltpu.VMEM((2, 2, packed, QB), bf16),
            pltpu.VMEM((2 * rows, PAIR), bf16),
            pltpu.VMEM((PAIR, 2 * rows), bf16),
            pltpu.VMEM((2, rows, PAIR), bf16),
            pltpu.SemaphoreType.DMA((5,)),
            pltpu.SemaphoreType.DMA((pairs,)),
        ],
        out_shape=[sds((2, rows, half), bf16)] * 3
        + [sds((2, rows, width), bf16)]
        + [sds((rows, half), bf16)] * 2
        + [sds((pairs, 2, packed, QB), bf16)],
        cost_estimate=cost(14),
        compiler_params=pltpu.CompilerParams(vmem_limit_bytes=FRONT_MB << 20),
    )(scal, lengths, tok, oth, skip, skip_oth, vectors, wq, wk, wv)


TILES = 4


def mlp_kernel(
    scal, att_own, att_oth, tok_far, cot_far, wo_far, bo, gain, shift, up_far, ub, down_far, db,
    out_far, gm_far, ga_keep, ga_send, dn_keep, dn_send, up_keep, up_send, ow_keep, ow_send, vec_ref,
    tok, cot, wo, up, down, ubias, normed, normed_t, xhat_ref, out_s, gm_s, dn_s, up_s, sems, out_sems, dn_sems, up_sems,
):
    core = scal[CORE]
    width = tok.shape[1]
    half = width // 2
    chunk = width // 16
    fchunk = half // 2
    parts = width // fchunk
    tiles = [(s + (TILES // 2) * (1 - core)) & (TILES - 1) for s in range(TILES)]
    span = [pl.ds(pl.multiple_of(t * width, width), width) for t in tiles]

    def fetch(src, dst, n):
        copy = pltpu.make_async_copy(src, dst, sems.at[n])
        copy.start()
        return copy

    wo_in, tok_in = fetch(wo_far, wo, 0), fetch(tok_far, tok, 1)
    up_in, down_in = [fetch(up_far.at[:, span[0]], up.at[0], 3)], []
    cot_in = fetch(cot_far, cot, 2)
    for s in range(TILES):
        if s:
            up_in.append(fetch(up_far.at[:, span[s]], up.at[s], 3 + 2 * s))
        down_in.append(fetch(down_far.at[span[s], :], down.at[s], 4 + 2 * s))

    def att_weight(which):
        return wo[pl.ds(pl.multiple_of(which * half, half), half), :]

    ubias[...] = row_of(ub)
    wo_in.wait()
    tok_in.wait()
    branch = dot(att_own[...], att_weight(core)) + dot(att_oth[...], att_weight(1 - core)) + row_of(bo)
    middle = tok[...].astype(f32) + branch
    xhat, scale = normalise(middle)
    xhat_ref[...] = xhat
    value = (xhat * row_of(gain) + row_of(shift)).astype(bf16)
    normed[...] = value
    normed_t[...] = value.T
    acc = middle + row_of(db)
    back = None
    sent = []
    up_in[0].wait()
    cot_in.wait()
    down_in[0].wait()
    ahead = dot(normed[...], up[0])
    for s in range(TILES):
        wide = dot_nt(cot[...], down[s])
        v = ahead + ubias[:, span[s]]
        if s + 1 < TILES:
            up_in[s + 1].wait()
            down_in[s + 1].wait()
            ahead = dot(normed[...], up[s + 1])
        sq = v * v
        t = jnp.tanh(v * (GELU_C + (GELU_C * GELU_A) * sq))
        half_t = 0.5 * (1.0 + t)
        act = (v * half_t).astype(bf16)
        slope = half_t + (0.5 * v) * (1.0 - t * t) * (GELU_C + (3.0 * GELU_C * GELU_A) * sq)
        grad = (wide * slope).astype(bf16)
        dn_s[s] = dot_tn(act, cot[...]).astype(bf16).reshape(parts, fchunk, width)
        for n in range(parts):
            for k, (out, side, table) in enumerate(((dn_keep, core, PLACE_D), (dn_send, 1 - core, PLACE_D_OTH))):
                cols = pl.ds(pl.multiple_of(side * half, half), half)
                place = scal[table + tiles[s] * parts + n]
                sent.append(pltpu.make_async_copy(dn_s.at[s, n, :, cols], out.at[place], dn_sems.at[s, n, k]))
                sent[-1].start()
        dup = dot(normed_t[...], grad).astype(bf16).reshape(16, chunk, width)
        keep = s >= TILES // 2
        for d in range(16):
            place = scal[(PLACE_U if keep else PLACE_U_OTH) + d]
            for g in range(2):
                up_s[s, place, g] = dup[d, :, g * half : (g + 1) * half]
        at = pl.ds(2 * (s % (TILES // 2)), 2)
        sent.append(pltpu.make_async_copy(up_s.at[s], (up_keep if keep else up_send).at[:, at], up_sems.at[s]))
        sent[-1].start()
        acc = acc + dot(act, down[s])
        part = dot_nt(grad, up[s])
        back = part if back is None else back + part
        sums = jnp.sum(grad.astype(f32), axis=0, keepdims=True)
        for g in range(2):
            vec_ref[pl.ds(V_UP + 2 * tiles[s] + g, 1), :] = sums[:, g * half : (g + 1) * half]
    out_s[...] = acc.astype(bf16)
    sent.append(pltpu.make_async_copy(out_s, out_far, out_sems.at[0]))
    sent[-1].start()
    xhat = xhat_ref[...]
    grad_out = cot[...].astype(f32)
    weighted = back * row_of(gain)
    dv = scale * (
        weighted
        - jnp.mean(weighted, axis=-1, keepdims=True)
        - xhat * jnp.mean(weighted * xhat, axis=-1, keepdims=True)
    )
    grad_middle = grad_out + dv
    gm_s[...] = grad_middle
    sent.append(pltpu.make_async_copy(gm_s, gm_far, out_sems.at[1]))
    sent[-1].start()
    branch = grad_middle.astype(bf16)

    def put(row, vector):
        vec_ref[row : row + 1, :] = vector[:, :half]
        vec_ref[row + 1 : row + 2, :] = vector[:, half:]

    put(V_DOWN, jnp.sum(grad_out, axis=0, keepdims=True))
    put(V_OUT, jnp.sum(branch.astype(f32), axis=0, keepdims=True))
    put(V_GAIN2, jnp.sum(back * xhat, axis=0, keepdims=True))
    put(V_SHIFT2, jnp.sum(back, axis=0, keepdims=True))
    ga = dot_nt(branch, wo[...]).astype(bf16)
    ga_keep[...] = jnp.where(core == 0, ga[:, :half], ga[:, half:])
    ga_send[...] = jnp.where(core == 0, ga[:, half:], ga[:, :half])
    wide_own = dot_tn(att_own[...], branch).astype(bf16).reshape(8, chunk, width)
    wide_oth = dot_tn(att_oth[...], branch).astype(bf16).reshape(8, chunk, width)

    def spread(keep, send):
        for d in range(8):
            own_place = scal[PLACE_E + core * 8 + d]
            oth_place = scal[PLACE_E + (1 - core) * 8 + d]
            ow_keep[own_place] = wide_own[d, :, keep]
            ow_keep[oth_place] = wide_oth[d, :, keep]
            ow_send[scal[PLACE_E_OTH + core * 8 + d]] = wide_own[d, :, send]
            ow_send[scal[PLACE_E_OTH + (1 - core) * 8 + d]] = wide_oth[d, :, send]

    left, right = slice(0, half), slice(half, width)
    pl.when(core == 0)(lambda: spread(left, right))
    pl.when(core != 0)(lambda: spread(right, left))
    for copy in sent:
        copy.wait()


def mlp(scal, att_own, att_oth, tok, cot, wo, bo, gain, shift, up, ub, down, db):
    rows, width = tok.shape
    half = width // 2
    hidden = up.shape[1]
    assert hidden == TILES * width
    here = pl.BlockSpec(memory_space=pltpu.VMEM)
    far = pl.BlockSpec(memory_space=pltpu.HBM)
    return pl.pallas_call(
        mlp_kernel,
        in_specs=[pl.BlockSpec(memory_space=pltpu.SMEM)]
        + [here] * 2
        + [far] * 3
        + [here] * 3
        + [far, here, far, here],
        out_specs=[far, far, here, here, far, far, far, far, here, here, here],
        scratch_shapes=[
            pltpu.VMEM((rows, width), bf16),
            pltpu.VMEM((rows, width), bf16),
            pltpu.VMEM((width, width), bf16),
            pltpu.VMEM((TILES, width, width), bf16),
            pltpu.VMEM((TILES, width, width), bf16),
            pltpu.VMEM((1, hidden), f32),
            pltpu.VMEM((rows, width), bf16),
            pltpu.VMEM((width, rows), bf16),
            pltpu.VMEM((rows, width), f32),
            pltpu.VMEM((rows, width), bf16),
            pltpu.VMEM((rows, width), f32),
            pltpu.VMEM((TILES, 4, half // 2, width), bf16),
            pltpu.VMEM((TILES, 16, 2, width // 16, half), bf16),
            pltpu.SemaphoreType.DMA((3 + 2 * TILES,)),
            pltpu.SemaphoreType.DMA((2,)),
            pltpu.SemaphoreType.DMA((TILES, 4, 2)),
            pltpu.SemaphoreType.DMA((TILES,)),
        ],
        out_shape=[
            sds((rows, width), bf16),
            sds((rows, width), f32),
            sds((rows, half), bf16),
            sds((rows, half), bf16),
            sds((16, half // 2, half), bf16),
            sds((16, half // 2, half), bf16),
            sds((16, TILES, width // 16, half), bf16),
            sds((16, TILES, width // 16, half), bf16),
            sds((16, width // 16, half), bf16),
            sds((16, width // 16, half), bf16),
            sds((16, half), f32),
        ],
        cost_estimate=cost(28),
        compiler_params=pltpu.CompilerParams(vmem_limit_bytes=MLP_MB << 20),
    )(scal, att_own, att_oth, tok, cot, wo, bo, gain, shift, up, ub, down, db)


def pair_back(scal, q_ref, k_ref, v_ref, o1, o2, p_ref, do1, do2, n_ref, x, scratch):
    vb, kt, db, ob, dk_acc, dv_acc = scratch
    core = scal[CORE]
    rows = q_ref.shape[1]
    total = 2 * rows
    width = n_ref.shape[2]
    for hf in range(2):
        rel = core ^ hf
        cut = slice(hf * rows, (hf + 1) * rows)
        vb[cut, :] = v_ref[rel]
        kt[:, cut] = k_ref[rel].T
    db[0] = do1[...]
    db[1] = do2[...]
    ob[0] = o1[...]
    ob[1] = o2[...]
    dk_acc[...] = jnp.zeros_like(dk_acc)
    dv_acc[...] = jnp.zeros_like(dv_acc)
    items = [(qb, h) for qb in reversed(range(total // QB)) for h in range(2)]

    def place(qb):
        return core ^ (qb * QB // rows), pl.ds(qb * QB % rows, QB)

    def grad_probs(qb, h):
        rel, at = place(qb)
        return dot_nt(vb[0 : (qb + 1) * QB, :], head_part(db[rel, at, :], h))

    ahead = grad_probs(*items[0])
    parts = []
    for n, (qb, h) in enumerate(items):
        dp = ahead
        if n + 1 < len(items):
            ahead = grad_probs(*items[n + 1])
        rel, at = place(qb)
        base, keys = key_rows(qb)
        cut = slice(h * HEAD, (h + 1) * HEAD)
        if h == 0:
            query_t = q_ref[rel, at, :].T
            grad_t = db[rel, at, :].T
            both = grad_t.astype(f32) * ob[rel, at, :].T.astype(f32)
        delta = jnp.sum(both[cut], axis=0, keepdims=True)
        p = p_ref[0, h, base : base + keys, :]
        ds = (p.astype(f32) * (dp - delta)).astype(bf16)
        dv_acc[cut, 0:keys] += dot_nt(grad_t[cut], p)
        dk_acc[cut, 0:keys] += dot_nt(query_t[cut], ds)
        parts.append(dot(kt[cut, 0:keys], ds))
        if h == 1:
            x[rel, at, 0:PAIR] = (jnp.concatenate(parts, axis=0).T * (HEAD**-0.5)).astype(bf16)
            parts = []
    for hf in range(2):
        rel = core ^ hf
        cut = slice(hf * rows, (hf + 1) * rows)
        x[rel, :, PAIR : 2 * PAIR] = dk_acc[:, cut].T.astype(bf16)
        x[rel, :, 2 * PAIR :] = dv_acc[:, cut].T.astype(bf16)
    grads = x[...].reshape(total, 3 * PAIR)
    dw = dot_tn(n_ref[...].reshape(total, width), grads).astype(bf16).reshape(16, width // 16, 3 * PAIR)
    return dw, jnp.sum(grads.astype(f32), axis=0, keepdims=True)


def first_pair_kernel(scal, *refs):
    inputs, (t_ref, x, sums_ref), scratch = refs[:9], refs[9:12], refs[12:]
    dw, sums = pair_back(scal, *inputs, x, scratch)
    sums_ref[0:1, :] = sums
    for d in range(16):
        t_ref[scal[PLACE_E + d]] = dw[d]


def second_pair_kernel(scal, *refs):
    inputs, (t_in, ow_keep, ow_recv), (t_low, t_high, x, sums_ref) = refs[:9], refs[9:12], refs[12:16]
    t_ref, *scratch = refs[16:]
    sides = ((t_low, slice(0, 8)), (t_high, slice(8, 16)))
    for out, at in sides:
        out[:, 0] = t_in[at]
        out[:, 2] = (ow_keep[at].astype(f32) + ow_recv[at].astype(f32)).astype(bf16)
    dw, sums = pair_back(scal, *inputs, x, scratch)
    sums_ref[0:1, :] = sums
    for d in range(16):
        t_ref[scal[PLACE_E + d]] = dw[d]
    for out, at in sides:
        out[:, 1] = t_ref[at]


def last_pair_kernel(scal, *refs):
    inputs, (x0, x1, sums0, sums1, vec_in, own, oth, wq, wk, wv) = refs[:9], refs[9:19]
    (t_ref, gn_ref, gs_ref, dv_own), (x, xs, ws, *scratch) = refs[19:23], refs[23:]
    core = scal[CORE]
    dw, sums = pair_back(scal, *inputs, x, scratch)
    for d in range(16):
        t_ref[scal[PLACE_T + d]] = dw[d]
    rows = own.shape[0]
    half = own.shape[1] // 2
    for p, piece in enumerate((x0, x1, x)):
        left = p * 3 * PAIR
        xs[:, left : left + 3 * PAIR] = piece[...].reshape(2 * rows, 3 * PAIR)
        dv_own[:, p * PAIR : (p + 1) * PAIR] = piece[0, :, 2 * PAIR :]
        gs_ref[:, 2 * half + p * PAIR : 2 * half + (p + 1) * PAIR] = piece[1, :, 2 * PAIR :]
        for k, weight in enumerate((wq, wk, wv)):
            ws[:, left + k * PAIR : left + (k + 1) * PAIR] = weight[:, p * PAIR : (p + 1) * PAIR]

    g = dot_nt(xs[...], ws[...])
    gn_ref[...] = g[:rows]
    gs_ref[:, : 2 * half] = g[rows:].astype(bf16)
    gains, shifts = 0.0, 0.0
    for rel, tok in ((0, own), (1, oth)):
        xhat, _ = normalise(tok[...].astype(f32))
        part = g[rel * rows : (rel + 1) * rows]
        gains += jnp.sum(part * xhat, axis=0, keepdims=True)
        shifts += jnp.sum(part, axis=0, keepdims=True)
    every = [sums0[0:1, :], sums1[0:1, :], sums]
    query_bias = jnp.concatenate([s[:, :PAIR] for s in every], axis=1)
    value_bias = jnp.concatenate([s[:, 2 * PAIR :] for s in every], axis=1)
    none = jnp.zeros_like(query_bias)
    vec = [vec_in[...], gains[:, :half], gains[:, half:], shifts[:, :half], shifts[:, half:]]
    vec += [jnp.where(core == 0, query_bias, none), jnp.where(core == 0, none, query_bias)]
    vec += [jnp.where(core == 0, value_bias, none), none]
    t_ref[16] = split_high_low(jnp.concatenate(vec, axis=0))


def pair_call(scal, pair, head_args, more):
    rows, width = head_args[8].shape[1:]
    half = width // 2
    chunk = width // 16
    head = pl.BlockSpec((2, rows, PAIR), lambda p, sc: (0, 0, pair))
    rel = pl.BlockSpec((rows, PAIR), lambda p, sc: (0, pair))
    in_specs = [head] * 3 + [
        rel,
        rel,
        pl.BlockSpec((1, 2, key_rows(2 * rows // QB)[0], QB), lambda p, sc: (pair, 0, 0, 0)),
        rel,
        rel,
        whole((2, rows, width)),
    ]
    scratch = [
        pltpu.VMEM((2 * rows, PAIR), bf16),
        pltpu.VMEM((PAIR, 2 * rows), bf16),
        pltpu.VMEM((2, rows, PAIR), bf16),
        pltpu.VMEM((2, rows, PAIR), bf16),
        pltpu.VMEM((PAIR, 2 * rows), f32),
        pltpu.VMEM((PAIR, 2 * rows), f32),
    ]
    grads = sds((2, rows, 3 * PAIR), bf16)
    more_specs = [whole(x.shape) for x in more]
    if pair == 2:
        column = pl.BlockSpec((width, half), lambda p, sc: (0, sc[CORE]))
        more_specs[-3:] = [column, column, whole((width, half))]
        scratch = [
            pltpu.VMEM(grads.shape, bf16),
            pltpu.VMEM((2 * rows, 9 * PAIR), bf16),
            pltpu.VMEM((width, 9 * PAIR), bf16),
        ] + scratch
        out_shape = [
            sds((17, chunk, half), bf16), sds((rows, width), f32), sds((rows, width + half), bf16),
            sds((rows, half), bf16),
        ]
    elif pair == 1:
        scratch = [pltpu.VMEM((16, chunk, half), bf16)] + scratch
        out_shape = [sds((8, 3, chunk, half), bf16)] * 2 + [grads, sds((8, half), f32)]
    else:
        out_shape = [sds((16, chunk, half), bf16), grads, sds((8, half), f32)]
    return pl.pallas_call(
        (first_pair_kernel, second_pair_kernel, last_pair_kernel)[pair],
        grid_spec=pltpu.PrefetchScalarGridSpec(
            num_scalar_prefetch=1,
            grid=(1,),
            in_specs=in_specs + more_specs,
            out_specs=[whole(x.shape) for x in out_shape],
            scratch_shapes=scratch,
        ),
        out_shape=out_shape,
        cost_estimate=cost(12 if pair == 2 else 8),
        compiler_params=params(44, 1),
    )(scal, *head_args, *more)


def split_high_low(vec):
    high = vec.astype(bf16)
    return jnp.concatenate([high, (vec - high.astype(f32)).astype(bf16)], axis=0)


def join_high_low(block):
    return block[:V_ROWS].astype(f32) + block[V_ROWS:].astype(f32)


def first_norm_back_kernel(scal, tok, gain, gn_own, arrived, grad_middle, dv_own, out_ref, skip_ref):
    width = tok.shape[1]
    gn_oth = arrived[:, :width]
    skip_ref[...] = jnp.where(scal[CORE] == 0, arrived[:, width:], dv_own[...])
    xhat, scale = normalise(tok[...].astype(f32))
    weighted = (gn_own[...] + gn_oth.astype(f32)) * row_of(gain)
    dv = scale * (
        weighted
        - jnp.mean(weighted, axis=-1, keepdims=True)
        - xhat * jnp.mean(weighted * xhat, axis=-1, keepdims=True)
    )
    out_ref[...] = (grad_middle[...] + dv).astype(bf16)


def first_norm_back(scal, tok, gain, gn_own, arrived, grad_middle, dv_own):
    rows, width = tok.shape
    tile = rows // 2
    block = pl.BlockSpec((tile, width), lambda s, sc: (s, 0))
    narrow = pl.BlockSpec((tile, width // 2), lambda s, sc: (s, 0))
    both = pl.BlockSpec((tile, width + width // 2), lambda s, sc: (s, 0))
    return pl.pallas_call(
        first_norm_back_kernel,
        grid_spec=pltpu.PrefetchScalarGridSpec(
            num_scalar_prefetch=1,
            grid=(2,),
            in_specs=[block, whole((width,)), block, both, block, narrow],
            out_specs=[block, narrow],
        ),
        out_shape=[sds((rows, width), bf16), sds((rows, width // 2), bf16)],
        cost_estimate=cost(4),
        compiler_params=params(32, 1),
    )(scal, tok, gain, gn_own, arrived, grad_middle, dv_own)


def flip(values, bits, dp_count):
    pairs = [((d * 2 + c), ((d ^ bits[c]) * 2 + c)) for d in range(dp_count) for c in range(2)]
    return lax.ppermute(values, ("dp", "seq"), pairs)


def swap(values):
    return lax.ppermute(values, "seq", [(0, 1), (1, 0)])


BEFORE_LAST = ('early', 'down')
AFTER_LAST = ('last', 'down', 'early', 'up', 'last', 'down', 'early', 'norm', 'down!', 'last', 'up', 'early', 'last', 'up')
STAGES = ((1, 2), (2, 1), (4, 4), (8, 8))
ORDER_D, ORDER_U, ORDER_E = (0, 1, 2, 3), (2, 0, 1, 3), (0, 1, 2, 3)


def stages(order):
    return [STAGES[n] for n in order]


def after(value, *others):
    return lax.optimization_barrier((value,) + others)[0]


class Halving:
    def __init__(self, parts, stages=STAGES, high=None):
        self.parts = list(parts)
        self.high = high
        self.size = parts[0].shape[0] * (1 if high is None else 2)
        self.stages = list(stages)
        self.begun = False

    def total(self, low, high):
        out = self.parts[0][low:high]
        for part in self.parts[1:]:
            out = out + part[low:high]
        return out

    def upper(self):
        if self.begun:
            self.parts = [lax.optimization_barrier(self.total(0, self.size))]
        self.begun = True
        self.size //= 2
        if self.high is not None:
            first, self.high = self.high, None
            return first
        return self.total(self.size, 2 * self.size)

    def result(self):
        return self.total(0, self.size)


def add_with_vec_kernel(mine, theirs, out):
    count = out.shape[0] - 1
    out[:count] = mine[:count] + theirs[:count]
    out[count] = split_high_low(join_high_low(mine[2 * count]) + join_high_low(theirs[count]))


class HalvingWithVec(Halving):
    def add(self):
        if len(self.parts) > 1:
            mine, theirs = self.parts
            self.parts = [
                pl.pallas_call(
                    add_with_vec_kernel,
                    out_shape=sds(theirs.shape, bf16),
                    compiler_params=pltpu.CompilerParams(vmem_limit_bytes=16 << 20),
                )(mine, theirs)
            ]

    def upper(self):
        self.add()
        return self.parts[0][(self.parts[0].shape[0] - 1) // 2 :]

    def result(self):
        self.add()
        return self.parts[0]


def arrived(chain, token):
    if chain.high is not None:
        chain.high, token = lax.optimization_barrier((chain.high, token))
    *chain.parts, token = lax.optimization_barrier((*chain.parts, token))
    return token


def send(token, *chains):
    for chain in chains:
        token = arrived(chain, token)
    bits = [chain.stages.pop(0) for chain in chains]
    assert all(b == bits[0] for b in bits)
    uppers = [chain.upper() for chain in chains]
    if len(chains) == 1:
        chains[0].parts.append(flip(uppers[0], bits[0], 16))
        return uppers[0]
    flat = [x.reshape(-1, x.shape[-1]) for x in uppers]
    token = jnp.concatenate(flat, axis=0)
    came = flip(token, bits[0], 16)
    at = 0
    for chain, x, rows in zip(chains, uppers, flat):
        chain.parts.append(came[at : at + rows.shape[0]].reshape(x.shape))
        at += rows.shape[0]
    return token


def both_sides(core, own, oth, put):
    @pl.when(core == 0)
    def _():
        put(0, own)
        put(1, oth)

    @pl.when(core != 0)
    def _():
        put(1, own)
        put(0, oth)


def finish_first_kernel(scal, down, early, down2, early2, gd, go):
    half = down.shape[1]

    def put(side, shares):
        down, early = shares
        gd[:, side * half : (side + 1) * half] = down[...].astype(f32)
        go[:, side * half : (side + 1) * half] = early[2].astype(f32)

    both_sides(scal[CORE], (down, early), (down2, early2), put)


def finish_last_kernel(scal, up, early, late, up2, early2, late2, gu, gq, gk, gv, *vectors):
    half = early.shape[2]

    def put(side, shares):
        up, early, late = shares
        for g in range(up.shape[0]):
            at = (side * up.shape[0] + g) * half
            gu[:, at : at + half] = up[g].astype(f32)
        at = side * half
        for p, piece in enumerate((early[0], early[1], late[0])):
            cols = slice(at + p * PAIR, at + (p + 1) * PAIR)
            gq[:, cols] = piece[:, :PAIR].astype(f32)
            gk[:, cols] = piece[:, PAIR : 2 * PAIR].astype(f32)
            if side == 0:
                gv[:, p * PAIR : (p + 1) * PAIR] = piece[:, 2 * PAIR :].astype(f32)

    both_sides(scal[CORE], (up, early, late), (up2, early2, late2), put)
    vec = join_high_low(late[1]) + join_high_low(late2[1])
    for ref, row in zip(vectors, (V_GAIN1, V_SHIFT1, V_QUERY, V_VALUE, V_OUT, V_GAIN2, V_SHIFT2, V_UP, V_DOWN)):
        for k in range(ref.shape[0] // half):
            ref[k * half : (k + 1) * half] = vec[row + k]


def finish(kernel, scal, shares, out_shape):
    out_shape = [sds(shape, f32) for shape in out_shape]
    return pl.pallas_call(
        kernel,
        grid_spec=pltpu.PrefetchScalarGridSpec(
            num_scalar_prefetch=1,
            grid=(1,),
            in_specs=[whole(x.shape) for x in shares],
            out_specs=[whole(s.shape) for s in out_shape],
        ),
        out_shape=out_shape,
        cost_estimate=cost(3),
        compiler_params=params(24, 1),
    )(scal, *shares)


def finish_any(core, down, up, early, late):
    half = down.shape[2]
    vec = lax.psum(join_high_low(late[16]), ("dp", "seq"))

    def columns(pieces):
        mine = jnp.concatenate([x.reshape(-1, x.shape[-1]).astype(f32) for x in pieces], axis=1)
        share = lax.psum_scatter(mine, "dp", scatter_dimension=0, tiled=True)
        other = swap(share)
        return jnp.where(core == 0, jnp.concatenate([share, other], 1), jnp.concatenate([other, share], 1))

    thirds = [early[:, 0], early[:, 1], late[:16]]
    gq, gk, gv = (columns([x[..., i * PAIR : (i + 1) * PAIR] for x in thirds]) for i in range(3))
    go = columns([early[:, 2]])
    gu = columns([up[:, g] for g in range(up.shape[1])])
    gd = columns([down])
    flat = lambda row, n: vec[row : row + n].reshape(-1)
    vectors = [flat(V_GAIN1, 2), flat(V_SHIFT1, 2), flat(V_QUERY, 2), flat(V_VALUE, 1), flat(V_OUT, 2)]
    vectors += [flat(V_GAIN2, 2), flat(V_SHIFT2, 2), flat(V_UP, 8), flat(V_DOWN, 2)]
    return [gq, gk, gv[:, :half], go, gu, gd] + vectors


def scalars(core, me, whole_tiles):
    at = jnp.arange(1 + 16 * 7, dtype=jnp.int32)
    table, chunk = (at - 1) >> 4, (at - 1) & 15
    if whole_tiles:
        off = chunk ^ me
        other = (table > 0) & ((table & 1) == 0)
        x_first = jnp.where(other, 1 - core, core) == 0
        x_bit, y_bit = off & 1, (off >> 1) & 1
        bits = (jnp.where(x_first, x_bit, y_bit), jnp.where(x_first, y_bit, x_bit), (off >> 2) & 1, (off >> 3) & 1)
        group = (table + 1) >> 1
        chunk = jnp.zeros_like(off)
        for b, bit in enumerate(bits):
            weight = jnp.int32(8 >> b)
            for g, order in enumerate((ORDER_D, ORDER_U, ORDER_E)):
                weight = jnp.where(group == g + 1, jnp.int32(8 >> order.index(b)), weight)
            chunk = chunk + bit * weight
    return jnp.where(at == 0, core, chunk).astype(jnp.int32)


def per_device(
    dp_count,
    tokens,
    skip_values,
    doc_lengths,
    gain_first,
    shift_first,
    query_weight,
    query_bias,
    key_weight,
    value_weight,
    value_bias,
    out_weight,
    out_bias,
    gain_second,
    shift_second,
    up_weight,
    up_bias,
    down_weight,
    down_bias,
    cotangent,
):
    rows, width = tokens.shape
    hidden = up_weight.shape[1]
    core = lax.axis_index("seq")
    scal = scalars(core, lax.axis_index("dp"), dp_count == 16)
    value_weight = jnp.where(core == 0, value_weight, jnp.zeros_like(value_weight))
    tokens_oth = swap(tokens)
    skip_oth = swap(skip_values)
    q, k, v, normed, att_own, att_send, probs = front(
        scal, doc_lengths, tokens.astype(f32), tokens_oth, jnp.where(core == 0, jnp.zeros_like(skip_values), skip_values), skip_oth,
        jnp.concatenate([gain_first, shift_first, query_bias, value_bias]).astype(f32),
        query_weight, key_weight, value_weight,
    )
    att_oth = swap(att_send)
    (output, grad_middle, ga_keep, ga_send, dn_keep, dn_send, up_keep, up_send, ow_keep, ow_send, vec) = mlp(
        scal, att_own, att_oth, tokens, cotangent, out_weight, out_bias, gain_second, shift_second,
        up_weight, up_bias, down_weight, down_bias,
    )
    whole_tiles = dp_count == 16
    ga_oth = swap(ga_send)
    dn_send, up_send, ow_send, _ = lax.optimization_barrier((dn_send, up_send, ow_send, ga_oth))
    dn_recv, up_recv, ow_recv = swap(dn_send), swap(up_send), swap(ow_send)
    down = Halving((dn_keep, dn_recv), stages(ORDER_D))
    up = Halving((up_keep, up_recv), stages(ORDER_U))
    head_args = [q, k, v, att_own, att_send, probs, ga_keep, ga_oth, normed]
    t0, x0, sums0 = pair_call(scal, 0, head_args, ())
    token = sums0
    if whole_tiles:
        token = send(token, down)
        token = send(token, up)
    early_low, early_high, x1, sums1 = pair_call(scal, 1, head_args, (after(t0, token), ow_keep, ow_recv))
    token = sums1
    early = Halving((early_low,), stages(ORDER_E), early_high)
    if whole_tiles:
        for chains in BEFORE_LAST:
            token = send(token, *(dict(early=early, down=down, up=up)[c] for c in chains.split()))
    late, gn_own, gn_send, dv_own = pair_call(
        scal, 2, head_args,
        (after(x0, token), x1, sums0, sums1, vec, tokens, tokens_oth, query_weight, key_weight, value_weight),
    )
    gn_oth = swap(gn_send)
    if whole_tiles:
        last = HalvingWithVec((late,))
        token = gn_send
        every = dict(early=early, down=down, up=up, last=last)
        for chains in AFTER_LAST:
            if chains == "gn!":
                gn_oth, token = lax.optimization_barrier((gn_oth, token))
                continue
            if chains.endswith("!"):
                chain = every[chains[:-1]]
                arrived(chain, token)
                token = chain.result()
                chain.parts = [token]
                continue
            if chains != "norm":
                token = send(token, *(every[c] for c in chains.split()))
                continue
            gn_held, token = lax.optimization_barrier((gn_oth, token))
            grad_tokens, grad_skip = first_norm_back(scal, tokens, gain_first, gn_own, gn_held, grad_middle, dv_own)
            token = grad_tokens
        high, wide = width // dp_count, (width // dp_count, width)
        token = arrived(down, token)
        arrived(early, token)
        down, early = down.result()[0], early.result()[0]
        down2, early2 = swap(down), swap(early)
        gd, go = finish(finish_first_kernel, scal, (down, early, down2, early2), [(hidden // dp_count, width), wide])
        arrived(up, gd)
        arrived(last, gd)
        up, last = up.result()[0], last.result()
        shares = (up, early, last, swap(up), early2, swap(last))
        vectors = [(n,) for n in (width, width, width, width // 2, width, width, width, hidden, width)]
        rest = finish(finish_last_kernel, scal, shares, [(high, hidden), wide, wide, (high, width // 2)] + vectors)
        gu, gq, gk, gv, gain1, shift1, gqb, gvb, gob, gain2, shift2, gub, gdb = rest
    else:
        grad_tokens, grad_skip = first_norm_back(scal, tokens, gain_first, gn_own, gn_oth, grad_middle, dv_own)
        rest = finish_any(core, down.result(), up.result(), jnp.concatenate([early_low, early_high]), late)
        gq, gk, gv, go, gu, gd, gain1, shift1, gqb, gvb, gob, gain2, shift2, gub, gdb = rest
    return (
        output, grad_tokens, grad_skip, gain1, shift1, gq, gqb, gk, gv, gvb, go, gob, gain2, shift2, gu, gub, gd, gdb,
    )


def solution(mesh):
    rows, full, shares = P(("dp", "seq"), None), P(), P("dp", None)
    return jax.shard_map(
        functools.partial(per_device, mesh.shape["dp"]),
        mesh=mesh,
        in_specs=(rows, rows, shares) + (full,) * 15 + (rows,),
        out_specs=(
            rows, rows, rows, full, full, shares, full, shares, shares, full, shares, full, full, full, shares, full,
            shares, full,
        ),
        check_vma=False,
    )
```
